32 devices in a mesh: dp: 16 (over z, x, core), fsdp: 2 (over y).
Axes of the slice: x: 2, y: 2, z: 4, core: 2. Of those that a mesh axis runs over, the one named last changes fastest.
Arguments:
- clean_in: bfloat16 [32, 384, 768], P(('dp', 'fsdp')), may hold values from -6 to 6
- noise_bits: int32 [32, 384], P(('dp', 'fsdp')), may hold values from 0 to 1, as said below
- mask_vector: bfloat16 [768], P('fsdp'), may hold values from -6 to 6
- gain_attn: bfloat16 [768], P('fsdp'), may hold values from 0.5 to 1.5
- w_qkv: bfloat16 [768, 2304], P('fsdp'), may hold values from -0.21875 to 0.21875
- w_out: bfloat16 [768, 768], P('fsdp'), may hold values from -0.875 to 0.875
- gain_mlp: bfloat16 [768], P('fsdp'), may hold values from 0.5 to 1.5
- w_up: bfloat16 [768, 3072], P('fsdp'), may hold values from -0.21875 to 0.21875
- bias_up: bfloat16 [3072], P('fsdp'), may hold values from -3 to 3
- w_down: bfloat16 [3072, 768], P('fsdp'), may hold values from -0.109375 to 0.109375
- bias_down: bfloat16 [768], P('fsdp'), may hold values from -2 to 2
- out_grad: bfloat16 [32, 768, 768], P(('dp', 'fsdp')), may hold values from -6 to 6
Outputs:
- block_out: bfloat16 [32, 768, 768], P(('dp', 'fsdp'))
- clean_grad: float32 [32, 384, 768], P(('dp', 'fsdp'))
- mask_vector_grad: float32 [768], P('fsdp')
- gain_attn_grad: float32 [768], P('fsdp')
- w_qkv_grad: float32 [768, 2304], P('fsdp')
- w_out_grad: float32 [768, 768], P('fsdp')
- gain_mlp_grad: float32 [768], P('fsdp')
- w_up_grad: float32 [768, 3072], P('fsdp')
- bias_up_grad: float32 [3072], P('fsdp')
- w_down_grad: float32 [3072, 768], P('fsdp')
- bias_down_grad: float32 [768], P('fsdp')
The draws below stay inside these ranges and needn't reach their ends.
Inputs may be any that keep to these rules, and one draw needn't show every extreme that they name: `noise_bits`: 1 marks a token replaced by mask_vector in the noisy copy; each aligned block of 16 tokens of a sequence is masked at a rate of its own.
All inputs are finite; a program needn't handle non-finite values.
Results may differ from the reference program's by a relative error of at most 0.014.
Values may be sent and summed in bfloat16 or wider, within the bound.
A program may use at most 256 MiB of HBM per device.

```python
import math
import jax
import jax.numpy as jnp
from jax import lax

D = 768
H = 12
HD = 64
FF = 3072
BLOCK = 16
LEN = 384
SEQS = 32


def draw_noise_bits(key, part):
    key = jax.random.fold_in(key, 11)
    rate_key, toss_key = jax.random.split(key)
    block_rates = jax.random.randint(rate_key, (SEQS, LEN // BLOCK), 30, 81)
    tosses = jax.random.randint(toss_key, (SEQS, LEN), 0, 100)
    return (tosses < jnp.repeat(block_rates, BLOCK, axis=1)).astype(jnp.int32)


def levels(rng, shape, pieces, low, top_value):
    factor_of = 1.0
    for dim, blocks in pieces:
        steps = jax.random.uniform(jax.random.fold_in(jax.random.fold_in(rng, 6), dim), (blocks,), jnp.float32, low / len(pieces), top_value / len(pieces))
        factor_of = factor_of * jnp.repeat(jnp.exp(steps), shape[dim] // blocks).reshape((-1,) + (1,) * (len(shape) - 1 - dim))
    return factor_of


def noise(key, dims, width, reach, pieces=(), kind=jnp.bfloat16):
    factor_of = levels(key, dims, pieces, -0.22, 0.18) if pieces else 1.0
    result = jax.random.normal(key, dims, jnp.float32) * width * factor_of
    return jnp.minimum(jnp.maximum(result, -reach), reach).astype(kind)


def setup_inputs(seed: int = 0) -> dict:
    arg_keys = jax.random.split(jax.random.key(seed), 13)
    clean_in = noise(arg_keys[0], (SEQS, LEN, D), 1.0, 6.0, ((0, 32),))
    noise_bits = draw_noise_bits(jax.random.fold_in(arg_keys[12], 71), 0)
    mask_vector = noise(arg_keys[2], (D,), 1.0, 6.0, ((0, 2),))
    gain_attn = jnp.clip(1.0 + 0.1 * jax.random.normal(arg_keys[3], (D,), jnp.float32), 0.5, 1.5).astype(jnp.bfloat16)
    w_qkv = noise(arg_keys[4], (D, 3 * D), D ** -0.5, 0.21875, ((0, 2),))
    w_out = noise(arg_keys[5], (D, D), (D // 16) ** -0.5, 0.875, ((0, 2),))
    gain_mlp = jnp.clip(1.0 + 0.1 * jax.random.normal(arg_keys[6], (D,), jnp.float32), 0.5, 1.5).astype(jnp.bfloat16)
    w_up = noise(arg_keys[7], (D, FF), D ** -0.5, 0.21875, ((0, 2),))
    bias_up = noise(arg_keys[8], (FF,), 0.5, 3.0, ((0, 2),))
    w_down = noise(arg_keys[9], (FF, D), FF ** -0.5, 0.109375, ((0, 2),))
    bias_down = noise(arg_keys[10], (D,), 0.3, 2.0, ((0, 2),))
    out_grad = noise(arg_keys[11], (SEQS, 2 * LEN, D), 1.0, 6.0, ((0, 32),))
    return dict(clean_in=clean_in, noise_bits=noise_bits, mask_vector=mask_vector, gain_attn=gain_attn, w_qkv=w_qkv, w_out=w_out, gain_mlp=gain_mlp, w_up=w_up, bias_up=bias_up, w_down=w_down, bias_down=bias_down, out_grad=out_grad)


@jax.custom_vjp
def low(v):
    return lax.optimization_barrier(v.astype(jnp.bfloat16)).astype(jnp.float32)

@jax.custom_vjp
def low_back(v):
    return v

def low_keep(v):
    return (low(v), None)

def low_pass(kept, grad):
    return (grad,)

def back_keep(v):
    return (v, None)

def back_low(kept, grad):
    return (low(grad),)
low.defvjp(low_keep, low_pass)
low_back.defvjp(back_keep, back_low)
exact_mode = lax.Precision.HIGHEST
norm_floor = 1e-05
tanh_scale = 0.7978845608028654
cubic_weight = 0.044715
masked_logit = -1000000000.0

def root_mean_normalize(inputs):
    centered = inputs - lax.optimization_barrier(jnp.mean(inputs, axis=-1, keepdims=True))
    variance = lax.optimization_barrier(jnp.mean(centered * centered, axis=-1, keepdims=True))
    return centered * lax.rsqrt(variance + norm_floor)

def gelu_value(inputs):
    cubic = inputs * inputs * inputs
    return 0.5 * inputs * (1.0 + jnp.tanh(tanh_scale * (inputs + cubic_weight * cubic)))

def rotary_tables(length, heads, head_size):
    positions = jnp.arange(length).astype(jnp.float32)
    halfway = head_size // 2
    spacing = 10000.0 ** (-2.0 * jnp.arange(halfway).astype(jnp.float32) / head_size)
    angles = positions[:, None] * spacing[None, :]
    angles = jnp.concatenate([angles, angles], axis=1)
    angles = jnp.tile(angles, (2, heads))
    return (jnp.cos(angles), jnp.sin(angles))

def turned(inputs, heads):
    parts = inputs.reshape(inputs.shape[:-1] + (heads, 2, -1))
    return jnp.concatenate([-parts[..., 1:, :], parts[..., :1, :]], axis=-2).reshape(inputs.shape)

def visible_pairs(length, block):
    row_index = jnp.arange(2 * length)
    is_clean = row_index >= length
    block_of = row_index % length // block
    row_clean = is_clean[:, None]
    col_clean = is_clean[None, :]
    row_block = block_of[:, None]
    col_block = block_of[None, :]
    noisy_side = ~row_clean & (~col_clean & (row_block == col_block) | col_clean & (col_block < row_block))
    clean_side = row_clean & col_clean & (col_block <= row_block)
    return noisy_side | clean_side

def forward(clean_rows, masked, visible, cosine, sine_table, mask_vector, gain_attn, w_qkv, w_out, gain_mlp, w_up, bias_up, w_down, bias_down):
    noisy_rows = jnp.where(masked[..., None], mask_vector, clean_rows)
    residual_state = jnp.concatenate([noisy_rows, clean_rows], axis=1)
    attention_normalized_input = low(root_mean_normalize(residual_state) * gain_attn)
    joined = low_back(jnp.einsum('gtd,de->gte', attention_normalized_input, w_qkv, precision=exact_mode))
    query_pre = joined[..., :D]
    key_pre = joined[..., D:2 * D]
    queries = low(query_pre * cosine + turned(query_pre, H) * sine_table)
    keys = low(key_pre * cosine + turned(key_pre, H) * sine_table)
    values = low(joined[..., 2 * D:])
    head_shape = residual_state.shape[:2] + (H, HD)
    query_heads = queries.reshape(head_shape)
    key_heads = keys.reshape(head_shape)
    value_heads = values.reshape(head_shape)
    scores = low_back(jnp.einsum('gqhd,gkhd->ghqk', query_heads, key_heads, precision=exact_mode))
    logits = jnp.where(visible, scores * HD ** (-0.5), masked_logit)
    highest = lax.optimization_barrier(jnp.max(logits, axis=-1, keepdims=True))
    exponent = jnp.exp(logits - highest)
    probs = exponent / lax.optimization_barrier(jnp.sum(exponent, axis=-1, keepdims=True))
    mixed = jnp.einsum('ghqk,gkhd->gqhd', low(probs), value_heads, precision=exact_mode).reshape(residual_state.shape)
    mixed = low(low_back(mixed))
    post_attention_state = residual_state + low_back(jnp.einsum('gtd,de->gte', mixed, w_out, precision=exact_mode))
    feedforward_normalized_input = low(root_mean_normalize(post_attention_state) * gain_mlp)
    pre_act = low_back(jnp.einsum('gtd,df->gtf', feedforward_normalized_input, w_up, precision=exact_mode) + bias_up)
    activated = low(gelu_value(pre_act))
    return post_attention_state + low_back(jnp.einsum('gtf,fd->gtd', activated, w_down, precision=exact_mode) + bias_down)

def reference(clean_in, noise_bits, mask_vector, gain_attn, w_qkv, w_out, gain_mlp, w_up, bias_up, w_down, bias_down, out_grad):
    group_size = math.gcd(SEQS, max(1, 4096 // (2 * LEN)))
    rounds = SEQS // group_size
    params = tuple((argument.astype(jnp.float32) for argument in (mask_vector, gain_attn, w_qkv, w_out, gain_mlp, w_up, bias_up, w_down, bias_down)))
    cosine, sine_table = rotary_tables(LEN, H, HD)
    visible = visible_pairs(LEN, BLOCK)
    clean_all = clean_in.astype(jnp.float32).reshape(rounds, group_size, LEN, D)
    masked_all = (noise_bits == 1).reshape(rounds, group_size, LEN)
    cotangent_all = out_grad.astype(jnp.float32).reshape(rounds, group_size, 2 * LEN, D)

    def one_round(totals, inputs):
        clean_rows, masked, cotangent = inputs

        def apply_layer(clean_value, *weights):
            return forward(clean_value, masked, visible, cosine, sine_table, *weights)
        output, pullback = jax.vjp(apply_layer, clean_rows, *params)
        gradients = pullback(cotangent)
        updated = tuple((running + gradient for running, gradient in zip(totals, gradients[1:])))
        return (updated, (output.astype(jnp.bfloat16), gradients[0]))
    starting = tuple((jnp.zeros_like(argument) for argument in params))
    totals, (outputs, clean_grads) = lax.scan(one_round, starting, (clean_all, masked_all, cotangent_all))
    return (outputs.reshape(SEQS, 2 * LEN, D), clean_grads.reshape(SEQS, LEN, D), totals[0], totals[1], totals[2], totals[3], totals[4], totals[5], totals[6], totals[7], totals[8])
```

```python
import functools
import math

import jax
import jax.numpy as jnp
import numpy as np
from jax import lax
from jax.experimental import pallas as pl
from jax.experimental.pallas import tpu as pltpu
from jax.sharding import PartitionSpec as P

HD = 64
BLOCK = 16
NORM_FLOOR = 1e-05
TANH_SCALE = 0.7978845608028654
CUBIC = 0.044715
BF = jnp.bfloat16
F32 = jnp.float32
MESH = pl.DeviceIdType.MESH
LOGIT_SCALE = 0.125 * math.log2(math.e)
NN = (((1,), (0,)), ((), ()))
NT = (((1,), (1,)), ((), ()))
TN = (((0,), (0,)), ((), ()))


def dot(a, b, dims=NN):
    return lax.dot_general(a, b, dims, preferred_element_type=F32)


def mo(x, n):
    return pl.multiple_of(x, n)


def normalize(x):
    d = x - jnp.mean(x, axis=-1, keepdims=True)
    inv = lax.rsqrt(jnp.mean(d * d, axis=-1, keepdims=True) + NORM_FLOOR)
    return d * inv, inv


def normalize_backward(g, xhat, inv, gain):
    e = g * gain
    return inv * (
        e
        - jnp.mean(e, axis=-1, keepdims=True)
        - xhat * jnp.mean(e * xhat, axis=-1, keepdims=True)
    )


def layer_kernel(
    nbits,
    clean_h, noise, small_in, cos_r, sin_r, wq_h, wo_h, wu_h, wd_h, og_h,
    out_h, cg_h, fin, oq_h, oo_h, ou_h, od_h,
    small, prow, mcol, mbf, mbb, mbe,
    stream, normed, wq, wo, wu, wd, og,
    qkv, qaug, mixed, aa, nm, act, dpre, xs, xr, daf, db, dm, dks, dsn,
    gd, g1, ryd, ry1, rxd, rx1, rad, ra1, rbd, rb1, red, re1,
    sbuf, srec, ss, rs, ls,
):
    L = 384
    D = 768
    T = 2 * L
    NT3 = L // 128
    d = lax.axis_index("dp")
    f = lax.axis_index("fsdp")
    c = lax.rem(d, 2)
    bits = [lax.rem(lax.div(d, 2 ** (b + 1)), 2) for b in range(nbits)]
    sib = (d + 1 - 2 * c, f)
    ypeer = (d, 1 - f)
    peers = [(d + (1 - 2 * bits[b]) * 2 ** (b + 1), f) for b in range(nbits)]
    u = 2 * bits[1] + bits[0]
    sem = [0]
    lsem = [0]
    ends = []

    def take(n=1):
        k = sem[0]
        sem[0] += n
        return k

    def rc(k, src, dst, dev):
        return pltpu.make_async_remote_copy(
            src_ref=src, dst_ref=dst, send_sem=ss.at[k], recv_sem=rs.at[k],
            device_id=dev, device_id_type=MESH,
        )

    def remote(make, n=1):
        k = take(n)
        fam = lambda i=0: make(k + i, i)
        ends.append((fam, n))
        return fam

    def sent(fam):
        for at, (other_fam, n) in enumerate(ends):
            if other_fam is fam:
                for i in range(n):
                    fam(i).wait_send()
                ends.pop(at)
                return

    def local(src, dst):
        k = lsem[0]
        lsem[0] += 1
        return lambda: pltpu.make_async_copy(src, dst, ls.at[k])

    bar = pltpu.get_barrier_semaphore()
    for dev in [sib, ypeer] + peers:
        pl.semaphore_signal(bar, inc=1, device_id=dev, device_id_type=MESH)

    l_clean = [
        local(clean_h.at[0, pl.ds(128 * i, 128)], stream.at[pl.ds(256 * i + 128, 128)])
        for i in range(NT3)
    ]
    mine = mo(f * L, 128)
    other = mo((1 - f) * L, 128)
    l_wq = [
        local(
            wq_h.at[:, pl.ds(mo(j * D + c * L, 128), L)],
            wq.at[pl.ds(mine, L), pl.ds(j * L, L)],
        )
        for j in range(3)
    ]
    l_wo = local(wo_h, wo.at[pl.ds(mine, L)])
    l_wu = [
        local(
            wu_h.at[:, pl.ds(mo(h * 1536 + c * D, 128), D)],
            wu.at[pl.ds(mine, L), pl.ds(h * D, D)],
        )
        for h in range(2)
    ]
    l_wd = local(wd_h.at[pl.ds(mo(c * D, 128), D)], wd.at[pl.ds(mo(f * D, 128), D)])
    l_og = [
        local(
            og_h.at[0, pl.ds((r % 2) * L + 128 * (r // 2), 128)],
            og.at[pl.ds(128 * r, 128)],
        )
        for r in range(2 * NT3)
    ]
    for cp in l_clean + l_wq:
        cp().start()
    small[pl.ds(f, 1)] = small_in[...][None]

    def y_wq(unit):
        rows = mo(96 * unit, 16)
        return remote(
            lambda k, j: rc(
                k,
                wq_h.at[pl.ds(rows, 96), pl.ds(mo(j * D + c * L, 128), L)],
                wq.at[pl.ds(mo(f * L + rows, 16), 96), pl.ds(j * L, L)],
                ypeer,
            ),
            3,
        )

    yw_q = y_wq(u)
    yw_q2 = y_wq(3 - u)
    y_small = remote(lambda k, i: rc(k, small_in, small.at[f], ypeer))

    def spread(buf, base, unit_rows, unit, dev):
        rows = mo(base + unit_rows * unit, 16)
        return remote(
            lambda k, i: rc(
                k, buf.at[pl.ds(rows, unit_rows)], buf.at[pl.ds(rows, unit_rows)], dev
            )
        )

    xw_q = spread(wq, other, 96, u, peers[0])
    zw_q = spread(wq, other, 96, u, peers[1])
    yw_u = remote(
        lambda k, h: rc(
            k,
            wu_h.at[pl.ds(mo(96 * u, 16), 96), pl.ds(mo(h * 1536 + c * D, 128), D)],
            wu.at[pl.ds(mo(f * L + 96 * u, 16), 96), pl.ds(h * D, D)],
            ypeer,
        ),
        2,
    )
    ux, uz = 2 * bits[1] + 1 - bits[0], 2 * (1 - bits[1]) + bits[0]
    xw_u = spread(wu, other, 96, u, peers[0])
    zw_u = spread(wu, other, 96, u, peers[1])
    xw_u2 = spread(wu, other, 48, 2 * uz, peers[0])
    zw_u2 = spread(wu, other, 48, 2 * ux + 1, peers[1])
    odown = mo((1 - f) * D, 128)
    yw_d = remote(
        lambda k, i: rc(
            k,
            wd_h.at[pl.ds(mo(c * D + 192 * u, 16), 192)],
            wd.at[pl.ds(mo(f * D + 192 * u, 16), 192)],
            ypeer,
        )
    )
    xw_d = spread(wd, odown, 192, u, peers[0])
    zw_d = spread(wd, odown, 192, u, peers[1])
    xw_d2 = spread(wd, odown, 96, 2 * uz, peers[0])
    zw_d2 = spread(wd, odown, 96, 2 * ux + 1, peers[1])
    yw_o = remote(
        lambda k, i: rc(
            k,
            wo_h.at[pl.ds(mo(192 * c + 96 * bits[0], 16), 96)],
            wo.at[pl.ds(mo(f * L + 192 * c + 96 * bits[0], 16), 96)],
            ypeer,
        )
    )
    xw_o = spread(wo, mo(other + 192 * c, 16), 96, bits[0], peers[0])
    sw_o = spread(wo, other, 192, c, sib)

    s_norm = remote(
        lambda k, i: rc(
            k, normed.at[pl.ds(mo(256 * i, 16), 256)],
            normed.at[pl.ds(mo(T + 256 * i, 16), 256)], sib,
        ),
        NT3,
    )
    s_og = remote(lambda k, i: rc(k, og.at[pl.ds(0, T)], og.at[pl.ds(T, T)], sib))

    def mixed_copy(k, i):
        s = 1 - i // 3 if isinstance(i, int) else 1 - lax.div(i, 3)
        p = i % 3 if isinstance(i, int) else lax.rem(i, 3)
        lanes = pl.ds(mo(c * L + 128 * p, 128), 128)
        return rc(
            k, mixed.at[pl.ds(mo(s * T, 16), T), lanes],
            mixed.at[pl.ds(mo((1 - s) * T, 16), T), lanes], sib,
        )

    s_mix = remote(mixed_copy, 6)

    def rows_copy(buf, src0, dst, dst0):
        return remote(
            lambda k, i: rc(
                k, buf.at[pl.ds(mo(src0 + 256 * i, 16), 256)],
                dst.at[pl.ds(mo(dst0 + 256 * i, 16), 256)], sib,
            ),
            NT3,
        )

    s_nm = rows_copy(nm, 0, nm, T)
    s_dn = rows_copy(xs, 0, xr, 0)
    s_db = rows_copy(db, 0, db, T)
    s_bo = rows_copy(xs, 0, xr, 0)
    right = pl.ds(D, D)
    s_da = remote(
        lambda k, i: rc(
            k, dpre.at[pl.ds(mo(256 * i, 16), 256), right],
            dpre.at[pl.ds(mo(T + 256 * i, 16), 256), right], sib,
        ),
        NT3,
    )

    class Chunk:
        pass

    chunks = {}

    def make_chunk(name, g, gbase, nr, l0, nl, recv, rbase, oref, orow, olane, blk):
        ch = Chunk()
        ch.name, ch.nr, ch.blk = name, nr, blk
        lanes = pl.ds(l0, nl)
        ry, rx, ra, rb, re = recv
        offs = [0]
        for j in range(3):
            offs.append(offs[-1] + bits[j] * (nr >> (j + 1)))

        def greg(off, n):
            return g.at[pl.ds(mo(gbase(f) + off, 16), n), lanes]

        def rreg(buf, n):
            return buf.at[pl.ds(rbase * n // 256 if rbase else 0, n), lanes]

        def oreg(off, n):
            return oref.at[pl.ds(mo(orow(c) + off, 16), n), pl.ds(mo(olane(c), 128), nl)]

        ch.y = remote(
            lambda k, i: rc(
                k, g.at[pl.ds(mo(gbase(1 - f), 16), nr), lanes], rreg(ry, nr), ypeer
            )
        )
        recvs = (rx, ra, rb)
        ch.rs = []
        for j in range(3):
            n = nr >> (j + 1)
            ch.rs.append(
                remote(
                    lambda k, i, j=j, n=n: rc(
                        k, greg(offs[j] + (1 - bits[j]) * n, n), rreg(recvs[j], n), peers[j]
                    )
                )
            )
        n3 = nr >> 3
        ch.extra = [
            remote(
                lambda k, i, j=j: rc(k, greg(offs[3], n3), rreg(re.at[j - 3], n3), peers[j])
            )
            for j in range(3, nbits)
        ]
        ch.own = local(greg(offs[3], n3), oreg(offs[3], n3))
        ch.ag2 = remote(
            lambda k, i: rc(k, greg(offs[3], n3), oreg(offs[3], n3), peers[2])
        )
        ch.ag1 = remote(
            lambda k, i: rc(k, oreg(offs[2], nr >> 2), oreg(offs[2], nr >> 2), peers[1])
        )
        ch.ag0 = remote(
            lambda k, i: rc(k, oreg(offs[1], nr >> 1), oreg(offs[1], nr >> 1), peers[0])
        )
        ch.ags = remote(lambda k, i: rc(k, oreg(0, nr), oreg(0, nr), sib))

        def add(off, n, rref):
            step = min(blk, n)
            gr = greg(off, n)

            def body(i, carry):
                sl = pl.ds(mo(i * step, 16), step)
                gr[sl, :] = (gr[sl, :].astype(F32) + rref[sl, :].astype(F32)).astype(BF)
                return carry

            lax.fori_loop(0, n // step, body, 0)

        def e_y():
            ch.y().wait_recv()
            add(0, nr, rreg(ry, nr))
            ch.rs[0]().start()

        def e_rs(j):
            ch.rs[j]().wait_recv()
            n = nr >> (j + 1)
            add(offs[j + 1], n, rreg(recvs[j], n))
            if j < 2:
                ch.rs[j + 1]().start()
                return
            for m, fam in enumerate(ch.extra):
                fam().start()
                sent(fam)
                fam().wait_recv()
                add(offs[3], n3, rreg(re.at[m], n3))
            ch.own().start()
            ch.ag2().start()

        def e_ag2():
            ch.own().wait()
            ch.ag2().wait_recv()
            ch.ag1().start()

        def e_ag1():
            ch.ag1().wait_recv()
            ch.ag0().start()

        def e_ag0():
            ch.ag0().wait_recv()
            ch.ags().start()

        def e_end():
            ch.ags().wait_recv()

        ch.events = [e_y, lambda: e_rs(0), lambda: e_rs(1), lambda: e_rs(2), e_ag2, e_ag1, e_ag0, e_end]
        chunks[name] = ch
        return ch

    zero = lambda x: 0
    recv_d = (ryd, rxd, rad, rbd, red)
    recv_1 = (ry1, rx1, ra1, rb1, re1)
    for k in range(3):
        make_chunk(
            f"d{k}", gd, lambda h, k=k: h * D + 256 * k, 256, 0, D, recv_d, 256 * k,
            od_h, lambda core, k=k: core * D + 256 * k, zero, 32,
        )
    for t in range(6):
        make_chunk(
            f"u{t}", g1, lambda h: h * L, L, 256 * t, 256, recv_1, 0,
            ou_h, zero, lambda core, t=t: (t // 3) * 1536 + core * D + (t % 3) * 256, 96,
        )
    for j in range(3):
        make_chunk(
            f"q{j}", g1, lambda h: h * L, L, 1536 + L * j, L, recv_1, 0,
            oq_h, zero, lambda core, j=j: j * D + core * L, 48,
        )
    make_chunk(
        "o", g1, lambda h: h * L, L, 1536 + 3 * L, L, recv_1, 0,
        oo_h, zero, lambda core: core * L, 48,
    )

    def event(name, stage):
        return chunks[name].events[stage]

    pl.semaphore_wait(bar, 2 + nbits)
    y_small().start()
    for j in range(3):
        yw_q(j).start()
    for j in range(3):
        yw_q2(j).start()
    for h in range(2):
        yw_u(h).start()
    yw_o().start()
    yw_d().start()
    for cp in l_og + l_wu + [l_wo, l_wd]:
        cp().start()

    lane = lax.broadcasted_iota(jnp.int32, (1, 128), 1)
    low_half = lane < HD
    rot_low = lax.rem(lane, HD) < HD // 2
    bm = [jnp.where(low_half, 1.0, 0.0).astype(BF), jnp.where(low_half, 0.0, 1.0).astype(BF)]
    selm = [low_half, lane >= HD]
    spare = [HD, 0]
    ir = lax.div(lax.broadcasted_iota(jnp.int32, (128, 128), 0), BLOCK)
    ic = lax.div(lax.broadcasted_iota(jnp.int32, (128, 128), 1), BLOCK)
    neg = -1e30
    mbf[0:128, :] = jnp.where(ic < ir, 0.0, neg)
    mbf[128:256, :] = jnp.where(ic <= ir, 0.0, neg)
    mbb[:, 0:128] = jnp.where(ir < ic, 0.0, neg)
    mbb[:, 128:256] = jnp.where(ir <= ic, 0.0, neg)
    mbe[...] = jnp.where(ir == ic, 0.0, neg)
    nf = noise[...].astype(F32)
    for i in range(NT3):
        mcol[128 * i : 128 * i + 128, :] = jnp.broadcast_to(
            nf[:, 128 * i : 128 * i + 128], (128, 128)
        ).T
    sbuf[0] = jnp.zeros((8, D), F32)

    y_small().wait_recv()
    prow[:, 0:L] = small[0]
    prow[:, L:D] = small[1]
    mvec = prow[0:1, :]
    gain_a = prow[1:2, :]
    gain_m = prow[2:3, :]
    bias_d = prow[3:4, :]
    bias_u = jnp.concatenate(
        [small[h, pl.ds(4 + 2 * c + r, 1), :] for h in range(2) for r in range(2)], axis=1
    )

    def wide(m):
        return jnp.concatenate([m] * (D // 128), axis=1)

    for i in range(NT3):
        l_clean[i]().wait()

    def attn_norm(i, carry):
        n0 = mo(256 * i, 128)
        x = stream[pl.ds(n0 + 128, 128), :].astype(F32)
        m = wide(mcol[pl.ds(mo(128 * i, 128), 128), :])
        y = jnp.where(m > 0.5, mvec, x)
        stream[pl.ds(n0, 128), :] = y.astype(BF)
        normed[pl.ds(n0, 128), :] = (normalize(y)[0] * gain_a).astype(BF)
        normed[pl.ds(n0 + 128, 128), :] = (normalize(x)[0] * gain_a).astype(BF)
        s_norm(i).start()
        return carry

    lax.fori_loop(0, NT3, attn_norm, 0)

    for j in range(3):
        l_wq[j]().wait()
        yw_q(j).wait_recv()
    xw_q().start()
    zw_q().start()
    for i in range(NT3):
        s_norm(i).wait_recv()
    for cp in l_og:
        cp().wait()
    s_og().start()
    for j in range(3):
        yw_q2(j).wait_recv()
    xw_q().wait_recv()
    zw_q().wait_recv()

    def turn(x, cos, sin):
        return x * cos + jnp.where(rot_low, pltpu.roll(x, 96, 1), pltpu.roll(x, 32, 1)) * sin

    def rows2(tab, i):
        t = tab[pl.ds(mo(128 * i, 128), 128), :]
        return jnp.concatenate([t, t], axis=0)

    def qkv_rows(r, carry):
        rows = pl.ds(mo(256 * r, 128), 256)
        joined = dot(normed[rows, :], wq[...])
        i = lax.rem(r, NT3)
        cos, sin = rows2(cos_r, i), rows2(sin_r, i)
        for p in range(6):
            x = joined[:, 128 * p : 128 * p + 128]
            qkv[rows, 128 * p : 128 * p + 128] = turn(x, cos, sin).astype(BF)
        qkv[rows, 2 * L : 3 * L] = joined[:, 2 * L : 3 * L].astype(BF)
        return carry

    lax.fori_loop(0, 2 * NT3, qkv_rows, 0)
    for h in range(2):
        l_wu[h]().wait()
        yw_u(h).wait_recv()
    xw_u().start()
    zw_u().start()

    def run_at(idx, table):
        for k, fns in table.items():
            def go(fns=fns):
                for fn in fns:
                    fn()
            pl.when(idx == k)(go)

    def w_o_1():
        l_wo().wait()
        yw_o().wait_recv()
        xw_o().start()

    def w_u_2():
        xw_u().wait_recv()
        zw_u().wait_recv()
        xw_u2().start()
        zw_u2().start()

    def w_o_2():
        xw_o().wait_recv()
        sw_o().start()

    def w_d_1():
        l_wd().wait()
        yw_d().wait_recv()
        xw_d().start()
        zw_d().start()

    def w_d_2():
        xw_d().wait_recv()
        zw_d().wait_recv()
        xw_d2().start()
        zw_d2().start()

    fwd_events = {2: [w_o_1], 3: [w_u_2, w_o_2], 4: [w_d_1]}

    def attn_fwd(n, carry):
        s, p = 1 - lax.div(n, 3), lax.rem(n, 3)
        r0 = s * T
        lq = pl.ds(mo(128 * p, 128), 128)
        lk = pl.ds(mo(L + 128 * p, 128), 128)
        lv = pl.ds(mo(2 * L + 128 * p, 128), 128)

        def rws(a, m):
            return pl.ds(mo(r0 + a, 128), m)

        for i in range(NT3):
            res = []
            for a in range(2):
                q = qkv[rws(256 * i, 256), lq] * bm[a]
                kc = jnp.concatenate(
                    [qkv[rws(256 * j + 128, 128), lk] for j in range(i + 1)], axis=0
                )
                vc = jnp.concatenate(
                    [qkv[rws(256 * j + 128, 128), lv] for j in range(i + 1)], axis=0
                ) * bm[a] + bm[1 - a]
                vn = qkv[rws(256 * i, 128), lv] * bm[a] + bm[1 - a]
                s1 = dot(q, kc, NT) * LOGIT_SCALE
                sn = dot(q[:128], qkv[rws(256 * i, 128), lk], NT) * LOGIT_SCALE + mbe[...]
                last = s1[:, 128 * i :] + mbf[...]
                s1 = last if i == 0 else jnp.concatenate([s1[:, : 128 * i], last], axis=1)
                m1 = jnp.max(s1, axis=1, keepdims=True)
                mn = jnp.maximum(m1[:128], jnp.max(sn, axis=1, keepdims=True))
                m = jnp.concatenate([mn, m1[128:]], axis=0)
                p1 = jnp.exp2(s1 - m).astype(BF)
                pn = jnp.exp2(sn - mn).astype(BF)
                o = dot(p1, vc)
                o = jnp.concatenate([o[:128] + dot(pn, vn), o[128:]], axis=0)
                val = (m + jnp.log2(o)) * (-1.0 / LOGIT_SCALE)
                hi = val.astype(BF).astype(F32)
                mid = (val - hi).astype(BF).astype(F32)
                lo = val - hi - mid
                extra = jnp.where(
                    lane == spare[a], hi,
                    jnp.where(lane == spare[a] + 1, mid, jnp.where(lane == spare[a] + 2, lo, 0.0)),
                )
                qaug[rws(256 * i, 256), pl.ds(mo(256 * p + 128 * a, 128), 128)] = jnp.where(
                    selm[a], q.astype(F32), extra
                ).astype(BF)
                res.append(o)
            data = jnp.where(low_half, res[0], res[1])
            sums = pltpu.roll(jnp.where(low_half, res[1], res[0]), HD, 1)
            mixed[rws(256 * i, 256), pl.ds(mo(c * L + 128 * p, 128), 128)] = (
                data * (1.0 / sums)
            ).astype(BF)
        s_mix(n).start()
        run_at(n, fwd_events)
        return carry

    lax.fori_loop(0, 6, attn_fwd, 0)

    sw_o().wait_recv()
    for n in range(3):
        s_mix(n).wait_recv()

    def out_proj(i, carry):
        rows = pl.ds(mo(256 * i, 128), 256)
        x = stream[rows, :].astype(F32) + dot(mixed[rows, :], wo[...])
        aa[rows, :] = x
        nm[rows, :] = (normalize(x)[0] * gain_m).astype(BF)
        s_nm(i).start()
        return carry

    lax.fori_loop(0, NT3, out_proj, 0)
    xw_u2().wait_recv()
    zw_u2().wait_recv()
    s_og().wait_recv()
    for i in range(NT3):
        s_nm(i).wait_recv()

    def loop_a(n, carry):
        odd = lax.rem(n, 2)
        h = (1 - f) * (1 - odd) + f * odd
        t = 3 * h + lax.div(n, 2)
        lanes = pl.ds(mo(256 * t, 128), 256)
        bu = jnp.zeros((1, 256), F32)
        for tt in range(6):
            bu = jnp.where(t == tt, bias_u[:, 256 * tt : 256 * tt + 256], bu)

        def rows_a(r, carry):
            rows = pl.ds(mo(512 * r, 128), 512)
            pre = dot(nm[rows, :], wu[:, lanes]) + bu
            sq = pre * pre
            half = 0.5 + 0.5 * jnp.tanh(pre * (TANH_SCALE + TANH_SCALE * CUBIC * sq))
            a = pre * half
            act[rows, lanes] = a.astype(BF)
            slope = half + 2.0 * a * (1.0 - half) * (
                TANH_SCALE + 3.0 * CUBIC * TANH_SCALE * sq
            )
            dpre[rows, lanes] = slope.astype(BF)
            return carry

        lax.fori_loop(0, 3, rows_a, 0)
        gd[pl.ds(mo(256 * t, 128), 256), :] = dot(act[:, lanes], og[...], TN).astype(BF)
        for k in range(3):
            pl.when(n == 2 * k)(lambda k=k: chunks[f"d{k}"].y().start())
        run_at(n, {0: [w_d_2]})
        return carry

    lax.fori_loop(0, 6, loop_a, 0)
    xw_d2().wait_recv()
    zw_d2().wait_recv()

    def loop_b(t, carry):
        lanes = pl.ds(mo(256 * t, 128), 256)

        def rows_b(r, tot):
            rows = pl.ds(mo(512 * r, 128), 512)
            g = dot(og[rows, :], wd[lanes, :], NT) * dpre[rows, lanes].astype(F32)
            dpre[rows, lanes] = g.astype(BF)
            return tot + jnp.sum(g, axis=0, keepdims=True)

        tot = lax.fori_loop(0, 3, rows_b, jnp.zeros((1, 256), F32))
        for tt in range(6):
            def put(tt=tt):
                sbuf[0, 4 + tt // 3 : 5 + tt // 3, 256 * (tt % 3) : 256 * (tt % 3) + 256] = tot
            pl.when(t == tt)(put)
        run_at(t, ev["b"])
        return carry

    ev = {
        "b": {1: [event("d0", 0)], 3: [event("d0", 1)], 5: [event("d0", 2), event("d1", 0)]},
        "u0": [event("d0", 3), event("d1", 1)],
        "u1": [event("d0", 4), event("d1", 2), event("d2", 0)],
        "dn": [event("d0", 5), event("d1", 3), event("d2", 1), event("u0", 0)],
        "dm": [event("d0", 6), event("d1", 4), event("d2", 2), event("u1", 0), event("u0", 1)],
        "att": {
            0: [event("d1", 5), event("d2", 3), event("u2", 0), event("u0", 2), event("u1", 1)],
            1: [event("d1", 6), event("d2", 4), event("u3", 0), event("u0", 3), event("u1", 2), event("u2", 1)],
            2: [event("d2", 5), event("u4", 0), event("u0", 4), event("u1", 3), event("u2", 2), event("u3", 1)],
            3: [event("d2", 6), event("u5", 0), event("u0", 5), event("u1", 4), event("u2", 3), event("u3", 2), event("u4", 1)],
            4: [event("u0", 6), event("u1", 5), event("u2", 4), event("u3", 3), event("u4", 2), event("u5", 1)],
            5: [event("o", 0), event("u1", 6), event("u2", 5), event("u3", 4), event("u4", 3), event("u5", 2)],
        },
        "qg": [event("o", 1), event("u2", 6), event("u3", 5), event("u4", 4), event("u5", 3)],
        "da": [event("q0", 0), event("o", 2), event("u3", 6), event("u4", 5), event("u5", 4)],
        "bo": [event("q1", 0), event("q0", 1), event("o", 3), event("u4", 6), event("u5", 5)],
    }
    tail = [
        event("q2", 0), event("q1", 1), event("q0", 2), event("o", 4), event("u5", 6),
        event("q2", 1), event("q1", 2), event("q0", 3), event("o", 5),
        event("q2", 2), event("q1", 3), event("q0", 4), event("o", 6),
        event("q2", 3), event("q1", 4), event("q0", 5),
        event("q2", 4), event("q1", 5), event("q0", 6),
        event("q2", 5), event("q1", 6), event("q2", 6),
    ] + [ch.events[7] for ch in chunks.values()]

    def handle(key):
        for fn in ev[key]:
            fn()

    lax.fori_loop(0, 6, loop_b, 0)

    for h in range(2):
        g1[:, h * D : h * D + D] = dot(nm[...], dpre[:, h * D : h * D + D], TN).astype(BF)
        for t in range(3 * h, 3 * h + 3):
            chunks[f"u{t}"].y().start()
        handle(f"u{h}")

    def dn_other(i, carry):
        x = dot(dpre[pl.ds(mo(T + 256 * i, 128), 256), :], wu[...], NT)
        xs[pl.ds(mo(256 * i, 128), 256), :] = x.astype(BF)
        s_dn(i).start()
        return carry

    lax.fori_loop(0, NT3, dn_other, 0)

    def dn_own(i, sums):
        rows = pl.ds(mo(256 * i, 128), 256)
        g = dot(dpre[rows, :], wu[...], NT)
        s_dn(i).wait_recv()
        g = g + xr[rows, :].astype(F32)
        xhat, inv = normalize(aa[rows, :])
        ograd = og[rows, :].astype(F32)
        after = ograd + normalize_backward(g, xhat, inv, gain_m)
        daf[rows, :] = after
        db[rows, :] = after.astype(BF)
        s_db(i).start()
        return (
            sums[0] + jnp.sum(g * xhat, axis=0, keepdims=True),
            sums[1] + jnp.sum(ograd, axis=0, keepdims=True),
        )

    zrow = jnp.zeros((1, D), F32)
    g_gain_m, g_bias_d = lax.fori_loop(0, NT3, dn_own, (zrow, zrow))
    sbuf[0, 2:3, :] = g_gain_m
    sbuf[0, 3:4, :] = g_bias_d
    handle("dn")

    wo_rows = pl.ds(mo(c * L, 128), L)
    dm[0:T, :] = dot(db[0:T, :], wo[wo_rows, :], NT).astype(BF)
    for i in range(NT3):
        s_db(i).wait_recv()
    dm[T : 2 * T, :] = dot(db[T : 2 * T, :], wo[wo_rows, :], NT).astype(BF)
    for n in range(3, 6):
        s_mix(n).wait_recv()
    g1[:, 1536 + 3 * L : 1536 + 4 * L] = dot(mixed[...], db[:, wo_rows], TN).astype(BF)
    chunks["o"].y().start()
    handle("dm")

    one_q = [
        jnp.where((lane >= s) & (lane < s + 3), 1.0, 0.0).astype(BF) for s in spare
    ]
    one_d = [
        jnp.where((lane >= s) & (lane < s + 2), 1.0, 0.0).astype(BF) for s in spare
    ]

    def attn_bwd(n, carry):
        s, p = lax.div(n, 3), lax.rem(n, 3)
        r0 = s * T
        lq = pl.ds(mo(128 * p, 128), 128)
        lk = pl.ds(mo(L + 128 * p, 128), 128)
        lv = pl.ds(mo(2 * L + 128 * p, 128), 128)

        def rws(a, m):
            return pl.ds(mo(r0 + a, 128), m)

        dog = dm[rws(0, T), lq]
        prod = dog.astype(F32) * mixed[
            rws(0, T), pl.ds(mo(c * L + 128 * p, 128), 128)
        ].astype(F32)
        doa = []
        for a in range(2):
            val = -jnp.sum(jnp.where(selm[a], prod, 0.0), axis=1, keepdims=True)
            hi = val.astype(BF).astype(F32)
            mid = val - hi
            extra = jnp.where(lane == spare[a], hi, jnp.where(lane == spare[a] + 1, mid, 0.0))
            doa.append(jnp.where(selm[a], dog.astype(F32), extra).astype(BF))
        for kt in range(NT3):
            q0 = 256 * kt
            nq = T - q0
            pts, dss, ptn, dsnn = [], [], [], []
            for a in range(2):
                qa = qaug[rws(q0, nq), pl.ds(mo(256 * p + 128 * a, 128), 128)]
                da = doa[a][q0:]
                kc = qkv[rws(q0 + 128, 128), lk] * bm[a] + one_q[a]
                kn = qkv[rws(q0, 128), lk] * bm[a] + one_q[a]
                vc = qkv[rws(q0 + 128, 128), lv] * bm[a] + one_d[a]
                vn = qkv[rws(q0, 128), lv] * bm[a] + one_d[a]
                st = dot(kc, qa, NT) * LOGIT_SCALE
                first = st[:, :256] + mbb[...]
                st = first if nq == 256 else jnp.concatenate([first, st[:, 256:]], axis=1)
                pt = jnp.exp2(st)
                ds = pt * dot(vc, da, NT)
                dpre[pl.ds(512 * a + 128 * kt, 128), pl.ds(q0, nq)] = ds.astype(BF)
                pts.append(pt.astype(BF))
                dss.append(ds.astype(BF))
                pn = jnp.exp2(dot(kn, qa[:128], NT) * LOGIT_SCALE + mbe[...])
                dn = pn * dot(vn, da[:128], NT)
                dsn[a, kt] = dn.astype(BF)
                ptn.append(pn.astype(BF))
                dsnn.append(dn.astype(BF))
            dom = [dm[rws(q0, nq), lq] * bm[a] for a in range(2)]
            qm = [qkv[rws(q0, nq), lq] * bm[a] for a in range(2)]
            domc, qmc = jnp.concatenate(dom, axis=0), jnp.concatenate(qm, axis=0)
            domn = jnp.concatenate([x[:128] for x in dom], axis=0)
            qmn = jnp.concatenate([x[:128] for x in qm], axis=0)
            dks[pl.ds(q0 + 128, 128), :] = dot(jnp.concatenate(dss, axis=1), qmc)
            dks[pl.ds(q0, 128), :] = dot(jnp.concatenate(dsnn, axis=1), qmn)
            qkv[rws(q0 + 128, 128), lv] = dot(jnp.concatenate(pts, axis=1), domc).astype(BF)
            qkv[rws(q0, 128), lv] = dot(jnp.concatenate(ptn, axis=1), domn).astype(BF)
        for i in range(NT3):
            dq = None
            for a in range(2):
                kc = jnp.concatenate(
                    [qkv[rws(256 * j + 128, 128), lk] for j in range(i + 1)], axis=0
                ) * bm[a]
                part = dot(
                    dpre[pl.ds(512 * a, 128 * (i + 1)), pl.ds(256 * i, 256)], kc, TN
                )
                pn = dot(dsn[a, i], qkv[rws(256 * i, 128), lk] * bm[a], TN)
                part = jnp.concatenate([part[:128] + pn, part[128:]], axis=0)
                dq = part if dq is None else dq + part
            cos, sin = rows2(cos_r, i), rows2(sin_r, i)
            qkv[rws(256 * i, 256), lq] = (turn(dq, cos, -sin) * 0.125).astype(BF)
        for i in range(NT3):
            cos, sin = rows2(cos_r, i), rows2(sin_r, i)
            dk = dks[pl.ds(256 * i, 256), :]
            qkv[rws(256 * i, 256), lk] = (turn(dk, cos, -sin) * 0.125).astype(BF)
        run_at(n, ev["att"])
        return carry

    lax.fori_loop(0, 6, attn_bwd, 0)

    for j in range(3):
        g1[:, 1536 + L * j : 1536 + L * j + L] = dot(
            normed[...], qkv[:, L * j : L * j + L], TN
        ).astype(BF)
        chunks[f"q{j}"].y().start()
    handle("qg")

    def da_other(i, carry):
        x = dot(qkv[pl.ds(mo(T + 256 * i, 128), 256), :], wq[...], NT)
        dpre[pl.ds(mo(256 * i, 128), 256), right] = x.astype(BF)
        s_da(i).start()
        return carry

    lax.fori_loop(0, NT3, da_other, 0)
    cg_out = [
        local(daf.at[pl.ds(256 * i, 128)], cg_h.at[0, pl.ds(128 * i, 128)]) for i in range(NT3)
    ]

    def da_own(i, sums):
        rows = pl.ds(mo(256 * i, 128), 256)
        g = dot(qkv[rows, :], wq[...], NT)
        s_da(i).wait_recv()
        g = g + dpre[pl.ds(mo(T + 256 * i, 128), 256), right].astype(F32)
        xhat, inv = normalize(stream[rows, :].astype(F32))
        ds = daf[rows, :] + normalize_backward(g, xhat, inv, gain_a)
        m = wide(mcol[pl.ds(mo(128 * i, 128), 128), :]) > 0.5
        daf[pl.ds(mo(256 * i, 128), 128), :] = ds[128:] + jnp.where(m, 0.0, ds[:128])
        return (
            sums[0] + jnp.sum(jnp.where(m, ds[:128], 0.0), axis=0, keepdims=True),
            sums[1] + jnp.sum(g * xhat, axis=0, keepdims=True),
        )

    g_mask, g_gain_a = lax.fori_loop(0, NT3, da_own, (zrow, zrow))
    for cp in cg_out:
        cp().start()
    sbuf[0, 0:1, :] = g_mask
    sbuf[0, 1:2, :] = g_gain_a

    smalls = [
        remote(lambda k, i, n=n, dev=dev: rc(k, sbuf.at[n], srec.at[n], dev))
        for n, dev in enumerate([sib, ypeer] + peers)
    ]
    s_last = remote(
        lambda k, i: rc(k, sbuf.at[nbits + 2], srec.at[nbits + 2], sib)
    )
    row = lax.broadcasted_iota(jnp.int32, (8, D), 0)

    def small_step(n):
        smalls[n]().wait_recv()
        new = srec[n]
        if n == 0:
            new = jnp.where(row < 4, new, 0.0)
        sbuf[n + 1] = sbuf[n] + new
        if n + 1 < len(smalls):
            smalls[n + 1]().start()
        else:
            s_last().start()

    smalls[0]().start()
    handle("da")
    small_step(0)

    sent(s_dn)

    def bo_other(i, carry):
        x = dot(act[pl.ds(mo(T + 256 * i, 128), 256), :], wd[...])
        xs[pl.ds(mo(256 * i, 128), 256), :] = x.astype(BF)
        s_bo(i).start()
        return carry

    lax.fori_loop(0, NT3, bo_other, 0)
    small_step(1)
    sent(s_nm)

    def bo_own(i, carry):
        rows = pl.ds(mo(256 * i, 128), 256)
        x = aa[rows, :] + dot(act[rows, :], wd[...])
        s_bo(i).wait_recv()
        nm[rows, :] = (x + xr[rows, :].astype(F32) + bias_d).astype(BF)
        return carry

    lax.fori_loop(0, NT3, bo_own, 0)
    l_out = [
        local(
            nm.at[pl.ds(128 * r, 128)],
            out_h.at[0, pl.ds((r % 2) * L + 128 * (r // 2), 128)],
        )
        for r in range(2 * NT3)
    ]
    for cp in l_out:
        cp().start()
    handle("bo")
    for n in range(2, len(smalls)):
        tail.insert(3 * (n - 1) - 3, lambda n=n: small_step(n))
    for fn in tail:
        fn()
    s_last().wait_recv()
    last = len(smalls)
    tot = sbuf[last]
    oth = srec[last]
    mh = jnp.where(f == 0, tot[0:4, 0:L], tot[0:4, L:D])
    fin[0:4, :] = mh
    for core_off, x in ((c, tot), (1 - c, oth)):
        v = jnp.where(f == 0, x[4:5, :], x[5:6, :])
        fin[pl.ds(4 + 2 * core_off, 1), :] = v[:, 0:L]
        fin[pl.ds(5 + 2 * core_off, 1), :] = v[:, L:D]
    for cp in l_out + cg_out:
        cp().wait()
    for fam, n in list(ends):
        sent(fam)


def tables(length):
    pos = np.arange(length, dtype=np.float32)
    half = HD // 2
    spacing = (10000.0 ** (-2.0 * np.arange(half, dtype=np.float64) / HD)).astype(np.float32)
    ang = (pos[:, None] * spacing[None, :]).astype(np.float64)
    cos = np.tile(np.cos(ang), (1, 4)).astype(np.float32)
    sin = np.sin(ang)
    sin = np.tile(np.concatenate([-sin, sin], axis=1), (1, 2)).astype(np.float32)
    return cos, sin


def on_device(
    nbits, clean_in, noise_bits, mask_vector, gain_attn, w_qkv, w_out, gain_mlp,
    w_up, bias_up, w_down, bias_down, out_grad,
):
    L, D, T = 384, 768, 768
    small = jnp.concatenate(
        [mask_vector, gain_attn, gain_mlp, bias_down, bias_up]
    ).reshape(8, L).astype(F32)
    cos, sin = tables(L)
    nx = max(1, nbits - 3)
    hbm = pl.BlockSpec(memory_space=pltpu.HBM)
    vm = pl.BlockSpec(memory_space=pltpu.VMEM)
    scratch = [
        ((2, 8, L), F32), ((8, D), F32), ((L, 128), F32), ((256, 128), F32),
        ((128, 256), F32), ((128, 128), F32),
        ((T, D), BF), ((2 * T, D), BF), ((D, 1152), BF), ((D, D), BF), ((D, 1536), BF),
        ((1536, D), BF), ((2 * T, D), BF),
        ((2 * T, 1152), BF), ((2 * T, D), BF), ((2 * T, D), BF), ((T, D), F32),
        ((2 * T, D), BF), ((2 * T, 1536), BF), ((2 * T, 1536), BF), ((T, D), BF),
        ((T, D), BF), ((T, D), F32), ((2 * T, D), BF), ((2 * T, L), BF), ((T, 128), F32),
        ((2, 3, 128, 128), BF),
        ((1536, D), BF), ((D, 3072), BF),
        ((D, D), BF), ((L, 3072), BF), ((L, D), BF), ((192, 3072), BF),
        ((192, D), BF), ((96, 3072), BF), ((96, D), BF), ((48, 3072), BF),
        ((nx, 96, D), BF), ((nx, 48, 3072), BF),
        ((nbits + 3, 8, D), F32), ((nbits + 3, 8, D), F32),
    ]
    if nbits == 3:
        scratch[37] = ((1, 16, 128), BF)
        scratch[38] = ((1, 16, 128), BF)
    nsem = 240 + 20 * nx
    outs = pl.pallas_call(
        functools.partial(layer_kernel, nbits),
        out_shape=[
            jax.ShapeDtypeStruct((1, T, D), BF),
            jax.ShapeDtypeStruct((1, L, D), F32),
            jax.ShapeDtypeStruct((8, L), F32),
            jax.ShapeDtypeStruct((L, 2304), BF),
            jax.ShapeDtypeStruct((L, D), BF),
            jax.ShapeDtypeStruct((L, 3072), BF),
            jax.ShapeDtypeStruct((1536, D), BF),
        ],
        in_specs=[hbm, vm, vm, vm, vm, hbm, hbm, hbm, hbm, hbm],
        out_specs=[hbm, hbm, vm, hbm, hbm, hbm, hbm],
        scratch_shapes=[pltpu.VMEM(s, t) for s, t in scratch]
        + [
            pltpu.SemaphoreType.DMA((nsem,)),
            pltpu.SemaphoreType.DMA((nsem,)),
            pltpu.SemaphoreType.DMA((64,)),
        ],
        compiler_params=pltpu.CompilerParams(
            collective_id=0, has_side_effects=True, vmem_limit_bytes=64 * 2**20
        ),
        name="layer",
    )(clean_in, noise_bits, small, cos, sin, w_qkv, w_out, w_up, w_down, out_grad)
    block_out, clean_grad, fin, gq, go, gu, gdn = outs
    return (
        block_out, clean_grad, fin[0], fin[1], gq.astype(F32), go.astype(F32), fin[2],
        gu.astype(F32), fin[4:8].reshape(1536), gdn.astype(F32), fin[3],
    )


def solution(mesh):
    nbits = int(math.log2(mesh.shape["dp"])) - 1
    seq = P(("dp", "fsdp"), None, None)
    row, vec = P("fsdp", None), P("fsdp")
    in_specs = (seq, P(("dp", "fsdp"), None), vec, vec, row, row, vec, row, vec, row, vec, seq)
    out_specs = (seq, seq, vec, vec, row, row, vec, row, vec, row, vec)
    return jax.shard_map(
        functools.partial(on_device, nbits), mesh=mesh,
        in_specs=in_specs, out_specs=out_specs, check_vma=False,
    )
```

```python
import functools
import math

import jax
import jax.numpy as jnp
import numpy as np
from jax import lax
from jax.experimental import pallas as pl
from jax.experimental.pallas import tpu as pltpu
from jax.sharding import PartitionSpec as P

HD = 64
BLOCK = 16
NORM_FLOOR = 1e-05
TANH_SCALE = 0.7978845608028654
CUBIC = 0.044715
BF = jnp.bfloat16
F32 = jnp.float32
MESH = pl.DeviceIdType.MESH
LOGIT_SCALE = 0.125 * math.log2(math.e)
N_SEND, N_RECV, N_LOCAL = 97, 190, 38
NN = (((1,), (0,)), ((), ()))
NT = (((1,), (1,)), ((), ()))
TN = (((0,), (0,)), ((), ()))


ROUTES = {
    "d0": "0yZ",
    "d1": "y0Z",
    "d2": "y0Z",
    "u0": "0yZ",
    "u1": "y0Z",
    "u2": "y012",
    "u3": "y012",
    "u4": "y102",
    "u5": "y012",
    "q0": "0y12",
    "q1": "0yZ",
    "q2": "y0Z",
    "o": "y102",
}
SCHEDULE = {
    ("u", 0): (
        ("d1", 0),
    ),
    ("u", 1): (
        ("d0", 0),
    ),
    ("dn", 0): (
        ("d2", 0),
        ("u0", 0),
    ),
    ("dn", 1): (
        ("u1", 0),
        ("d1", 1),
    ),
    ("dm", 0): (
        ("u2", 0),
        ("d2", 1),
    ),
    ("att", 0): (
        ("u1", 1),
        ("d1", 2),
        ("u3", 0),
    ),
    ("att", 1): (
        ("u2", 1),
        ("d2", 2),
        ("u4", 0),
    ),
    ("q", 0): (
        ("u3", 1),
        ("u1", 2),
    ),
    ("att", 2): (
        ("u2", 2),
        ("u5", 0),
    ),
    ("att", 3): (
        ("d1", 3),
        ("d0", 1),
    ),
    ("q", 1): (
        ("u4", 1),
        ("d2", 3),
        ("q0", 0),
        ("u3", 2),
        ("u0", 1),
    ),
    ("att", 4): (
        ("u1", 3),
        ("u5", 1),
        ("u2", 3),
    ),
    ("att", 5): (
        ("d1", 4),
        ("o", 0),
        ("d0", 2),
        ("u3", 3),
        ("u5", 2),
    ),
    ("q", 2): (
        ("q0", 1),
        ("u0", 2),
    ),
    ("da", 0): (
        ("u2", 4),
        ("q1", 0),
        ("u4", 2),
        ("o", 1),
    ),
    ("da", 1): (
        ("d0", 3),
        ("u3", 4),
        ("d2", 4),
        ("u5", 3),
    ),
    ("bo", 0): (
        ("q2", 0),
        ("q0", 2),
        ("u1", 4),
        ("u0", 3),
        ("o", 2),
        ("q1", 1),
        ("u2", 5),
    ),
    ("bo", 1): (
        ("s", 0),
        ("u4", 3),
        ("u3", 5),
        ("u5", 4),
        ("q0", 3),
        ("d0", 4),
    ),
    "tail": (
        ("o", 3),
        ("q2", 1),
        ("u5", 5),
        ("q1", 2),
        ("u0", 4),
        ("u4", 4),
        ("q0", 4),
        ("u2", 6),
        ("s", 1),
        ("o", 4),
        ("u3", 6),
        ("u5", 6),
        ("q2", 2),
        ("q0", 5),
        ("u4", 5),
        ("o", 5),
        ("q1", 3),
        ("s", 2),
        ("q0", 6),
        ("q2", 3),
        ("u4", 6),
        ("q1", 4),
        ("o", 6),
        ("s", 3),
        ("q2", 4),
        ("s", 4),
    ),
}


def dot(a, b, dims=NN):
    return lax.dot_general(a, b, dims, preferred_element_type=F32)


def mo(x, n):
    return pl.multiple_of(x, n)


def normalize(x):
    d = x - jnp.mean(x, axis=-1, keepdims=True)
    inv = lax.rsqrt(jnp.mean(d * d, axis=-1, keepdims=True) + NORM_FLOOR)
    return d * inv, inv


def normalize_backward(g, xhat, inv, gain):
    e = g * gain
    return inv * (
        e
        - jnp.mean(e, axis=-1, keepdims=True)
        - xhat * jnp.mean(e * xhat, axis=-1, keepdims=True)
    )


def layer_kernel(
    nbits,
    clean_h, noise, v_mask, v_ga, v_gm, v_bd, v_bu, cos_r, sin_r, wq_h, wo_h, wu_h, wd_h, og_h,
    out_h, cg_h, fin, o1_h, od_h,
    small_in, small, prow, mcol, mbf, mbb, mbe,
    stream, normed, wq, wo, wu, wd, og,
    qkv, qaug, mixed, aa, nm, act, dpre, xs, xr, daf, db, dm, dks, dsn,
    gd, g1, r0d, r01, r1d, r11, r2d, r21, r3d, r31, red, re1,
    sbuf, srec, ss, rs, ls,
):
    L = 384
    D = 768
    T = 2 * L
    NT3 = L // 128
    d = lax.axis_index("dp")
    f = lax.axis_index("fsdp")
    c = lax.rem(d, 2)
    bits = [lax.rem(lax.div(d, 2 ** (b + 1)), 2) for b in range(nbits)]
    sib = (d + 1 - 2 * c, f)
    ypeer = (d, 1 - f)
    peers = [(d + (1 - 2 * bits[b]) * 2 ** (b + 1), f) for b in range(nbits)]
    u = 2 * bits[1] + bits[0]
    send_count, recv_count, local_count = [0], [0], [0]
    ends = []

    def take_send(n):
        k = send_count[0]
        send_count[0] += n
        return k

    def take_recv(n=1):
        k = recv_count[0]
        recv_count[0] += n
        return k

    def rc(k, src, dst, dev):
        return pltpu.make_async_remote_copy(
            src_ref=src, dst_ref=dst, send_sem=ss.at[k[0]], recv_sem=rs.at[k[1]],
            device_id=dev, device_id_type=MESH,
        )

    def remote(make, n=1):
        k = (take_send(n), take_recv(n))
        fam = lambda i=0: make((k[0] + i, k[1] + i), i)
        ends.append((fam, n))
        return fam

    def sent(fam):
        for at, (other_fam, n) in enumerate(ends):
            if other_fam is fam:
                for i in range(n):
                    fam(i).wait_send()
                ends.pop(at)
                return

    def local(src, dst):
        k = local_count[0]
        local_count[0] += 1
        return lambda: pltpu.make_async_copy(src, dst, ls.at[k])

    bar = pltpu.get_barrier_semaphore()
    for dev in [sib, ypeer] + peers:
        pl.semaphore_signal(bar, inc=1, device_id=dev, device_id_type=MESH)

    l_clean = [
        local(clean_h.at[0, pl.ds(128 * i, 128)], stream.at[pl.ds(256 * i + 128, 128)])
        for i in range(NT3)
    ]
    mine = mo(f * L, 128)
    other = mo((1 - f) * L, 128)
    l_wq = [
        local(
            wq_h.at[:, pl.ds(mo(j * D + c * L, 128), L)],
            wq.at[pl.ds(mine, L), pl.ds(j * L, L)],
        )
        for j in range(3)
    ]
    l_wo = local(wo_h, wo.at[pl.ds(mine, L)])
    l_wu = [
        local(
            wu_h.at[:, pl.ds(mo(h * 1536 + c * D, 128), D)],
            wu.at[pl.ds(mine, L), pl.ds(h * D, D)],
        )
        for h in range(2)
    ]
    l_wd = local(wd_h.at[pl.ds(mo(c * D, 128), D)], wd.at[pl.ds(mo(f * D, 128), D)])
    l_og = [
        local(
            og_h.at[0, pl.ds((r % 2) * L + 128 * (r // 2), 128)],
            og.at[pl.ds(128 * r, 128)],
        )
        for r in range(2 * NT3)
    ]
    for cp in l_clean + l_wq:
        cp().start()
    for r, v in enumerate((v_mask, v_ga, v_gm, v_bd)):
        small_in[r : r + 1, :] = v[...].astype(F32).reshape(1, L)
    for r in range(4):
        small_in[4 + r : 5 + r, :] = v_bu[pl.ds(L * r, L)].astype(F32).reshape(1, L)
    small[pl.ds(f, 1)] = small_in[...][None]

    def y_wq(unit):
        rows = mo(96 * unit, 16)
        return remote(
            lambda k, j: rc(
                k,
                wq_h.at[pl.ds(rows, 96), pl.ds(mo(j * D + c * L, 128), L)],
                wq.at[pl.ds(mo(f * L + rows, 16), 96), pl.ds(j * L, L)],
                ypeer,
            ),
            3,
        )

    yw_q = y_wq(u)
    yw_q2 = y_wq(3 - u)
    y_small = remote(lambda k, i: rc(k, small_in, small.at[f], ypeer))

    def spread(buf, base, unit_rows, unit, dev):
        rows = mo(base + unit_rows * unit, 16)
        return remote(
            lambda k, i: rc(
                k, buf.at[pl.ds(rows, unit_rows)], buf.at[pl.ds(rows, unit_rows)], dev
            )
        )


    def spread_q(dev):
        rows = mo(other + 96 * u, 16)
        return remote(
            lambda k, j: rc(
                k, wq.at[pl.ds(rows, 96), pl.ds(j * L, L)],
                wq.at[pl.ds(rows, 96), pl.ds(j * L, L)], dev,
            ),
            3,
        )

    xw_q = spread_q(peers[0])
    zw_q = spread_q(peers[1])
    yw_u = remote(
        lambda k, h: rc(
            k,
            wu_h.at[pl.ds(mo(96 * u, 16), 96), pl.ds(mo(h * 1536 + c * D, 128), D)],
            wu.at[pl.ds(mo(f * L + 96 * u, 16), 96), pl.ds(h * D, D)],
            ypeer,
        ),
        2,
    )
    ux, uz = 2 * bits[1] + 1 - bits[0], 2 * (1 - bits[1]) + bits[0]
    xw_u = spread(wu, other, 96, u, peers[0])
    zw_u = spread(wu, other, 96, u, peers[1])
    xw_u2 = spread(wu, other, 48, 2 * uz, peers[0])
    zw_u2 = spread(wu, other, 48, 2 * ux + 1, peers[1])
    odown = mo((1 - f) * D, 128)
    yw_d = remote(
        lambda k, i: rc(
            k,
            wd_h.at[pl.ds(mo(c * D + 192 * u, 16), 192)],
            wd.at[pl.ds(mo(f * D + 192 * u, 16), 192)],
            ypeer,
        )
    )
    xw_d = spread(wd, odown, 192, u, peers[0])
    zw_d = spread(wd, odown, 192, u, peers[1])
    xw_d2 = spread(wd, odown, 96, 2 * uz, peers[0])
    zw_d2 = spread(wd, odown, 96, 2 * ux + 1, peers[1])
    yw_o = remote(
        lambda k, i: rc(
            k,
            wo_h.at[pl.ds(mo(192 * c + 96 * bits[0], 16), 96)],
            wo.at[pl.ds(mo(f * L + 192 * c + 96 * bits[0], 16), 96)],
            ypeer,
        )
    )
    xw_o = spread(wo, mo(other + 192 * c, 16), 96, bits[0], peers[0])
    sw_o = spread(wo, other, 192, c, sib)

    s_norm = remote(
        lambda k, i: rc(
            k, normed.at[pl.ds(mo(256 * i, 16), 256)],
            normed.at[pl.ds(mo(T + 256 * i, 16), 256)], sib,
        ),
        NT3,
    )
    s_og = remote(lambda k, i: rc(k, og.at[pl.ds(0, T)], og.at[pl.ds(T, T)], sib))

    def mixed_copy(k, i):
        s = 1 - i // 3 if isinstance(i, int) else 1 - lax.div(i, 3)
        p = i % 3 if isinstance(i, int) else lax.rem(i, 3)
        lanes = pl.ds(mo(c * L + 128 * p, 128), 128)
        return rc(
            k, mixed.at[pl.ds(mo(s * T, 16), T), lanes],
            mixed.at[pl.ds(mo((1 - s) * T, 16), T), lanes], sib,
        )

    s_mix = remote(mixed_copy, 6)

    def rows_copy(buf, src0, dst, dst0):
        return remote(
            lambda k, i: rc(
                k, buf.at[pl.ds(mo(src0 + 256 * i, 16), 256)],
                dst.at[pl.ds(mo(dst0 + 256 * i, 16), 256)], sib,
            ),
            NT3,
        )

    s_nm = rows_copy(nm, 0, nm, T)
    s_dn = rows_copy(xs, 0, xr, 0)
    s_db = rows_copy(db, 0, db, T)
    s_bo = rows_copy(xs, 0, xr, 0)
    right = pl.ds(D, D)
    s_da = remote(
        lambda k, i: rc(
            k, dpre.at[pl.ds(mo(256 * i, 16), 256), right],
            dpre.at[pl.ds(mo(T + 256 * i, 16), 256), right], sib,
        ),
        NT3,
    )

    class Chunk:
        pass

    chunks = {}

    def make_chunk(name, g, gbase, nr, l0, nl, recv, rbase, oref, orow, blk):
        ch = Chunk()
        lanes = pl.ds(l0, nl)
        route = ROUTES[name]

        def greg(h, off, n):
            return g.at[pl.ds(mo(gbase(h) + off, 16), n), lanes]

        def rreg(stage, at, n):
            return recv[stage].at[pl.ds((rbase >> stage) + at, n), lanes]

        def oreg(core, off, n):
            return oref.at[core, pl.ds(mo(orow + off, 16), n), lanes]

        def send(copies, before=()):
            for cp in before:
                cp().wait_send()
            for cp in copies:
                cp().start()

        k_send = take_send(3)

        def copy(i, src, dst, dev):
            k = take_recv()
            return lambda: pltpu.make_async_remote_copy(
                src_ref=src(), dst_ref=dst(), send_sem=ss.at[k_send + i], recv_sem=rs.at[k],
                device_id=dev, device_id_type=MESH,
            )

        def add(h, off, n, parts):
            gr = greg(h, off, n)
            step = min(blk, n)

            def body(i, carry):
                sl = pl.ds(mo(i * step, 16), step)
                x = gr[sl, :].astype(F32)
                for stage, at in parts:
                    x = x + rreg(stage, at, n)[sl, :].astype(F32)
                gr[sl, :] = x.astype(BF)
                return carry

            lax.fori_loop(0, n // step, body, 0)

        sends, adds, gathers = [], [], []
        off, n, both, stage = 0, nr, True, 0
        for step in route:
            if step == "y":
                sends.append([copy(
                    0, lambda off=off, n=n: greg(1 - f, off, n),
                    lambda stage=stage, n=n: rreg(stage, 0, n), ypeer,
                )])
                adds.append([(f, off, n, [(stage, 0)])])
                both = False
                stage += 1
            elif step == "Z":
                m4 = n // 4
                out, parts, back = [], [], []
                where = [(stage, 0), (stage, m4), (stage + 1, 0)]
                mine_off = off + (2 * bits[1] + bits[2]) * m4
                for i, (x1, x2) in enumerate(((0, 1), (1, 0), (1, 1))):
                    b1 = 1 - bits[1] if x1 else bits[1]
                    b2 = 1 - bits[2] if x2 else bits[2]
                    dev = (d + (b1 - bits[1]) * 4 + (b2 - bits[2]) * 8, f)
                    to = off + (2 * b1 + b2) * m4
                    st, at = where[i]
                    out.append(copy(
                        i, lambda to=to, m4=m4: greg(f, to, m4),
                        lambda st=st, at=at, m4=m4: rreg(st, at, m4), dev,
                    ))
                    back.append(dev)
                    parts.append((st, at))
                sends.append(out)
                adds.append([(f, mine_off, m4, parts)])
                gathers.append((mine_off, m4, back))
                off, n, stage = mine_off, m4, stage + 2
            else:
                j = int(step)
                m2 = n // 2
                give, keep = off + (1 - bits[j]) * m2, off + bits[j] * m2
                owners = [0, 1] if both else [f]
                sends.append([
                    copy(
                        i, lambda h=h, give=give, m2=m2: greg(h, give, m2),
                        lambda stage=stage, i=i, m2=m2: rreg(stage, i * m2, m2), peers[j],
                    )
                    for i, h in enumerate(owners)
                ])
                adds.append([(h, keep, m2, [(stage, i * m2)]) for i, h in enumerate(owners)])
                gathers.append((keep, m2, [peers[j]]))
                off, n, stage = keep, m2, stage + 1
        extra = [
            copy(
                0, lambda off=off, n=n: greg(f, off, n),
                lambda j=j, n=n: recv[4].at[j - 3, pl.ds((rbase >> 3), n), lanes], peers[j],
            )
            for j in range(3, nbits)
        ]
        own = local(greg(f, off, n), oreg(c, off, n))
        back = []
        for depth, (at, m, devs) in enumerate(reversed(gathers)):
            back.append([
                copy(
                    i,
                    (lambda at=at, m=m: greg(f, at, m)) if depth == 0
                    else (lambda at=at, m=m: oreg(c, at, m)),
                    lambda at=at, m=m: oreg(c, at, m), dev,
                )
                for i, dev in enumerate(devs)
            ])
        back.append([copy(0, lambda: oreg(c, 0, nr), lambda: oreg(c, 0, nr), sib)])

        def reduce_event(i):
            for cp in sends[i]:
                cp().wait_recv()
            for h, at, m, parts in adds[i]:
                add(h, at, m, parts)
            if i + 1 < len(sends):
                send(sends[i + 1], sends[i])
                return
            send((), sends[i])
            for m, cp in enumerate(extra):
                send([cp])
                send((), [cp])
                cp().wait_recv()
                gr = greg(f, off, n)
                gr[...] = (
                    gr[...].astype(F32)
                    + recv[4][m, pl.ds((rbase >> 3), n), lanes].astype(F32)
                ).astype(BF)
            own().start()
            send(back[0])

        def gather_event(i):
            for cp in back[i]:
                cp().wait_recv()
            if i == 0:
                own().wait()
            if i + 1 < len(back):
                send(back[i + 1], back[i])
            else:
                send((), back[i])

        ch.start = lambda: send(sends[0])
        ch.events = [functools.partial(reduce_event, i) for i in range(len(sends))] + [
            functools.partial(gather_event, i) for i in range(len(back))
        ]
        chunks[name] = ch

    recv_d = (r0d, r1d, r2d, r3d, red)
    recv_1 = (r01, r11, r21, r31, re1)
    for k in range(3):
        make_chunk(
            f"d{k}", gd, lambda h, k=k: h * D + 256 * k, 256, 0, D, recv_d, 256 * k,
            od_h, 256 * k, 32,
        )
    for t in range(6):
        make_chunk(f"u{t}", g1, lambda h: h * L, L, 256 * t, 256, recv_1, 0, o1_h, 0, 48)
    for p in range(3):
        make_chunk(f"q{p}", g1, lambda h: h * L, L, 1536 + L * p, L, recv_1, 0, o1_h, 0, 48)
    make_chunk("o", g1, lambda h: h * L, L, 1536 + 3 * L, L, recv_1, 0, o1_h, 0, 48)

    def handle(key):
        for name, stage in SCHEDULE.get(key, ()):
            chunks[name].events[stage]()

    def handle_at(idx, keys):
        for i, key in keys.items():
            if SCHEDULE.get(key):
                pl.when(idx == i)(lambda key=key: handle(key))

    pl.semaphore_wait(bar, 2 + nbits)
    y_small().start()
    for j in range(3):
        yw_q(j).start()
    for j in range(3):
        yw_q2(j).start()
    for h in range(2):
        yw_u(h).start()
    yw_o().start()
    yw_d().start()
    for cp in l_og + l_wu + [l_wo, l_wd]:
        cp().start()

    lane = lax.broadcasted_iota(jnp.int32, (1, 128), 1)
    low_half = lane < HD
    rot_low = lax.rem(lane, HD) < HD // 2
    bm = [jnp.where(low_half, 1.0, 0.0).astype(BF), jnp.where(low_half, 0.0, 1.0).astype(BF)]
    selm = [low_half, lane >= HD]
    spare = [HD, 0]
    ir = lax.div(lax.broadcasted_iota(jnp.int32, (128, 128), 0), BLOCK)
    ic = lax.div(lax.broadcasted_iota(jnp.int32, (128, 128), 1), BLOCK)
    neg = -1e30
    mbf[0:128, :] = jnp.where(ic < ir, 0.0, neg)
    mbf[128:256, :] = jnp.where(ic <= ir, 0.0, neg)
    mbb[:, 0:128] = jnp.where(ir < ic, 0.0, neg)
    mbb[:, 128:256] = jnp.where(ir <= ic, 0.0, neg)
    mbe[...] = jnp.where(ir == ic, 0.0, neg)
    nf = noise[...].astype(F32)
    for i in range(NT3):
        mcol[128 * i : 128 * i + 128, :] = jnp.broadcast_to(
            nf[:, 128 * i : 128 * i + 128], (128, 128)
        ).T
    sbuf[0] = jnp.zeros((8, D), F32)

    y_small().wait_recv()
    prow[:, 0:L] = small[0]
    prow[:, L:D] = small[1]
    mvec = prow[0:1, :]
    gain_a = prow[1:2, :]
    gain_m = prow[2:3, :]
    bias_d = prow[3:4, :]

    def wide(m):
        return jnp.concatenate([m] * (D // 128), axis=1)

    for i in range(NT3):
        l_clean[i]().wait()

    def attn_norm(i, carry):
        n0 = mo(256 * i, 128)
        x = stream[pl.ds(n0 + 128, 128), :].astype(F32)
        m = wide(mcol[pl.ds(mo(128 * i, 128), 128), :])
        y = jnp.where(m > 0.5, mvec, x)
        stream[pl.ds(n0, 128), :] = y.astype(BF)
        normed[pl.ds(n0, 128), :] = (normalize(y)[0] * gain_a).astype(BF)
        normed[pl.ds(n0 + 128, 128), :] = (normalize(x)[0] * gain_a).astype(BF)
        s_norm(i).start()
        return carry

    lax.fori_loop(0, NT3, attn_norm, 0)

    for j in range(3):
        yw_q(j).wait_recv()
        xw_q(j).start()
        zw_q(j).start()
    for i in range(NT3):
        s_norm(i).wait_recv()
    for cp in l_og:
        cp().wait()
    s_og().start()
    for j in range(3):
        l_wq[j]().wait()
        yw_q2(j).wait_recv()
        xw_q(j).wait_recv()
        zw_q(j).wait_recv()

    def turn(x, cos, sin):
        return x * cos + jnp.where(rot_low, pltpu.roll(x, 96, 1), pltpu.roll(x, 32, 1)) * sin

    def rows2(tab, i):
        t = tab[pl.ds(mo(128 * i, 128), 128), :]
        return jnp.concatenate([t, t], axis=0)

    def qkv_rows(r, carry):
        rows = pl.ds(mo(256 * r, 128), 256)
        joined = dot(normed[rows, :], wq[...])
        i = lax.rem(r, NT3)
        cos, sin = rows2(cos_r, i), rows2(sin_r, i)
        for p in range(6):
            x = joined[:, 128 * p : 128 * p + 128]
            qkv[rows, 128 * p : 128 * p + 128] = turn(x, cos, sin).astype(BF)
        qkv[rows, 2 * L : 3 * L] = joined[:, 2 * L : 3 * L].astype(BF)
        return carry

    lax.fori_loop(0, 2 * NT3, qkv_rows, 0)
    for h in range(2):
        l_wu[h]().wait()
        yw_u(h).wait_recv()
    xw_u().start()
    zw_u().start()

    def run_at(idx, table):
        for k, fns in table.items():
            def go(fns=fns):
                for fn in fns:
                    fn()
            pl.when(idx == k)(go)

    def w_o_1():
        l_wo().wait()
        yw_o().wait_recv()
        xw_o().start()

    def w_u_2():
        xw_u().wait_recv()
        zw_u().wait_recv()
        xw_u2().start()
        zw_u2().start()

    def w_o_2():
        xw_o().wait_recv()
        sw_o().start()

    def w_d_1():
        l_wd().wait()
        yw_d().wait_recv()
        xw_d().start()
        zw_d().start()

    def w_d_2():
        xw_d().wait_recv()
        zw_d().wait_recv()
        xw_d2().start()
        zw_d2().start()

    fwd_events = {2: [w_o_1], 3: [w_u_2, w_o_2], 4: [w_d_1]}

    def attn_fwd(n, carry):
        s, p = 1 - lax.div(n, 3), lax.rem(n, 3)
        r0 = s * T
        lq = pl.ds(mo(128 * p, 128), 128)
        lk = pl.ds(mo(L + 128 * p, 128), 128)
        lv = pl.ds(mo(2 * L + 128 * p, 128), 128)

        def rws(a, m):
            return pl.ds(mo(r0 + a, 128), m)

        for i in range(NT3):
            res = []
            for a in range(2):
                q = qkv[rws(256 * i, 256), lq] * bm[a]
                kc = jnp.concatenate(
                    [qkv[rws(256 * j + 128, 128), lk] for j in range(i + 1)], axis=0
                )
                vc = jnp.concatenate(
                    [qkv[rws(256 * j + 128, 128), lv] for j in range(i + 1)], axis=0
                ) * bm[a] + bm[1 - a]
                vn = qkv[rws(256 * i, 128), lv] * bm[a] + bm[1 - a]
                s1 = dot(q, kc, NT) * LOGIT_SCALE
                sn = dot(q[:128], qkv[rws(256 * i, 128), lk], NT) * LOGIT_SCALE + mbe[...]
                last = s1[:, 128 * i :] + mbf[...]
                s1 = last if i == 0 else jnp.concatenate([s1[:, : 128 * i], last], axis=1)
                m1 = jnp.max(s1, axis=1, keepdims=True)
                mn = jnp.maximum(m1[:128], jnp.max(sn, axis=1, keepdims=True))
                m = jnp.concatenate([mn, m1[128:]], axis=0)
                p1 = jnp.exp2(s1 - m).astype(BF)
                pn = jnp.exp2(sn - mn).astype(BF)
                o = dot(p1, vc)
                o = jnp.concatenate([o[:128] + dot(pn, vn), o[128:]], axis=0)
                val = (m + jnp.log2(o)) * (-1.0 / LOGIT_SCALE)
                hi = val.astype(BF).astype(F32)
                mid = (val - hi).astype(BF).astype(F32)
                lo = val - hi - mid
                extra = jnp.where(
                    lane == spare[a], hi,
                    jnp.where(lane == spare[a] + 1, mid, jnp.where(lane == spare[a] + 2, lo, 0.0)),
                )
                qaug[rws(256 * i, 256), pl.ds(mo(256 * p + 128 * a, 128), 128)] = jnp.where(
                    selm[a], q.astype(F32), extra
                ).astype(BF)
                res.append(o)
            data = jnp.where(low_half, res[0], res[1])
            sums = pltpu.roll(jnp.where(low_half, res[1], res[0]), HD, 1)
            mixed[rws(256 * i, 256), pl.ds(mo(c * L + 128 * p, 128), 128)] = (
                data * (1.0 / sums)
            ).astype(BF)
        s_mix(n).start()
        run_at(n, fwd_events)
        return carry

    lax.fori_loop(0, 6, attn_fwd, 0)

    sw_o().wait_recv()
    for n in range(3):
        s_mix(n).wait_recv()

    def out_proj(i, carry):
        rows = pl.ds(mo(256 * i, 128), 256)
        x = stream[rows, :].astype(F32) + dot(mixed[rows, :], wo[...])
        aa[rows, :] = x
        nm[rows, :] = (normalize(x)[0] * gain_m).astype(BF)
        s_nm(i).start()
        return carry

    lax.fori_loop(0, NT3, out_proj, 0)
    xw_u2().wait_recv()
    zw_u2().wait_recv()

    for n in range(2):
        h = 1 - f if n == 0 else f
        lanes = pl.ds(mo(h * D, 128), D)
        bu = jnp.concatenate(
            [small[h, pl.ds(4 + 2 * c + r, 1), :] for r in range(2)], axis=1
        )

        def rows_a(r, carry, n=n, lanes=lanes, bu=bu):
            if n == 0:
                @pl.when(r == 2)
                def _():
                    for i in range(NT3):
                        s_nm(i).wait_recv()

            rows = pl.ds(mo(L * r, 128), L)
            pre = dot(nm[rows, :], wu[:, lanes]) + bu
            sq = pre * pre
            half = 0.5 + 0.5 * jnp.tanh(pre * (TANH_SCALE + TANH_SCALE * CUBIC * sq))
            a = pre * half
            act[rows, lanes] = a.astype(BF)
            slope = half + 2.0 * a * (1.0 - half) * (
                TANH_SCALE + 3.0 * CUBIC * TANH_SCALE * sq
            )
            dpre[rows, lanes] = slope.astype(BF)
            return carry

        lax.fori_loop(0, 4, rows_a, 0)
        if n == 0:
            s_og().wait_recv()
            w_d_2()

        def down_grad(k, carry, n=n, h=h):
            at = mo(h * D + 256 * k, 128)
            gd[pl.ds(at, 256), :] = dot(act[:, pl.ds(at, 256)], og[...], TN).astype(BF)
            for i in range(3):
                early = ROUTES[f"d{i}"][0] == "y"
                if early == (n == 0):
                    pl.when(k == i)(chunks[f"d{i}"].start)
            handle_at(k, {i: ("a", n, i) for i in range(3)})
            return carry

        handle(("a", n))
        lax.fori_loop(0, 3, down_grad, 0)
    xw_d2().wait_recv()
    zw_d2().wait_recv()

    for n in range(2):
        lanes = pl.ds(n * D, D)

        def rows_b(r, tot, lanes=lanes):
            rows = pl.ds(mo(L * r, 128), L)
            g = dot(og[rows, :], wd[lanes, :], NT) * dpre[rows, lanes].astype(F32)
            dpre[rows, lanes] = g.astype(BF)
            return tot + jnp.sum(g, axis=0, keepdims=True)

        sbuf[0, 4 + n : 5 + n, :] = lax.fori_loop(0, 4, rows_b, jnp.zeros((1, D), F32))
        handle(("b", n))
        g1[:, n * D : n * D + D] = dot(nm[...], dpre[:, n * D : n * D + D], TN).astype(BF)
        for t in range(3 * n, 3 * n + 3):
            chunks[f"u{t}"].start()
        handle(("u", n))

    def dn_other(i, carry):
        x = dot(dpre[pl.ds(mo(T + 256 * i, 128), 256), :], wu[...], NT)
        xs[pl.ds(mo(256 * i, 128), 256), :] = x.astype(BF)
        s_dn(i).start()
        return carry

    lax.fori_loop(0, NT3, dn_other, 0)
    handle(("dn", 0))

    def dn_own(i, sums):
        rows = pl.ds(mo(256 * i, 128), 256)
        g = dot(dpre[rows, :], wu[...], NT)
        s_dn(i).wait_recv()
        g = g + xr[rows, :].astype(F32)
        xhat, inv = normalize(aa[rows, :])
        ograd = og[rows, :].astype(F32)
        after = ograd + normalize_backward(g, xhat, inv, gain_m)
        daf[rows, :] = after
        db[rows, :] = after.astype(BF)
        s_db(i).start()
        return (
            sums[0] + jnp.sum(g * xhat, axis=0, keepdims=True),
            sums[1] + jnp.sum(ograd, axis=0, keepdims=True),
        )

    zrow = jnp.zeros((1, D), F32)
    g_gain_m, g_bias_d = lax.fori_loop(0, NT3, dn_own, (zrow, zrow))
    sbuf[0, 2:3, :] = g_gain_m
    sbuf[0, 3:4, :] = g_bias_d
    handle(("dn", 1))

    wo_rows = pl.ds(mo(c * L, 128), L)
    dm[0:T, :] = dot(db[0:T, :], wo[wo_rows, :], NT).astype(BF)
    for i in range(NT3):
        s_db(i).wait_recv()
    dm[T : 2 * T, :] = dot(db[T : 2 * T, :], wo[wo_rows, :], NT).astype(BF)
    for n in range(3, 6):
        s_mix(n).wait_recv()
    g1[:, 1536 + 3 * L : 1536 + 4 * L] = dot(mixed[...], db[:, wo_rows], TN).astype(BF)
    chunks["o"].start()
    handle(("dm", 0))

    one_q = [
        jnp.where((lane >= s) & (lane < s + 3), 1.0, 0.0).astype(BF) for s in spare
    ]
    one_d = [
        jnp.where((lane >= s) & (lane < s + 2), 1.0, 0.0).astype(BF) for s in spare
    ]

    def attn_bwd(n, carry):
        s, p = lax.rem(n, 2), lax.div(n, 2)
        r0 = s * T
        lq = pl.ds(mo(128 * p, 128), 128)
        lk = pl.ds(mo(L + 128 * p, 128), 128)
        lv = pl.ds(mo(2 * L + 128 * p, 128), 128)

        def rws(a, m):
            return pl.ds(mo(r0 + a, 128), m)

        dog = dm[rws(0, T), lq]
        prod = dog.astype(F32) * mixed[
            rws(0, T), pl.ds(mo(c * L + 128 * p, 128), 128)
        ].astype(F32)
        doa = []
        for a in range(2):
            val = -jnp.sum(jnp.where(selm[a], prod, 0.0), axis=1, keepdims=True)
            hi = val.astype(BF).astype(F32)
            mid = val - hi
            extra = jnp.where(lane == spare[a], hi, jnp.where(lane == spare[a] + 1, mid, 0.0))
            doa.append(jnp.where(selm[a], dog.astype(F32), extra).astype(BF))
        for kt in range(NT3):
            q0 = 256 * kt
            nq = T - q0
            pts, dss, ptn, dsnn = [], [], [], []
            for a in range(2):
                qa = qaug[rws(q0, nq), pl.ds(mo(256 * p + 128 * a, 128), 128)]
                da = doa[a][q0:]
                kc = qkv[rws(q0 + 128, 128), lk] * bm[a] + one_q[a]
                kn = qkv[rws(q0, 128), lk] * bm[a] + one_q[a]
                vc = qkv[rws(q0 + 128, 128), lv] * bm[a] + one_d[a]
                vn = qkv[rws(q0, 128), lv] * bm[a] + one_d[a]
                st = dot(kc, qa, NT) * LOGIT_SCALE
                first = st[:, :256] + mbb[...]
                st = first if nq == 256 else jnp.concatenate([first, st[:, 256:]], axis=1)
                pt = jnp.exp2(st)
                ds = pt * dot(vc, da, NT)
                dpre[pl.ds(512 * a + 128 * kt, 128), pl.ds(q0, nq)] = ds.astype(BF)
                pts.append(pt.astype(BF))
                dss.append(ds.astype(BF))
                pn = jnp.exp2(dot(kn, qa[:128], NT) * LOGIT_SCALE + mbe[...])
                dn = pn * dot(vn, da[:128], NT)
                dsn[a, kt] = dn.astype(BF)
                ptn.append(pn.astype(BF))
                dsnn.append(dn.astype(BF))
            dom = [dm[rws(q0, nq), lq] * bm[a] for a in range(2)]
            qm = [qkv[rws(q0, nq), lq] * bm[a] for a in range(2)]
            domc, qmc = jnp.concatenate(dom, axis=0), jnp.concatenate(qm, axis=0)
            domn = jnp.concatenate([x[:128] for x in dom], axis=0)
            qmn = jnp.concatenate([x[:128] for x in qm], axis=0)
            dks[pl.ds(q0 + 128, 128), :] = dot(jnp.concatenate(dss, axis=1), qmc)
            dks[pl.ds(q0, 128), :] = dot(jnp.concatenate(dsnn, axis=1), qmn)
            qkv[rws(q0 + 128, 128), lv] = dot(jnp.concatenate(pts, axis=1), domc).astype(BF)
            qkv[rws(q0, 128), lv] = dot(jnp.concatenate(ptn, axis=1), domn).astype(BF)
        for i in range(NT3):
            dq = None
            for a in range(2):
                kc = jnp.concatenate(
                    [qkv[rws(256 * j + 128, 128), lk] for j in range(i + 1)], axis=0
                ) * bm[a]
                part = dot(
                    dpre[pl.ds(512 * a, 128 * (i + 1)), pl.ds(256 * i, 256)], kc, TN
                )
                pn = dot(dsn[a, i], qkv[rws(256 * i, 128), lk] * bm[a], TN)
                part = jnp.concatenate([part[:128] + pn, part[128:]], axis=0)
                dq = part if dq is None else dq + part
            cos, sin = rows2(cos_r, i), rows2(sin_r, i)
            qkv[rws(256 * i, 256), lq] = (turn(dq, cos, -sin) * 0.125).astype(BF)
        for i in range(NT3):
            cos, sin = rows2(cos_r, i), rows2(sin_r, i)
            dk = dks[pl.ds(256 * i, 256), :]
            qkv[rws(256 * i, 256), lk] = (turn(dk, cos, -sin) * 0.125).astype(BF)
        handle_at(n, {i: ("att", i) for i in range(6)})

        @pl.when(s == 1)
        def _():
            dj = jnp.concatenate([qkv[:, lq], qkv[:, lk], qkv[:, lv]], axis=1)
            g1[:, pl.ds(mo(1536 + L * p, 128), L)] = dot(normed[...], dj, TN).astype(BF)

        for i in range(3):
            pl.when(n == 2 * i + 1)(chunks[f"q{i}"].start)
        handle_at(n, {2 * i + 1: ("q", i) for i in range(3)})
        return carry

    lax.fori_loop(0, 6, attn_bwd, 0)

    def da_other(i, carry):
        x = dot(qkv[pl.ds(mo(T + 256 * i, 128), 256), :], wq[...], NT)
        dpre[pl.ds(mo(256 * i, 128), 256), right] = x.astype(BF)
        s_da(i).start()
        return carry

    lax.fori_loop(0, NT3, da_other, 0)
    handle(("da", 0))
    cg_out = [
        local(daf.at[pl.ds(256 * i, 128)], cg_h.at[0, pl.ds(128 * i, 128)]) for i in range(NT3)
    ]

    def da_own(i, sums):
        rows = pl.ds(mo(256 * i, 128), 256)
        g = dot(qkv[rows, :], wq[...], NT)
        s_da(i).wait_recv()
        g = g + dpre[pl.ds(mo(T + 256 * i, 128), 256), right].astype(F32)
        xhat, inv = normalize(stream[rows, :].astype(F32))
        ds = daf[rows, :] + normalize_backward(g, xhat, inv, gain_a)
        m = wide(mcol[pl.ds(mo(128 * i, 128), 128), :]) > 0.5
        daf[pl.ds(mo(256 * i, 128), 128), :] = ds[128:] + jnp.where(m, 0.0, ds[:128])
        return (
            sums[0] + jnp.sum(jnp.where(m, ds[:128], 0.0), axis=0, keepdims=True),
            sums[1] + jnp.sum(g * xhat, axis=0, keepdims=True),
        )

    g_mask, g_gain_a = lax.fori_loop(0, NT3, da_own, (zrow, zrow))
    for cp in cg_out:
        cp().start()
    sbuf[0, 0:1, :] = g_mask
    sbuf[0, 1:2, :] = g_gain_a

    smalls = [
        remote(lambda k, i, n=n, dev=dev: rc(k, sbuf.at[n], srec.at[n], dev))
        for n, dev in enumerate([sib, ypeer] + peers)
    ]
    s_last = remote(
        lambda k, i: rc(k, sbuf.at[nbits + 2], srec.at[nbits + 2], sib)
    )
    row = lax.broadcasted_iota(jnp.int32, (8, D), 0)

    def small_step(n):
        smalls[n]().wait_recv()
        new = srec[n]
        if n == 0:
            new = jnp.where(row < 4, new, 0.0)
        sbuf[n + 1] = sbuf[n] + new
        if n + 1 < len(smalls):
            smalls[n + 1]().start()
        else:
            s_last().start()

    def small_rest():
        for n in range(4, len(smalls)):
            small_step(n)

    small_sum = Chunk()
    small_sum.events = [functools.partial(small_step, n) for n in range(4)] + [
        small_rest, lambda: s_last().wait_recv(),
    ]
    chunks["s"] = small_sum
    smalls[0]().start()
    handle(("da", 1))

    sent(s_dn)

    def bo_other(i, carry):
        x = dot(act[pl.ds(mo(T + 256 * i, 128), 256), :], wd[...])
        xs[pl.ds(mo(256 * i, 128), 256), :] = x.astype(BF)
        s_bo(i).start()
        return carry

    lax.fori_loop(0, NT3, bo_other, 0)
    handle(("bo", 0))
    sent(s_nm)

    def bo_own(i, carry):
        rows = pl.ds(mo(256 * i, 128), 256)
        x = aa[rows, :] + dot(act[rows, :], wd[...])
        s_bo(i).wait_recv()
        nm[rows, :] = (x + xr[rows, :].astype(F32) + bias_d).astype(BF)
        return carry

    lax.fori_loop(0, NT3, bo_own, 0)
    l_out = [
        local(
            nm.at[pl.ds(128 * r, 128)],
            out_h.at[0, pl.ds((r % 2) * L + 128 * (r // 2), 128)],
        )
        for r in range(2 * NT3)
    ]
    for cp in l_out:
        cp().start()
    handle(("bo", 1))
    handle("tail")
    for ch in chunks.values():
        ch.events[-1]()
    last = len(smalls)
    tot = sbuf[last]
    oth = srec[last]
    mh = jnp.where(f == 0, tot[0:4, 0:L], tot[0:4, L:D])
    fin[0:4, :] = mh
    for core_off, x in ((c, tot), (1 - c, oth)):
        v = jnp.where(f == 0, x[4:5, :], x[5:6, :])
        fin[pl.ds(4 + 2 * core_off, 1), :] = v[:, 0:L]
        fin[pl.ds(5 + 2 * core_off, 1), :] = v[:, L:D]
    for cp in l_out + cg_out:
        cp().wait()
    for fam, n in list(ends):
        sent(fam)


def tables(length):
    pos = np.arange(length, dtype=np.float32)
    half = HD // 2
    spacing = (10000.0 ** (-2.0 * np.arange(half, dtype=np.float64) / HD)).astype(np.float32)
    ang = (pos[:, None] * spacing[None, :]).astype(np.float64)
    cos = np.tile(np.cos(ang), (1, 4)).astype(np.float32)
    sin = np.sin(ang)
    sin = np.tile(np.concatenate([-sin, sin], axis=1), (1, 2)).astype(np.float32)
    return cos, sin


def finish_kernel(
    o1_h, od_h, fin, bo_h, cg_h,
    gq_h, go_h, gu_h, gd_h, out_h, clean_h, v_mask, v_ga, v_gm, v_bd, v_bu,
    b1, bd, fq, fo, fu, fd, bo, cg, ls,
):
    L, D, NB = 384, 768, 4
    count = [0]

    def copy(src, dst):
        k = count[0]
        count[0] += 1
        cp = pltpu.make_async_copy(src, dst, ls.at[k])
        cp.start()
        return cp

    rows = [pl.ds(L // NB * r, L // NB) for r in range(NB)]
    in1 = [copy(o1_h.at[:, rows[r]], b1.at[:, rows[r]]) for r in range(NB)]
    ind = [copy(od_h.at[core], bd.at[core]) for core in range(2)]
    through = [copy(bo_h, bo), copy(cg_h, cg)]
    outs = []
    for r in range(NB):
        in1[r].wait()
        for core in range(2):
            for h in range(2):
                fu[rows[r], 1536 * h + D * core : 1536 * h + D * core + D] = b1[
                    core, rows[r], D * h : D * h + D
                ].astype(F32)
            for p in range(3):
                for kind in range(3):
                    src = 1536 + L * p + 128 * kind
                    dst = D * kind + L * core + 128 * p
                    fq[rows[r], dst : dst + 128] = b1[core, rows[r], src : src + 128].astype(F32)
            fo[rows[r], L * core : L * core + L] = b1[
                core, rows[r], 1536 + 3 * L : 1536 + 4 * L
            ].astype(F32)
        for buf, ref in ((fu, gu_h), (fq, gq_h), (fo, go_h)):
            outs.append(copy(buf.at[rows[r]], ref.at[rows[r]]))
        if r < 2:
            through[r].wait()
            outs.append(copy((bo, cg)[r], (out_h, clean_h)[r]))
    for core in range(2):
        ind[core].wait()
        for r in range(2):
            part = slice(L * r, L * r + L)
            at = D * core + L * r
            fd[at : at + L, :] = bd[core, part, :].astype(F32)
            outs.append(copy(fd.at[pl.ds(at, L)], gd_h.at[pl.ds(at, L)]))
    v_mask[...] = fin[0, :]
    v_ga[...] = fin[1, :]
    v_gm[...] = fin[2, :]
    v_bd[...] = fin[3, :]
    for r in range(4):
        v_bu[L * r : L * r + L] = fin[4 + r, :]
    for cp in outs:
        cp.wait()


def on_device(
    nbits, clean_in, noise_bits, mask_vector, gain_attn, w_qkv, w_out, gain_mlp,
    w_up, bias_up, w_down, bias_down, out_grad,
):
    L, D, T = 384, 768, 768
    cos, sin = tables(L)
    nx = max(1, nbits - 3)
    hbm = pl.BlockSpec(memory_space=pltpu.HBM)
    vm = pl.BlockSpec(memory_space=pltpu.VMEM)
    scratch = [
        ((8, L), F32), ((2, 8, L), F32), ((8, D), F32), ((L, 128), F32), ((256, 128), F32),
        ((128, 256), F32), ((128, 128), F32),
        ((T, D), BF), ((2 * T, D), BF), ((D, 1152), BF), ((D, D), BF), ((D, 1536), BF),
        ((1536, D), BF), ((2 * T, D), BF),
        ((2 * T, 1152), BF), ((2 * T, D), BF), ((2 * T, D), BF), ((T, D), F32),
        ((2 * T, D), BF), ((2 * T, 1536), BF), ((2 * T, 1536), BF), ((T, D), BF),
        ((T, D), BF), ((T, D), F32), ((2 * T, D), BF), ((2 * T, L), BF), ((T, 128), F32),
        ((2, 3, 128, 128), BF),
        ((1536, D), BF), ((D, 3072), BF),
        ((D, D), BF), ((L, 3072), BF), ((L, D), BF), ((192, 3072), BF),
        ((192, D), BF), ((96, 3072), BF), ((96, D), BF), ((48, 3072), BF),
        ((nx, 96, D), BF) if nbits > 3 else ((1, 16, 128), BF),
        ((nx, 48, 3072), BF) if nbits > 3 else ((1, 16, 128), BF),
        ((nbits + 3, 8, D), F32), ((nbits + 3, 8, D), F32),
    ]
    block_out, clean_grad, fin, g1, gd = pl.pallas_call(
        functools.partial(layer_kernel, nbits),
        out_shape=[
            jax.ShapeDtypeStruct((1, T, D), BF),
            jax.ShapeDtypeStruct((1, L, D), F32),
            jax.ShapeDtypeStruct((8, L), F32),
            jax.ShapeDtypeStruct((2, L, 3072), BF),
            jax.ShapeDtypeStruct((2, D, D), BF),
        ],
        in_specs=[hbm] + [vm] * 8 + [hbm] * 5,
        out_specs=[hbm, hbm, vm, hbm, hbm],
        scratch_shapes=[pltpu.VMEM(s, t) for s, t in scratch]
        + [
            pltpu.SemaphoreType.DMA((N_SEND,)),
            pltpu.SemaphoreType.DMA((N_RECV + 20 * (nx - 1),)),
            pltpu.SemaphoreType.DMA((N_LOCAL,)),
        ],
        compiler_params=pltpu.CompilerParams(
            collective_id=0, has_side_effects=True, vmem_limit_bytes=64 * 2**20
        ),
        name="layer",
    )(
        clean_in, noise_bits, mask_vector, gain_attn, gain_mlp, bias_down, bias_up, cos, sin,
        w_qkv, w_out, w_up, w_down, out_grad,
    )
    vec = jax.ShapeDtypeStruct((L,), F32)
    gq, go, gu, gdown, out, clean, v_mask, v_ga, v_gm, v_bd, v_bu = pl.pallas_call(
        finish_kernel,
        out_shape=[
            jax.ShapeDtypeStruct((L, 2304), F32),
            jax.ShapeDtypeStruct((L, D), F32),
            jax.ShapeDtypeStruct((L, 3072), F32),
            jax.ShapeDtypeStruct((1536, D), F32),
            jax.ShapeDtypeStruct((1, T, D), BF),
            jax.ShapeDtypeStruct((1, L, D), F32),
            vec, vec, vec, vec, jax.ShapeDtypeStruct((4 * L,), F32),
        ],
        in_specs=[hbm, hbm, vm, hbm, hbm],
        out_specs=[hbm] * 6 + [vm] * 5,
        scratch_shapes=[
            pltpu.VMEM((2, L, 3072), BF), pltpu.VMEM((2, D, D), BF),
            pltpu.VMEM((L, 2304), F32), pltpu.VMEM((L, D), F32),
            pltpu.VMEM((L, 3072), F32), pltpu.VMEM((1536, D), F32),
            pltpu.VMEM((1, T, D), BF), pltpu.VMEM((1, L, D), F32),
            pltpu.SemaphoreType.DMA((26,)),
        ],
        compiler_params=pltpu.CompilerParams(vmem_limit_bytes=64 * 2**20),
        name="finish",
    )(g1, gd, fin, block_out, clean_grad)
    return out, clean, v_mask, v_ga, gq, go, v_gm, gu, v_bu, gdown, v_bd


def solution(mesh):
    nbits = int(math.log2(mesh.shape["dp"])) - 1
    seq = P(("dp", "fsdp"), None, None)
    row, vec = P("fsdp", None), P("fsdp")
    in_specs = (seq, P(("dp", "fsdp"), None), vec, vec, row, row, vec, row, vec, row, vec, seq)
    out_specs = (seq, seq, vec, vec, row, row, vec, row, vec, row, vec)
    return jax.shard_map(
        functools.partial(on_device, nbits), mesh=mesh,
        in_specs=in_specs, out_specs=out_specs, check_vma=False,
    )
```

```python
import functools
import math

import jax
import jax.numpy as jnp
import numpy as np
from jax import lax
from jax.experimental import pallas as pl
from jax.experimental.pallas import tpu as pltpu
from jax.sharding import PartitionSpec as P

HD = 64
BLOCK = 16
NORM_FLOOR = 1e-05
TANH_SCALE = 0.7978845608028654
CUBIC = 0.044715
BF = jnp.bfloat16
F32 = jnp.float32
MESH = pl.DeviceIdType.MESH
LOGIT_SCALE = 0.125 * math.log2(math.e)
N_SEND, N_RECV, N_LOCAL = 102, 182, 38
NN = (((1,), (0,)), ((), ()))
NT = (((1,), (1,)), ((), ()))
TN = (((0,), (0,)), ((), ()))


ROUTES = {
    "d0": "y0Z",
    "d1": "y0Z",
    "d2": "y012",
    "u0": "10y2",
    "u1": "0y12",
    "u2": "y0Z",
    "u3": "y012",
    "u4": "1y02",
    "u5": "1y02",
    "q0": "0y12",
    "q1": "y102",
    "q2": "y0Z",
    "o": "0y12",
}
SCHEDULE = {
    ("b", 1): (
        ("d0", 0),
    ),
    ("dn", 0): (
        ("d1", 0),
        ("d0", 1),
    ),
    ("dn", 1): (
        ("u0", 0),
        ("u1", 0),
    ),
    ("dm", 0): (
        ("u4", 0),
        ("d2", 0),
        ("d1", 1),
    ),
    ("att", 0): (
        ("u0", 1),
        ("u5", 0),
        ("u2", 0),
    ),
    ("att", 1): (
        ("d0", 2),
    ),
    ("q", 0): (
        ("u3", 0),
        ("d1", 2),
    ),
    ("att", 2): (
        ("o", 0),
        ("u1", 1),
    ),
    ("att", 3): (
        ("u4", 1),
        ("u0", 2),
        ("d0", 3),
        ("d2", 1),
    ),
    ("q", 1): (
        ("u5", 1),
        ("u2", 1),
        ("u1", 2),
    ),
    ("att", 4): (
        ("d1", 3),
        ("o", 1),
        ("u0", 3),
        ("d2", 2),
    ),
    ("att", 5): (
        ("u2", 2),
        ("q0", 0),
        ("u1", 3),
    ),
    ("q", 2): (
        ("o", 2),
        ("u3", 1),
        ("u0", 4),
        ("q1", 0),
        ("u4", 2),
        ("d2", 3),
    ),
    ("da", 0): (
        ("u2", 3),
        ("q0", 1),
    ),
    ("da", 1): (
        ("u1", 4),
        ("u3", 2),
        ("d0", 4),
        ("o", 3),
        ("u5", 2),
        ("q1", 1),
        ("u4", 3),
    ),
    ("bo", 0): (
        ("d2", 4),
        ("s", 0),
        ("d1", 4),
        ("q2", 0),
        ("q0", 2),
        ("u0", 5),
        ("u1", 5),
        ("u3", 3),
    ),
    ("bo", 1): (
        ("u2", 4),
        ("o", 4),
        ("u5", 3),
        ("q1", 2),
        ("s", 1),
        ("u4", 4),
        ("d2", 5),
    ),
    "tail": (
        ("q0", 3),
        ("q2", 1),
        ("u0", 6),
        ("u3", 4),
        ("u1", 6),
        ("s", 2),
        ("o", 5),
        ("u4", 5),
        ("u5", 4),
        ("q1", 3),
        ("q0", 4),
        ("d2", 6),
        ("q2", 2),
        ("u3", 5),
        ("s", 3),
        ("o", 6),
        ("u4", 6),
        ("u5", 5),
        ("q1", 4),
        ("q0", 5),
        ("u3", 6),
        ("q1", 5),
        ("q2", 3),
        ("s", 4),
        ("u5", 6),
        ("q0", 6),
        ("q1", 6),
        ("q2", 4),
    ),
}


def dot(a, b, dims=NN):
    return lax.dot_general(a, b, dims, preferred_element_type=F32)


def mo(x, n):
    return pl.multiple_of(x, n)


def normalize(x):
    d = x - jnp.mean(x, axis=-1, keepdims=True)
    inv = lax.rsqrt(jnp.mean(d * d, axis=-1, keepdims=True) + NORM_FLOOR)
    return d * inv, inv


def normalize_backward(g, xhat, inv, gain):
    e = g * gain
    return inv * (
        e
        - jnp.mean(e, axis=-1, keepdims=True)
        - xhat * jnp.mean(e * xhat, axis=-1, keepdims=True)
    )


def layer_kernel(
    nbits,
    clean_h, noise, v_mask, v_ga, v_gm, v_bd, v_bu, cos_r, sin_r, wq_h, wo_h, wu_h, wd_h, og_h,
    out_h, cg_h, fin, o1_h, od_h,
    small_in, small, prow, mcol, mbb, mbe,
    stream, normed, wq, wo, wu, wd, og,
    qkv, lbuf, mixed, aa, nm, act, dpre, xs, xr, daf, db, dm, dks,
    gd, g1, r0d, r01, r1d, r11, r2d, r21, r3d, r31, red, re1,
    sbuf, srec, ss, rs, ls,
):
    L = 384
    D = 768
    T = 2 * L
    NT3 = L // 128
    d = lax.axis_index("dp")
    f = lax.axis_index("fsdp")
    c = lax.rem(d, 2)
    bits = [lax.rem(lax.div(d, 2 ** (b + 1)), 2) for b in range(nbits)]
    sib = (d + 1 - 2 * c, f)
    ypeer = (d, 1 - f)
    peers = [(d + (1 - 2 * bits[b]) * 2 ** (b + 1), f) for b in range(nbits)]
    u = 2 * bits[1] + bits[0]
    send_count, recv_count, local_count = [0], [0], [0]
    ends = []

    def take_send(n):
        k = send_count[0]
        send_count[0] += n
        return k

    def take_recv(n=1):
        k = recv_count[0]
        recv_count[0] += n
        return k

    def rc(k, src, dst, dev):
        return pltpu.make_async_remote_copy(
            src_ref=src, dst_ref=dst, send_sem=ss.at[k[0]], recv_sem=rs.at[k[1]],
            device_id=dev, device_id_type=MESH,
        )

    def remote(make, n=1):
        k = (take_send(n), take_recv(n))
        fam = lambda i=0: make((k[0] + i, k[1] + i), i)
        ends.append((fam, n))
        return fam

    def sent(fam):
        for at, (other_fam, n) in enumerate(ends):
            if other_fam is fam:
                for i in range(n):
                    fam(i).wait_send()
                ends.pop(at)
                return

    def local(src, dst):
        k = local_count[0]
        local_count[0] += 1
        return lambda: pltpu.make_async_copy(src, dst, ls.at[k])

    bar = pltpu.get_barrier_semaphore()
    for dev in [sib, ypeer] + peers:
        pl.semaphore_signal(bar, inc=1, device_id=dev, device_id_type=MESH)

    l_clean = [
        local(clean_h.at[0, pl.ds(128 * i, 128)], stream.at[pl.ds(256 * i + 128, 128)])
        for i in range(NT3)
    ]
    mine = mo(f * L, 128)
    other = mo((1 - f) * L, 128)
    l_wq = [
        local(
            wq_h.at[:, pl.ds(mo(j * D + c * L, 128), L)],
            wq.at[pl.ds(mine, L), pl.ds(j * L, L)],
        )
        for j in range(3)
    ]
    l_wo = local(wo_h, wo.at[pl.ds(mine, L)])
    l_wu = [
        local(
            wu_h.at[:, pl.ds(mo(h * 1536 + c * D, 128), D)],
            wu.at[pl.ds(mine, L), pl.ds(h * D, D)],
        )
        for h in range(2)
    ]
    l_wd = local(wd_h.at[pl.ds(mo(c * D, 128), D)], wd.at[pl.ds(mo(f * D, 128), D)])
    l_og = [
        local(
            og_h.at[0, pl.ds((r % 2) * L + 128 * (r // 2), 128)],
            og.at[pl.ds(128 * r, 128)],
        )
        for r in range(2 * NT3)
    ]
    for cp in l_clean + l_wq:
        cp().start()
    for r, v in enumerate((v_mask, v_ga, v_gm, v_bd)):
        small_in[r : r + 1, :] = v[...].astype(F32).reshape(1, L)
    for r in range(4):
        small_in[4 + r : 5 + r, :] = v_bu[pl.ds(L * r, L)].astype(F32).reshape(1, L)
    small[pl.ds(f, 1)] = small_in[...][None]

    def y_wq(unit):
        rows = mo(96 * unit, 16)
        return remote(
            lambda k, j: rc(
                k,
                wq_h.at[pl.ds(rows, 96), pl.ds(mo(j * D + c * L, 128), L)],
                wq.at[pl.ds(mo(f * L + rows, 16), 96), pl.ds(j * L, L)],
                ypeer,
            ),
            3,
        )

    yw_q = y_wq(u)
    yw_q2 = y_wq(3 - u)
    y_small = remote(lambda k, i: rc(k, small_in, small.at[f], ypeer))

    def spread(buf, base, unit_rows, unit, dev):
        rows = mo(base + unit_rows * unit, 16)
        return remote(
            lambda k, i: rc(
                k, buf.at[pl.ds(rows, unit_rows)], buf.at[pl.ds(rows, unit_rows)], dev
            )
        )


    def spread_q(dev):
        rows = mo(other + 96 * u, 16)
        return remote(
            lambda k, j: rc(
                k, wq.at[pl.ds(rows, 96), pl.ds(j * L, L)],
                wq.at[pl.ds(rows, 96), pl.ds(j * L, L)], dev,
            ),
            3,
        )

    xw_q = spread_q(peers[0])
    zw_q = spread_q(peers[1])
    def half_of(i):
        if isinstance(i, int):
            return 1 - f if i == 0 else f
        return (1 - f) * (1 - i) + f * i

    def up_lanes(i):
        return pl.ds(mo(half_of(i) * D, 128), D)

    def y_wu_to(unit):
        rows = mo(96 * unit, 16)

        def make(k, i):
            h = f if i == 0 else 1 - f
            return rc(
                k,
                wu_h.at[pl.ds(rows, 96), pl.ds(mo(h * 1536 + c * D, 128), D)],
                wu.at[pl.ds(mo(f * L + rows, 16), 96), pl.ds(mo(h * D, 128), D)],
                ypeer,
            )

        return remote(make, 2)

    def spread_u(dev):
        rows = mo(other + 96 * u, 16)
        return remote(
            lambda k, i: rc(
                k, wu.at[pl.ds(rows, 96), up_lanes(i)], wu.at[pl.ds(rows, 96), up_lanes(i)], dev
            ),
            2,
        )

    yw_u = y_wu_to(u)
    yw_u2 = y_wu_to(3 - u)
    xw_u = spread_u(peers[0])
    zw_u = spread_u(peers[1])
    ux, uz = 2 * bits[1] + 1 - bits[0], 2 * (1 - bits[1]) + bits[0]
    odown = mo((1 - f) * D, 128)
    yw_d = remote(
        lambda k, i: rc(
            k,
            wd_h.at[pl.ds(mo(c * D + 192 * u + 96 * i, 16), 96)],
            wd.at[pl.ds(mo(f * D + 192 * u + 96 * i, 16), 96)],
            ypeer,
        ),
        2,
    )

    def spread_d(dev):
        def make(k, i):
            rows = pl.ds(mo(odown + 192 * u + 96 * i, 16), 96)
            return rc(k, wd.at[rows], wd.at[rows], dev)

        return remote(make, 2)

    xw_d = spread_d(peers[0])
    zw_d = spread_d(peers[1])
    xw_d2 = spread(wd, odown, 96, 2 * uz, peers[0])
    zw_d2 = spread(wd, odown, 96, 2 * ux + 1, peers[1])
    yw_o = remote(
        lambda k, i: rc(
            k,
            wo_h.at[pl.ds(mo(192 * c + 96 * bits[0], 16), 96)],
            wo.at[pl.ds(mo(f * L + 192 * c + 96 * bits[0], 16), 96)],
            ypeer,
        )
    )
    xw_o = spread(wo, mo(other + 192 * c, 16), 96, bits[0], peers[0])
    sw_o = spread(wo, other, 192, c, sib)

    s_norm = remote(
        lambda k, i: rc(
            k, normed.at[pl.ds(mo(256 * i, 16), 256)],
            normed.at[pl.ds(mo(T + 256 * i, 16), 256)], sib,
        ),
        NT3,
    )
    s_og = remote(lambda k, i: rc(k, og.at[pl.ds(0, T)], og.at[pl.ds(T, T)], sib))

    def mixed_copy(k, i):
        s = 1 - i // 3 if isinstance(i, int) else 1 - lax.div(i, 3)
        p = i % 3 if isinstance(i, int) else lax.rem(i, 3)
        lanes = pl.ds(mo(c * L + 128 * p, 128), 128)
        return rc(
            k, mixed.at[pl.ds(mo(s * T, 16), T), lanes],
            mixed.at[pl.ds(mo((1 - s) * T, 16), T), lanes], sib,
        )

    s_mix = remote(mixed_copy, 6)

    def rows_copy(buf, src0, dst, dst0):
        return remote(
            lambda k, i: rc(
                k, buf.at[pl.ds(mo(src0 + 256 * i, 16), 256)],
                dst.at[pl.ds(mo(dst0 + 256 * i, 16), 256)], sib,
            ),
            NT3,
        )

    s_nm = rows_copy(nm, 0, nm, T)
    s_dn = rows_copy(xs, 0, xr, 0)
    s_db = rows_copy(db, 0, db, T)
    s_bo = rows_copy(xs, 0, xr, 0)
    right = pl.ds(D, D)
    s_da = remote(
        lambda k, i: rc(
            k, dpre.at[pl.ds(mo(256 * i, 16), 256), right],
            dpre.at[pl.ds(mo(T + 256 * i, 16), 256), right], sib,
        ),
        NT3,
    )

    class Chunk:
        pass

    chunks = {}

    def make_chunk(name, g, gbase, nr, l0, nl, recv, rbase, oref, orow, blk):
        ch = Chunk()
        lanes = pl.ds(l0, nl)
        route = ROUTES[name]

        def greg(h, off, n):
            return g.at[pl.ds(mo(gbase(h) + off, 16), n), lanes]

        def rreg(stage, at, n):
            return recv[stage].at[pl.ds((rbase >> stage) + at, n), lanes]

        def oreg(core, off, n):
            return oref.at[core, pl.ds(mo(orow + off, 16), n), lanes]

        def send(copies, before=()):
            for cp in before:
                cp().wait_send()
            for cp in copies:
                cp().start()

        k_send = take_send(3)

        def copy(i, src, dst, dev):
            k = take_recv()
            return lambda: pltpu.make_async_remote_copy(
                src_ref=src(), dst_ref=dst(), send_sem=ss.at[k_send + i], recv_sem=rs.at[k],
                device_id=dev, device_id_type=MESH,
            )

        def add(h, off, n, parts):
            gr = greg(h, off, n)
            step = min(blk, n)

            def body(i, carry):
                sl = pl.ds(mo(i * step, 16), step)
                x = gr[sl, :].astype(F32)
                for stage, at in parts:
                    x = x + rreg(stage, at, n)[sl, :].astype(F32)
                gr[sl, :] = x.astype(BF)
                return carry

            lax.fori_loop(0, n // step, body, 0)

        sends, adds, gathers = [], [], []
        off, n, both, stage = 0, nr, True, 0
        for step in route:
            if step == "y":
                sends.append([copy(
                    0, lambda off=off, n=n: greg(1 - f, off, n),
                    lambda stage=stage, n=n: rreg(stage, 0, n), ypeer,
                )])
                adds.append([(f, off, n, [(stage, 0)])])
                both = False
                stage += 1
            elif step == "Z":
                m4 = n // 4
                out, parts, back = [], [], []
                where = [(stage, 0), (stage, m4), (stage + 1, 0)]
                mine_off = off + (2 * bits[1] + bits[2]) * m4
                for i, (x1, x2) in enumerate(((0, 1), (1, 0), (1, 1))):
                    b1 = 1 - bits[1] if x1 else bits[1]
                    b2 = 1 - bits[2] if x2 else bits[2]
                    dev = (d + (b1 - bits[1]) * 4 + (b2 - bits[2]) * 8, f)
                    to = off + (2 * b1 + b2) * m4
                    st, at = where[i]
                    out.append(copy(
                        i, lambda to=to, m4=m4: greg(f, to, m4),
                        lambda st=st, at=at, m4=m4: rreg(st, at, m4), dev,
                    ))
                    back.append(dev)
                    parts.append((st, at))
                sends.append(out)
                adds.append([(f, mine_off, m4, parts)])
                gathers.append((mine_off, m4, back))
                off, n, stage = mine_off, m4, stage + 2
            else:
                j = int(step)
                m2 = n // 2
                give, keep = off + (1 - bits[j]) * m2, off + bits[j] * m2
                owners = [0, 1] if both else [f]
                sends.append([
                    copy(
                        i, lambda h=h, give=give, m2=m2: greg(h, give, m2),
                        lambda stage=stage, i=i, m2=m2: rreg(stage, i * m2, m2), peers[j],
                    )
                    for i, h in enumerate(owners)
                ])
                adds.append([(h, keep, m2, [(stage, i * m2)]) for i, h in enumerate(owners)])
                gathers.append((keep, m2, [peers[j]]))
                off, n, stage = keep, m2, stage + 1
        extra = [
            copy(
                0, lambda off=off, n=n: greg(f, off, n),
                lambda j=j, n=n: recv[4].at[j - 3, pl.ds((rbase >> 3), n), lanes], peers[j],
            )
            for j in range(3, nbits)
        ]
        own = local(greg(f, off, n), oreg(c, off, n))
        back = []
        for depth, (at, m, devs) in enumerate(reversed(gathers)):
            back.append([
                copy(
                    i,
                    (lambda at=at, m=m: greg(f, at, m)) if depth == 0
                    else (lambda at=at, m=m: oreg(c, at, m)),
                    lambda at=at, m=m: oreg(c, at, m), dev,
                )
                for i, dev in enumerate(devs)
            ])
        back.append([copy(0, lambda: oreg(c, 0, nr), lambda: oreg(c, 0, nr), sib)])

        def reduce_event(i):
            for cp in sends[i]:
                cp().wait_recv()
            for h, at, m, parts in adds[i]:
                add(h, at, m, parts)
            if i + 1 < len(sends):
                send(sends[i + 1], sends[i])
                return
            send((), sends[i])
            for m, cp in enumerate(extra):
                send([cp])
                send((), [cp])
                cp().wait_recv()
                gr = greg(f, off, n)
                gr[...] = (
                    gr[...].astype(F32)
                    + recv[4][m, pl.ds((rbase >> 3), n), lanes].astype(F32)
                ).astype(BF)
            own().start()
            send(back[0])

        def gather_event(i):
            for cp in back[i]:
                cp().wait_recv()
            if i == 0:
                own().wait()
            if i + 1 < len(back):
                send(back[i + 1], back[i])
            else:
                send((), back[i])

        ch.start = lambda: send(sends[0])
        ch.events = [functools.partial(reduce_event, i) for i in range(len(sends))] + [
            functools.partial(gather_event, i) for i in range(len(back))
        ]
        chunks[name] = ch

    recv_d = (r0d, r1d, r2d, r3d, red)
    recv_1 = (r01, r11, r21, r31, re1)
    for k in range(3):
        make_chunk(
            f"d{k}", gd, lambda h, k=k: h * D + 256 * k, 256, 0, D, recv_d, 256 * k,
            od_h, 256 * k, 32,
        )
    for t in range(6):
        make_chunk(f"u{t}", g1, lambda h: h * L, L, 256 * t, 256, recv_1, 0, o1_h, 0, 48)
    for p in range(3):
        make_chunk(f"q{p}", g1, lambda h: h * L, L, 1536 + L * p, L, recv_1, 0, o1_h, 0, 48)
    make_chunk("o", g1, lambda h: h * L, L, 1536 + 3 * L, L, recv_1, 0, o1_h, 0, 48)

    def handle(key):
        for name, stage in SCHEDULE.get(key, ()):
            chunks[name].events[stage]()

    def handle_at(idx, keys):
        for i, key in keys.items():
            if SCHEDULE.get(key):
                pl.when(idx == i)(lambda key=key: handle(key))

    pl.semaphore_wait(bar, 2 + nbits)
    y_small().start()
    for j in range(3):
        yw_q(j).start()
    for j in range(3):
        yw_q2(j).start()
    yw_o().start()
    for i in range(2):
        yw_u(i).start()
        yw_u2(i).start()
    for i in range(2):
        yw_d(i).start()
    for cp in l_og + l_wu + [l_wo, l_wd]:
        cp().start()

    lane = lax.broadcasted_iota(jnp.int32, (1, 128), 1)
    low_half = lane < HD
    rot_low = lax.rem(lane, HD) < HD // 2
    bm = [jnp.where(low_half, 1.0, 0.0).astype(BF), jnp.where(low_half, 0.0, 1.0).astype(BF)]
    ir = lax.div(lax.broadcasted_iota(jnp.int32, (128, 128), 0), BLOCK)
    ic = lax.div(lax.broadcasted_iota(jnp.int32, (128, 128), 1), BLOCK)
    neg = -1e30
    mbb[:, 0:128] = jnp.where(ir < ic, 0.0, neg)
    mbb[:, 128:256] = jnp.where(ir <= ic, 0.0, neg)
    mbe[...] = jnp.where(ir == ic, 0.0, neg)
    nf = noise[...].astype(F32)
    for i in range(NT3):
        mcol[128 * i : 128 * i + 128, :] = jnp.broadcast_to(
            nf[:, 128 * i : 128 * i + 128], (128, 128)
        ).T
    sbuf[0] = jnp.zeros((8, D), F32)

    y_small().wait_recv()
    prow[:, 0:L] = small[0]
    prow[:, L:D] = small[1]
    mvec = prow[0:1, :]
    gain_a = prow[1:2, :]
    gain_m = prow[2:3, :]
    bias_d = prow[3:4, :]

    def wide(m):
        return jnp.concatenate([m] * (D // 128), axis=1)

    for i in range(NT3):
        l_clean[i]().wait()

    def attn_norm(i, carry):
        n0 = mo(256 * i, 128)
        x = stream[pl.ds(n0 + 128, 128), :].astype(F32)
        m = wide(mcol[pl.ds(mo(128 * i, 128), 128), :])
        y = jnp.where(m > 0.5, mvec, x)
        stream[pl.ds(n0, 128), :] = y.astype(BF)
        normed[pl.ds(n0, 128), :] = (normalize(y)[0] * gain_a).astype(BF)
        normed[pl.ds(n0 + 128, 128), :] = (normalize(x)[0] * gain_a).astype(BF)
        s_norm(i).start()
        return carry

    lax.fori_loop(0, NT3, attn_norm, 0)

    for j in range(3):
        yw_q(j).wait_recv()
        xw_q(j).start()
        zw_q(j).start()
    for i in range(NT3):
        s_norm(i).wait_recv()
    for cp in l_og:
        cp().wait()
    s_og().start()
    for j in range(3):
        l_wq[j]().wait()
        yw_q2(j).wait_recv()
        xw_q(j).wait_recv()
        zw_q(j).wait_recv()

    def turn(x, cos, sin):
        return x * cos + jnp.where(rot_low, pltpu.roll(x, 96, 1), pltpu.roll(x, 32, 1)) * sin

    def rows2(tab, i):
        t = tab[pl.ds(mo(128 * i, 128), 128), :]
        return jnp.concatenate([t, t], axis=0)

    def qkv_rows(r, carry):
        rows = pl.ds(mo(256 * r, 128), 256)
        joined = dot(normed[rows, :], wq[...])
        i = lax.rem(r, NT3)
        cos, sin = rows2(cos_r, i), rows2(sin_r, i)
        for p in range(6):
            x = joined[:, 128 * p : 128 * p + 128]
            qkv[rows, 128 * p : 128 * p + 128] = turn(x, cos, sin).astype(BF)
        qkv[rows, 2 * L : 3 * L] = joined[:, 2 * L : 3 * L].astype(BF)
        return carry

    lax.fori_loop(0, 2 * NT3, qkv_rows, 0)

    def run_at(idx, table):
        for k, fns in table.items():
            def go(fns=fns):
                for fn in fns:
                    fn()
            pl.when(idx == k)(go)

    def w_o_1():
        l_wo().wait()
        yw_o().wait_recv()
        xw_o().start()

    def w_o_2():
        xw_o().wait_recv()
        sw_o().start()

    def w_u(i):
        yw_u(i).wait_recv()
        xw_u(i).start()
        zw_u(i).start()

    def w_u_end(i):
        yw_u2(i).wait_recv()
        xw_u(i).wait_recv()
        zw_u(i).wait_recv()

    def w_d(i):
        yw_d(i).wait_recv()
        xw_d(i).start()
        zw_d(i).start()

    fwd_events = {0: [w_o_1], 2: [lambda: w_u(0)], 4: [w_o_2]}

    def attn_fwd(n, carry):
        s, p = 1 - lax.div(n, 3), lax.rem(n, 3)
        r0 = s * T
        lq = pl.ds(mo(128 * p, 128), 128)
        lk = pl.ds(mo(L + 128 * p, 128), 128)
        lv = pl.ds(mo(2 * L + 128 * p, 128), 128)

        def rws(a, m):
            return pl.ds(mo(r0 + a, 128), m)

        kcl = [qkv[rws(256 * j + 128, 128), lk] for j in range(NT3)]
        vcl = [qkv[rws(256 * j + 128, 128), lv] for j in range(NT3)]
        blocks = [(i, a) for i in range(NT3) for a in range(2)]
        sc, pr, mixes = {}, {}, {}
        for i, a in blocks:
            q = qkv[rws(256 * i, 256), lq]
            kc = jnp.concatenate(kcl[: i + 1], axis=0) * bm[a]
            st = dot(kc, q, NT) * LOGIT_SCALE
            kn = qkv[rws(256 * i, 128), lk] * bm[a]
            sn = dot(kn, q[:128], NT) * LOGIT_SCALE + mbe[...]
            last = st[128 * i :] + mbb[...]
            st = last if i == 0 else jnp.concatenate([st[: 128 * i], last], axis=0)
            sc[i, a] = st, sn
        for i, a in blocks:
            st, sn = sc[i, a]
            m1 = jnp.max(st, axis=0, keepdims=True)
            mn = jnp.maximum(m1[:, :128], jnp.max(sn, axis=0, keepdims=True))
            m = jnp.concatenate([mn, m1[:, 128:]], axis=1)
            pt, pn = jnp.exp2(st - m), jnp.exp2(sn - mn)
            tot = jnp.sum(pt, axis=0, keepdims=True)
            totn = tot[:, :128] + jnp.sum(pn, axis=0, keepdims=True)
            tot = jnp.concatenate([totn, tot[:, 128:]], axis=1)
            lbuf[(s * 3 + p) * 2 + a, :, 256 * i : 256 * i + 256] = m + jnp.log2(tot)
            pr[i, a] = pt.astype(BF), pn.astype(BF)
        for i, a in blocks:
            vc = jnp.concatenate(vcl[: i + 1], axis=0) * bm[a] + bm[1 - a]
            vn = qkv[rws(256 * i, 128), lv] * bm[a] + bm[1 - a]
            o = dot(pr[i, a][0], vc, TN)
            mixes[i, a] = jnp.concatenate([o[:128] + dot(pr[i, a][1], vn, TN), o[128:]], axis=0)
        for i in range(NT3):
            o0, o1 = mixes[i, 0], mixes[i, 1]
            sums = pltpu.roll(jnp.where(low_half, o1, o0), HD, 1)
            mixed[rws(256 * i, 256), pl.ds(mo(c * L + 128 * p, 128), 128)] = (
                jnp.where(low_half, o0, o1) * (1.0 / sums)
            ).astype(BF)
        s_mix(n).start()
        run_at(n, fwd_events)
        return carry

    lax.fori_loop(0, 6, attn_fwd, 0)

    sw_o().wait_recv()
    for n in range(3):
        s_mix(n).wait_recv()

    def out_proj(i, carry):
        rows = pl.ds(mo(256 * i, 128), 256)
        x = stream[rows, :].astype(F32) + dot(mixed[rows, :], wo[...])
        aa[rows, :] = x
        nm[rows, :] = (normalize(x)[0] * gain_m).astype(BF)
        s_nm(i).start()
        return carry

    lax.fori_loop(0, NT3, out_proj, 0)
    for h in range(2):
        l_wu[h]().wait()
    w_u_end(0)
    w_u(1)

    for n in range(2):
        h = half_of(n)
        lanes = up_lanes(n)
        if n == 1:
            w_u_end(1)
            w_d(0)
        bu = jnp.concatenate(
            [small[h, pl.ds(4 + 2 * c + r, 1), :] for r in range(2)], axis=1
        )

        def rows_a(r, carry, n=n, lanes=lanes, bu=bu):
            if n == 0:
                @pl.when(r == 2)
                def _():
                    for i in range(NT3):
                        s_nm(i).wait_recv()

            rows = pl.ds(mo(L * r, 128), L)
            pre = dot(nm[rows, :], wu[:, lanes]) + bu
            sq = pre * pre
            half = 0.5 + 0.5 * jnp.tanh(pre * (TANH_SCALE + TANH_SCALE * CUBIC * sq))
            a = pre * half
            act[rows, lanes] = a.astype(BF)
            slope = half + 2.0 * a * (1.0 - half) * (
                TANH_SCALE + 3.0 * CUBIC * TANH_SCALE * sq
            )
            dpre[rows, lanes] = slope.astype(BF)
            return carry

        lax.fori_loop(0, 4, rows_a, 0)
        if n == 0:
            s_og().wait_recv()
        else:
            w_d(1)

        def down_grad(k, carry, n=n, h=h):
            at = mo(h * D + 256 * k, 128)
            gd[pl.ds(at, 256), :] = dot(act[:, pl.ds(at, 256)], og[...], TN).astype(BF)
            for i in range(3):
                early = ROUTES[f"d{i}"][0] == "y"
                if early == (n == 0):
                    pl.when(k == i)(chunks[f"d{i}"].start)
            handle_at(k, {i: ("a", n, i) for i in range(3)})
            return carry

        handle(("a", n))
        lax.fori_loop(0, 3, down_grad, 0)
    zw_d(0).wait_recv()
    xw_d2().start()
    l_wd().wait()

    for n in range(2):
        h = half_of(1 - n)
        lanes = up_lanes(1 - n)

        def rows_b(r, tot, lanes=lanes):
            rows = pl.ds(mo(L * r, 128), L)
            g = dot(og[rows, :], wd[lanes, :], NT) * dpre[rows, lanes].astype(F32)
            dpre[rows, lanes] = g.astype(BF)
            return tot + jnp.sum(g, axis=0, keepdims=True)

        if n == 1:
            xw_d(0).wait_recv()
            zw_d(1).wait_recv()
            xw_d2().wait_recv()
            zw_d2().wait_recv()
        sbuf[0, pl.ds(4 + h, 1), :] = lax.fori_loop(0, 4, rows_b, jnp.zeros((1, D), F32))
        if n == 0:
            xw_d(1).wait_recv()
            zw_d2().start()
        handle(("b", n))
    for n in range(2):
        g1[:, n * D : n * D + D] = dot(nm[...], dpre[:, n * D : n * D + D], TN).astype(BF)
        for t in range(3 * n, 3 * n + 3):
            chunks[f"u{t}"].start()
        handle(("u", n))

    def dn_other(i, carry):
        x = dot(dpre[pl.ds(mo(T + 256 * i, 128), 256), :], wu[...], NT)
        xs[pl.ds(mo(256 * i, 128), 256), :] = x.astype(BF)
        s_dn(i).start()
        return carry

    lax.fori_loop(0, NT3, dn_other, 0)
    handle(("dn", 0))

    def dn_own(i, sums):
        rows = pl.ds(mo(256 * i, 128), 256)
        g = dot(dpre[rows, :], wu[...], NT)
        s_dn(i).wait_recv()
        g = g + xr[rows, :].astype(F32)
        xhat, inv = normalize(aa[rows, :])
        ograd = og[rows, :].astype(F32)
        after = ograd + normalize_backward(g, xhat, inv, gain_m)
        daf[rows, :] = after
        db[rows, :] = after.astype(BF)
        s_db(i).start()
        return (
            sums[0] + jnp.sum(g * xhat, axis=0, keepdims=True),
            sums[1] + jnp.sum(ograd, axis=0, keepdims=True),
        )

    zrow = jnp.zeros((1, D), F32)
    g_gain_m, g_bias_d = lax.fori_loop(0, NT3, dn_own, (zrow, zrow))
    sbuf[0, 2:3, :] = g_gain_m
    sbuf[0, 3:4, :] = g_bias_d
    handle(("dn", 1))

    wo_rows = pl.ds(mo(c * L, 128), L)
    dm[0:T, :] = dot(db[0:T, :], wo[wo_rows, :], NT).astype(BF)
    for i in range(NT3):
        s_db(i).wait_recv()
    dm[T : 2 * T, :] = dot(db[T : 2 * T, :], wo[wo_rows, :], NT).astype(BF)
    for n in range(3, 6):
        s_mix(n).wait_recv()
    g1[:, 1536 + 3 * L : 1536 + 4 * L] = dot(mixed[...], db[:, wo_rows], TN).astype(BF)
    chunks["o"].start()
    handle(("dm", 0))

    pick_lane = lax.rem(lax.broadcasted_iota(jnp.int32, (8, 256), 1), 128)
    pick_row = lax.broadcasted_iota(jnp.int32, (8, 256), 0)
    pick = jnp.where(pick_row == lax.div(pick_lane, HD), 1.0, 0.0).astype(BF)

    def attn_bwd(n, carry):
        s, p = lax.rem(n, 2), lax.div(n, 2)
        r0 = s * T
        lq = pl.ds(mo(128 * p, 128), 128)
        lk = pl.ds(mo(L + 128 * p, 128), 128)
        lv = pl.ds(mo(2 * L + 128 * p, 128), 128)

        def rws(a, m):
            return pl.ds(mo(r0 + a, 128), m)

        prod = dm[rws(0, T), lq].astype(F32) * mixed[
            rws(0, T), pl.ds(mo(c * L + 128 * p, 128), 128)
        ].astype(F32)
        hi = prod.astype(BF)
        lo = (prod - hi.astype(F32)).astype(BF)
        drow = dot(pick, jnp.concatenate([hi, lo], axis=1), NT)

        def heads(x, y):
            return jnp.where(low_half, x, y)

        blocks = [(kt, a) for kt in range(NT3) for a in range(2)]
        sc, dp, res = {}, {}, {}
        for kt, a in blocks:
            q0, nq = 256 * kt, T - 256 * kt
            q = qkv[rws(q0, nq), lq]
            lt = lbuf[(s * 3 + p) * 2 + a][:, q0:]
            kc = qkv[rws(q0 + 128, 128), lk] * bm[a]
            kn = qkv[rws(q0, 128), lk] * bm[a]
            st = dot(kc, q, NT) * LOGIT_SCALE - lt
            first = st[:, :256] + mbb[...]
            st = first if nq == 256 else jnp.concatenate([first, st[:, 256:]], axis=1)
            sn = dot(kn, q[:128], NT) * LOGIT_SCALE - lt[:, :128] + mbe[...]
            sc[kt, a] = st, sn
        for kt, a in blocks:
            q0, nq = 256 * kt, T - 256 * kt
            do = dm[rws(q0, nq), lq]
            vc = qkv[rws(q0 + 128, 128), lv] * bm[a]
            vn = qkv[rws(q0, 128), lv] * bm[a]
            dr = drow[a : a + 1, q0:]
            dp[kt, a] = dot(vc, do, NT) - dr, dot(vn, do[:128], NT) - dr[:, :128]
        for b in blocks:
            pt, pn = jnp.exp2(sc[b][0]), jnp.exp2(sc[b][1])
            res[b] = (
                (pt * dp[b][0]).astype(BF), (pn * dp[b][1]).astype(BF),
                pt.astype(BF), pn.astype(BF),
            )
        for kt in range(NT3):
            q0, nq = 256 * kt, T - 256 * kt
            q, do = qkv[rws(q0, nq), lq], dm[rws(q0, nq), lq]
            r0_, r1_ = res[kt, 0], res[kt, 1]
            dks[pl.ds(q0 + 128, 128), :] = heads(dot(r0_[0], q), dot(r1_[0], q))
            dks[pl.ds(q0, 128), :] = heads(dot(r0_[1], q[:128]), dot(r1_[1], q[:128]))
            qkv[rws(q0 + 128, 128), lv] = heads(dot(r0_[2], do), dot(r1_[2], do)).astype(BF)
            qkv[rws(q0, 128), lv] = heads(
                dot(r0_[3], do[:128]), dot(r1_[3], do[:128])
            ).astype(BF)
        dqs = []
        for i in range(NT3):
            kc = jnp.concatenate([qkv[rws(256 * j + 128, 128), lk] for j in range(i + 1)], axis=0)
            kn = qkv[rws(256 * i, 128), lk]
            both = []
            for a in range(2):
                ds = jnp.concatenate(
                    [
                        res[kt, a][0][:, 256 * (i - kt) : 256 * (i - kt) + 256]
                        for kt in range(i + 1)
                    ],
                    axis=0,
                )
                x = dot(ds, kc, TN)
                x = jnp.concatenate([x[:128] + dot(res[i, a][1], kn, TN), x[128:]], axis=0)
                both.append(x)
            dqs.append(heads(*both))
        for i in range(NT3):
            cos, sin = rows2(cos_r, i), rows2(sin_r, i)
            dk = dks[pl.ds(256 * i, 256), :]
            qkv[rws(256 * i, 256), lq] = (turn(dqs[i], cos, -sin) * 0.125).astype(BF)
            qkv[rws(256 * i, 256), lk] = (turn(dk, cos, -sin) * 0.125).astype(BF)
        handle_at(n, {i: ("att", i) for i in range(6)})

        @pl.when(s == 1)
        def _():
            dj = jnp.concatenate([qkv[:, lq], qkv[:, lk], qkv[:, lv]], axis=1)
            g1[:, pl.ds(mo(1536 + L * p, 128), L)] = dot(normed[...], dj, TN).astype(BF)

        for i in range(3):
            pl.when(n == 2 * i + 1)(chunks[f"q{i}"].start)
        handle_at(n, {2 * i + 1: ("q", i) for i in range(3)})
        return carry

    lax.fori_loop(0, 6, attn_bwd, 0)

    def da_other(i, carry):
        x = dot(qkv[pl.ds(mo(T + 256 * i, 128), 256), :], wq[...], NT)
        dpre[pl.ds(mo(256 * i, 128), 256), right] = x.astype(BF)
        s_da(i).start()
        return carry

    lax.fori_loop(0, NT3, da_other, 0)
    handle(("da", 0))
    cg_out = [
        local(daf.at[pl.ds(256 * i, 128)], cg_h.at[0, pl.ds(128 * i, 128)]) for i in range(NT3)
    ]

    def da_own(i, sums):
        rows = pl.ds(mo(256 * i, 128), 256)
        g = dot(qkv[rows, :], wq[...], NT)
        s_da(i).wait_recv()
        g = g + dpre[pl.ds(mo(T + 256 * i, 128), 256), right].astype(F32)
        xhat, inv = normalize(stream[rows, :].astype(F32))
        ds = daf[rows, :] + normalize_backward(g, xhat, inv, gain_a)
        m = wide(mcol[pl.ds(mo(128 * i, 128), 128), :]) > 0.5
        daf[pl.ds(mo(256 * i, 128), 128), :] = ds[128:] + jnp.where(m, 0.0, ds[:128])
        return (
            sums[0] + jnp.sum(jnp.where(m, ds[:128], 0.0), axis=0, keepdims=True),
            sums[1] + jnp.sum(g * xhat, axis=0, keepdims=True),
        )

    g_mask, g_gain_a = lax.fori_loop(0, NT3, da_own, (zrow, zrow))
    for cp in cg_out:
        cp().start()
    sbuf[0, 0:1, :] = g_mask
    sbuf[0, 1:2, :] = g_gain_a

    smalls = [
        remote(lambda k, i, n=n, dev=dev: rc(k, sbuf.at[n], srec.at[n], dev))
        for n, dev in enumerate([sib, ypeer] + peers)
    ]
    s_last = remote(
        lambda k, i: rc(k, sbuf.at[nbits + 2], srec.at[nbits + 2], sib)
    )
    row = lax.broadcasted_iota(jnp.int32, (8, D), 0)

    def small_step(n):
        smalls[n]().wait_recv()
        new = srec[n]
        if n == 0:
            new = jnp.where(row < 4, new, 0.0)
        sbuf[n + 1] = sbuf[n] + new
        if n + 1 < len(smalls):
            smalls[n + 1]().start()
        else:
            s_last().start()

    def small_rest():
        for n in range(4, len(smalls)):
            small_step(n)

    small_sum = Chunk()
    small_sum.events = [functools.partial(small_step, n) for n in range(4)] + [
        small_rest, lambda: s_last().wait_recv(),
    ]
    chunks["s"] = small_sum
    smalls[0]().start()
    handle(("da", 1))

    sent(s_dn)

    def bo_other(i, carry):
        x = dot(act[pl.ds(mo(T + 256 * i, 128), 256), :], wd[...])
        xs[pl.ds(mo(256 * i, 128), 256), :] = x.astype(BF)
        s_bo(i).start()
        return carry

    lax.fori_loop(0, NT3, bo_other, 0)
    handle(("bo", 0))
    sent(s_nm)

    def bo_own(i, carry):
        rows = pl.ds(mo(256 * i, 128), 256)
        x = aa[rows, :] + dot(act[rows, :], wd[...])
        s_bo(i).wait_recv()
        nm[rows, :] = (x + xr[rows, :].astype(F32) + bias_d).astype(BF)
        return carry

    lax.fori_loop(0, NT3, bo_own, 0)
    l_out = [
        local(
            nm.at[pl.ds(128 * r, 128)],
            out_h.at[0, pl.ds((r % 2) * L + 128 * (r // 2), 128)],
        )
        for r in range(2 * NT3)
    ]
    for cp in l_out:
        cp().start()
    handle(("bo", 1))
    handle("tail")
    for ch in chunks.values():
        ch.events[-1]()
    last = len(smalls)
    tot = sbuf[last]
    oth = srec[last]
    mh = jnp.where(f == 0, tot[0:4, 0:L], tot[0:4, L:D])
    fin[0:4, :] = mh
    for core_off, x in ((c, tot), (1 - c, oth)):
        v = jnp.where(f == 0, x[4:5, :], x[5:6, :])
        fin[pl.ds(4 + 2 * core_off, 1), :] = v[:, 0:L]
        fin[pl.ds(5 + 2 * core_off, 1), :] = v[:, L:D]
    for cp in l_out + cg_out:
        cp().wait()
    for fam, n in list(ends):
        sent(fam)


def tables(length):
    pos = np.arange(length, dtype=np.float32)
    half = HD // 2
    spacing = (10000.0 ** (-2.0 * np.arange(half, dtype=np.float64) / HD)).astype(np.float32)
    ang = (pos[:, None] * spacing[None, :]).astype(np.float64)
    cos = np.tile(np.cos(ang), (1, 4)).astype(np.float32)
    sin = np.sin(ang)
    sin = np.tile(np.concatenate([-sin, sin], axis=1), (1, 2)).astype(np.float32)
    return cos, sin


def finish_kernel(
    o1_h, od_h, fin, bo_h, cg_h,
    gq_h, go_h, gu_h, gd_h, out_h, clean_h, v_mask, v_ga, v_gm, v_bd, v_bu,
    b1, bd, fq, fo, fu, fd, bo, cg, ls,
):
    L, D, NB = 384, 768, 4
    count = [0]

    def copy(src, dst):
        k = count[0]
        count[0] += 1
        cp = pltpu.make_async_copy(src, dst, ls.at[k])
        cp.start()
        return cp

    rows = [pl.ds(L // NB * r, L // NB) for r in range(NB)]
    in1 = [copy(o1_h.at[:, rows[r]], b1.at[:, rows[r]]) for r in range(NB)]
    ind = [copy(od_h.at[core], bd.at[core]) for core in range(2)]
    through = [copy(bo_h, bo), copy(cg_h, cg)]
    outs = []
    for r in range(NB):
        in1[r].wait()
        for core in range(2):
            for h in range(2):
                fu[rows[r], 1536 * h + D * core : 1536 * h + D * core + D] = b1[
                    core, rows[r], D * h : D * h + D
                ].astype(F32)
            for p in range(3):
                for kind in range(3):
                    src = 1536 + L * p + 128 * kind
                    dst = D * kind + L * core + 128 * p
                    fq[rows[r], dst : dst + 128] = b1[core, rows[r], src : src + 128].astype(F32)
            fo[rows[r], L * core : L * core + L] = b1[
                core, rows[r], 1536 + 3 * L : 1536 + 4 * L
            ].astype(F32)
        for buf, ref in ((fu, gu_h), (fq, gq_h), (fo, go_h)):
            outs.append(copy(buf.at[rows[r]], ref.at[rows[r]]))
        if r < 2:
            through[r].wait()
            outs.append(copy((bo, cg)[r], (out_h, clean_h)[r]))
    for core in range(2):
        ind[core].wait()
        for r in range(2):
            part = slice(L * r, L * r + L)
            at = D * core + L * r
            fd[at : at + L, :] = bd[core, part, :].astype(F32)
            outs.append(copy(fd.at[pl.ds(at, L)], gd_h.at[pl.ds(at, L)]))
    v_mask[...] = fin[0, :]
    v_ga[...] = fin[1, :]
    v_gm[...] = fin[2, :]
    v_bd[...] = fin[3, :]
    for r in range(4):
        v_bu[L * r : L * r + L] = fin[4 + r, :]
    for cp in outs:
        cp.wait()


def on_device(
    nbits, clean_in, noise_bits, mask_vector, gain_attn, w_qkv, w_out, gain_mlp,
    w_up, bias_up, w_down, bias_down, out_grad,
):
    L, D, T = 384, 768, 768
    cos, sin = tables(L)
    nx = max(1, nbits - 3)
    hbm = pl.BlockSpec(memory_space=pltpu.HBM)
    vm = pl.BlockSpec(memory_space=pltpu.VMEM)
    scratch = [
        ((8, L), F32), ((2, 8, L), F32), ((8, D), F32), ((L, 128), F32),
        ((128, 256), F32), ((128, 128), F32),
        ((T, D), BF), ((2 * T, D), BF), ((D, 1152), BF), ((D, D), BF), ((D, 1536), BF),
        ((1536, D), BF), ((2 * T, D), BF),
        ((2 * T, 1152), BF), ((12, 1, T), F32), ((2 * T, D), BF), ((T, D), F32),
        ((2 * T, D), BF), ((2 * T, 1536), BF), ((2 * T, 1536), BF), ((T, D), BF),
        ((T, D), BF), ((T, D), F32), ((2 * T, D), BF), ((2 * T, L), BF), ((T, 128), F32),
        ((1536, D), BF), ((D, 3072), BF),
        ((D, D), BF), ((L, 3072), BF), ((L, D), BF), ((192, 3072), BF),
        ((192, D), BF), ((96, 3072), BF), ((96, D), BF), ((48, 3072), BF),
        ((nx, 96, D), BF) if nbits > 3 else ((1, 16, 128), BF),
        ((nx, 48, 3072), BF) if nbits > 3 else ((1, 16, 128), BF),
        ((nbits + 3, 8, D), F32), ((nbits + 3, 8, D), F32),
    ]
    block_out, clean_grad, fin, g1, gd = pl.pallas_call(
        functools.partial(layer_kernel, nbits),
        out_shape=[
            jax.ShapeDtypeStruct((1, T, D), BF),
            jax.ShapeDtypeStruct((1, L, D), F32),
            jax.ShapeDtypeStruct((8, L), F32),
            jax.ShapeDtypeStruct((2, L, 3072), BF),
            jax.ShapeDtypeStruct((2, D, D), BF),
        ],
        in_specs=[hbm] + [vm] * 8 + [hbm] * 5,
        out_specs=[hbm, hbm, vm, hbm, hbm],
        scratch_shapes=[pltpu.VMEM(s, t) for s, t in scratch]
        + [
            pltpu.SemaphoreType.DMA((N_SEND + 1 * (nbits - 3),)),
            pltpu.SemaphoreType.DMA((N_RECV + 14 * (nbits - 3),)),
            pltpu.SemaphoreType.DMA((N_LOCAL,)),
        ],
        compiler_params=pltpu.CompilerParams(
            collective_id=0, has_side_effects=True, vmem_limit_bytes=64 * 2**20
        ),
        name="layer",
    )(
        clean_in, noise_bits, mask_vector, gain_attn, gain_mlp, bias_down, bias_up, cos, sin,
        w_qkv, w_out, w_up, w_down, out_grad,
    )
    vec = jax.ShapeDtypeStruct((L,), F32)
    gq, go, gu, gdown, out, clean, v_mask, v_ga, v_gm, v_bd, v_bu = pl.pallas_call(
        finish_kernel,
        out_shape=[
            jax.ShapeDtypeStruct((L, 2304), F32),
            jax.ShapeDtypeStruct((L, D), F32),
            jax.ShapeDtypeStruct((L, 3072), F32),
            jax.ShapeDtypeStruct((1536, D), F32),
            jax.ShapeDtypeStruct((1, T, D), BF),
            jax.ShapeDtypeStruct((1, L, D), F32),
            vec, vec, vec, vec, jax.ShapeDtypeStruct((4 * L,), F32),
        ],
        in_specs=[hbm, hbm, vm, hbm, hbm],
        out_specs=[hbm] * 6 + [vm] * 5,
        scratch_shapes=[
            pltpu.VMEM((2, L, 3072), BF), pltpu.VMEM((2, D, D), BF),
            pltpu.VMEM((L, 2304), F32), pltpu.VMEM((L, D), F32),
            pltpu.VMEM((L, 3072), F32), pltpu.VMEM((1536, D), F32),
            pltpu.VMEM((1, T, D), BF), pltpu.VMEM((1, L, D), F32),
            pltpu.SemaphoreType.DMA((26,)),
        ],
        compiler_params=pltpu.CompilerParams(vmem_limit_bytes=64 * 2**20),
        name="finish",
    )(g1, gd, fin, block_out, clean_grad)
    return out, clean, v_mask, v_ga, gq, go, v_gm, gu, v_bu, gdown, v_bd


def solution(mesh):
    nbits = int(math.log2(mesh.shape["dp"])) - 1
    seq = P(("dp", "fsdp"), None, None)
    row, vec = P("fsdp", None), P("fsdp")
    in_specs = (seq, P(("dp", "fsdp"), None), vec, vec, row, row, vec, row, vec, row, vec, seq)
    out_specs = (seq, seq, vec, vec, row, row, vec, row, vec, row, vec)
    return jax.shard_map(
        functools.partial(on_device, nbits), mesh=mesh,
        in_specs=in_specs, out_specs=out_specs, check_vma=False,
    )
```

```python
import functools
import math

import jax
import jax.numpy as jnp
import numpy as np
from jax import lax
from jax.experimental import pallas as pl
from jax.experimental.pallas import tpu as pltpu
from jax.sharding import PartitionSpec as P

HD = 64
BLOCK = 16
NORM_FLOOR = 1e-05
TANH_SCALE = 0.7978845608028654
CUBIC = 0.044715
BF = jnp.bfloat16
F32 = jnp.float32
MESH = pl.DeviceIdType.MESH
LOGIT_SCALE = 0.125 * math.log2(math.e)
N_SEND, N_RECV, N_LOCAL = 102, 185, 38
NN = (((1,), (0,)), ((), ()))
NT = (((1,), (1,)), ((), ()))
TN = (((0,), (0,)), ((), ()))


ROUTES = {
    "d0": "y0Z",
    "d1": "0y12",
    "d2": "y0Z",
    "u0": "y012",
    "u1": "y0Z",
    "u2": "10y2",
    "u3": "1y02",
    "u4": "y0Z",
    "u5": "y0Z",
    "q0": "0y12",
    "q1": "y102",
    "q2": "y0Z",
    "o": "0y12",
}
SCHEDULE = {
    ("b", 1): (
        ("d0", 0),
    ),
    ("dn", 0): (
        ("d1", 0),
        ("d2", 0),
    ),
    ("dn", 1): (
        ("u2", 0),
        ("d0", 1),
        ("u0", 0),
    ),
    ("dm", 0): (
        ("u3", 0),
        ("d2", 1),
        ("u1", 0),
    ),
    ("att", 0): (
        ("u2", 1),
        ("u4", 0),
        ("u0", 1),
        ("d0", 2),
    ),
    ("q", 0): (
        ("u5", 0),
        ("u0", 2),
        ("d2", 2),
    ),
    ("att", 2): (
        ("o", 0),
        ("d1", 1),
        ("u1", 1),
    ),
    ("att", 3): (
        ("d0", 3),
        ("u0", 3),
        ("u3", 1),
        ("u4", 1),
        ("u2", 2),
    ),
    ("q", 1): (
        ("d1", 2),
    ),
    ("att", 4): (
        ("d2", 3),
        ("o", 1),
        ("u1", 2),
    ),
    ("att", 5): (
        ("q0", 0),
        ("u0", 4),
        ("u5", 1),
        ("u4", 2),
    ),
    ("q", 2): (
        ("o", 2),
        ("u2", 3),
    ),
    ("da", 0): (
        ("q1", 0),
        ("d1", 3),
        ("u0", 5),
        ("d0", 4),
        ("u3", 2),
        ("u1", 3),
    ),
    ("da", 1): (
        ("q0", 1),
        ("u5", 2),
        ("d2", 4),
        ("u4", 3),
    ),
    ("bo", 0): (
        ("o", 3),
        ("s", 0),
        ("q1", 1),
        ("u0", 6),
        ("u2", 4),
        ("q2", 0),
        ("u1", 4),
        ("d1", 4),
        ("q0", 2),
    ),
    ("bo", 1): (
        ("u3", 3),
        ("u4", 4),
        ("s", 1),
        ("u5", 3),
        ("q1", 2),
    ),
    "tail": (
        ("u2", 5),
        ("d1", 5),
        ("o", 4),
        ("q0", 3),
        ("u3", 4),
        ("q2", 1),
        ("s", 2),
        ("q1", 3),
        ("u2", 6),
        ("u5", 4),
        ("o", 5),
        ("q0", 4),
        ("q2", 2),
        ("s", 3),
        ("d1", 6),
        ("q1", 4),
        ("u3", 5),
        ("q0", 5),
        ("o", 6),
        ("q2", 3),
        ("q1", 5),
        ("s", 4),
        ("u3", 6),
        ("q0", 6),
        ("q1", 6),
        ("q2", 4),
    ),
}


def dot(a, b, dims=NN):
    return lax.dot_general(a, b, dims, preferred_element_type=F32)


def mo(x, n):
    return pl.multiple_of(x, n)


def normalize(x):
    d = x - jnp.mean(x, axis=-1, keepdims=True)
    inv = lax.rsqrt(jnp.mean(d * d, axis=-1, keepdims=True) + NORM_FLOOR)
    return d * inv, inv


def normalize_backward(g, xhat, inv, gain):
    e = g * gain
    return inv * (
        e
        - jnp.mean(e, axis=-1, keepdims=True)
        - xhat * jnp.mean(e * xhat, axis=-1, keepdims=True)
    )


def layer_kernel(
    nbits,
    clean_h, noise, v_mask, v_ga, v_gm, v_bd, v_bu, cos_r, sin_r, wq_h, wo_h, wu_h, wd_h, og_h,
    out_h, cg_h, fin, o1_h, od_h,
    small_in, small, prow, mcol, mbb, mbe,
    stream, normed, wq, wo, wu, wd, og,
    qkv, lbuf, mixed, aa, nm, act, dpre, xs, xr, daf, db, dm, dks,
    gd, g1, r0d, r01, r1d, r11, r2d, r21, r3d, r31, red, re1,
    sbuf, srec, ss, rs, ls,
):
    L = 384
    D = 768
    T = 2 * L
    NT3 = L // 128
    d = lax.axis_index("dp")
    f = lax.axis_index("fsdp")
    c = lax.rem(d, 2)
    bits = [lax.rem(lax.div(d, 2 ** (b + 1)), 2) for b in range(nbits)]
    sib = (d + 1 - 2 * c, f)
    ypeer = (d, 1 - f)
    peers = [(d + (1 - 2 * bits[b]) * 2 ** (b + 1), f) for b in range(nbits)]
    u = 2 * bits[1] + bits[0]
    send_count, recv_count, local_count = [0], [0], [0]
    ends = []

    def take_send(n):
        k = send_count[0]
        send_count[0] += n
        return k

    def take_recv(n=1):
        k = recv_count[0]
        recv_count[0] += n
        return k

    def rc(k, src, dst, dev):
        return pltpu.make_async_remote_copy(
            src_ref=src, dst_ref=dst, send_sem=ss.at[k[0]], recv_sem=rs.at[k[1]],
            device_id=dev, device_id_type=MESH,
        )

    def remote(make, n=1):
        k = (take_send(n), take_recv(n))
        fam = lambda i=0: make((k[0] + i, k[1] + i), i)
        ends.append((fam, n))
        return fam

    def sent(fam):
        for at, (other_fam, n) in enumerate(ends):
            if other_fam is fam:
                for i in range(n):
                    fam(i).wait_send()
                ends.pop(at)
                return

    def local(src, dst):
        k = local_count[0]
        local_count[0] += 1
        return lambda: pltpu.make_async_copy(src, dst, ls.at[k])

    bar = pltpu.get_barrier_semaphore()
    for dev in [sib, ypeer] + peers:
        pl.semaphore_signal(bar, inc=1, device_id=dev, device_id_type=MESH)

    l_clean = [
        local(clean_h.at[0, pl.ds(128 * i, 128)], stream.at[pl.ds(256 * i + 128, 128)])
        for i in range(NT3)
    ]
    mine = mo(f * L, 128)
    other = mo((1 - f) * L, 128)
    l_wq = [
        local(
            wq_h.at[:, pl.ds(mo(j * D + c * L, 128), L)],
            wq.at[pl.ds(mine, L), pl.ds(j * L, L)],
        )
        for j in range(3)
    ]
    l_wo = local(wo_h, wo.at[pl.ds(mine, L)])
    l_wu = [
        local(
            wu_h.at[:, pl.ds(mo(h * 1536 + c * D, 128), D)],
            wu.at[pl.ds(mine, L), pl.ds(h * D, D)],
        )
        for h in range(2)
    ]
    l_wd = local(wd_h.at[pl.ds(mo(c * D, 128), D)], wd.at[pl.ds(mo(f * D, 128), D)])
    l_og = [
        local(
            og_h.at[0, pl.ds((r % 2) * L + 128 * (r // 2), 128)],
            og.at[pl.ds(128 * r, 128)],
        )
        for r in range(2 * NT3)
    ]
    for cp in l_clean + l_wq:
        cp().start()
    for r, v in enumerate((v_mask, v_ga, v_gm, v_bd)):
        small_in[r : r + 1, :] = v[...].astype(F32).reshape(1, L)
    for r in range(4):
        small_in[4 + r : 5 + r, :] = v_bu[pl.ds(L * r, L)].astype(F32).reshape(1, L)
    small[pl.ds(f, 1)] = small_in[...][None]

    def y_wq(unit):
        rows = mo(96 * unit, 16)
        return remote(
            lambda k, j: rc(
                k,
                wq_h.at[pl.ds(rows, 96), pl.ds(mo(j * D + c * L, 128), L)],
                wq.at[pl.ds(mo(f * L + rows, 16), 96), pl.ds(j * L, L)],
                ypeer,
            ),
            3,
        )

    yw_q = y_wq(u)
    yw_q2 = y_wq(3 - u)
    y_small = remote(lambda k, i: rc(k, small_in, small.at[f], ypeer))

    def spread(buf, base, unit_rows, unit, dev):
        rows = mo(base + unit_rows * unit, 16)
        return remote(
            lambda k, i: rc(
                k, buf.at[pl.ds(rows, unit_rows)], buf.at[pl.ds(rows, unit_rows)], dev
            )
        )


    def spread_q(dev):
        rows = mo(other + 96 * u, 16)
        return remote(
            lambda k, j: rc(
                k, wq.at[pl.ds(rows, 96), pl.ds(j * L, L)],
                wq.at[pl.ds(rows, 96), pl.ds(j * L, L)], dev,
            ),
            3,
        )

    xw_q = spread_q(peers[0])
    zw_q = spread_q(peers[1])
    def half_of(i):
        if isinstance(i, int):
            return 1 - f if i == 0 else f
        return (1 - f) * (1 - i) + f * i

    def up_lanes(i):
        return pl.ds(mo(half_of(i) * D, 128), D)

    def y_wu_to(unit):
        rows = mo(96 * unit, 16)

        def make(k, i):
            h = f if i == 0 else 1 - f
            return rc(
                k,
                wu_h.at[pl.ds(rows, 96), pl.ds(mo(h * 1536 + c * D, 128), D)],
                wu.at[pl.ds(mo(f * L + rows, 16), 96), pl.ds(mo(h * D, 128), D)],
                ypeer,
            )

        return remote(make, 2)

    def spread_u(dev):
        rows = mo(other + 96 * u, 16)
        return remote(
            lambda k, i: rc(
                k, wu.at[pl.ds(rows, 96), up_lanes(i)], wu.at[pl.ds(rows, 96), up_lanes(i)], dev
            ),
            2,
        )

    yw_u = y_wu_to(u)
    yw_u2 = y_wu_to(3 - u)
    xw_u = spread_u(peers[0])
    zw_u = spread_u(peers[1])
    ux, uz = 2 * bits[1] + 1 - bits[0], 2 * (1 - bits[1]) + bits[0]
    odown = mo((1 - f) * D, 128)
    yw_d = remote(
        lambda k, i: rc(
            k,
            wd_h.at[pl.ds(mo(c * D + 192 * u + 96 * i, 16), 96)],
            wd.at[pl.ds(mo(f * D + 192 * u + 96 * i, 16), 96)],
            ypeer,
        ),
        2,
    )

    def spread_d(dev):
        def make(k, i):
            rows = pl.ds(mo(odown + 192 * u + 96 * i, 16), 96)
            return rc(k, wd.at[rows], wd.at[rows], dev)

        return remote(make, 2)

    xw_d = spread_d(peers[0])
    zw_d = spread_d(peers[1])
    xw_d2 = spread(wd, odown, 96, 2 * uz, peers[0])
    zw_d2 = spread(wd, odown, 96, 2 * ux + 1, peers[1])
    yw_o = remote(
        lambda k, i: rc(
            k,
            wo_h.at[pl.ds(mo(192 * c + 96 * bits[0], 16), 96)],
            wo.at[pl.ds(mo(f * L + 192 * c + 96 * bits[0], 16), 96)],
            ypeer,
        )
    )
    xw_o = spread(wo, mo(other + 192 * c, 16), 96, bits[0], peers[0])
    sw_o = spread(wo, other, 192, c, sib)

    s_norm = remote(
        lambda k, i: rc(
            k, normed.at[pl.ds(mo(256 * i, 16), 256)],
            normed.at[pl.ds(mo(T + 256 * i, 16), 256)], sib,
        ),
        NT3,
    )
    s_og = remote(lambda k, i: rc(k, og.at[pl.ds(0, T)], og.at[pl.ds(T, T)], sib))

    def mixed_copy(k, i):
        s = 1 - i // 3 if isinstance(i, int) else 1 - lax.div(i, 3)
        p = i % 3 if isinstance(i, int) else lax.rem(i, 3)
        lanes = pl.ds(mo(c * L + 128 * p, 128), 128)
        return rc(
            k, mixed.at[pl.ds(mo(s * T, 16), T), lanes],
            mixed.at[pl.ds(mo((1 - s) * T, 16), T), lanes], sib,
        )

    s_mix = remote(mixed_copy, 6)

    def rows_copy(buf, src0, dst, dst0):
        return remote(
            lambda k, i: rc(
                k, buf.at[pl.ds(mo(src0 + 256 * i, 16), 256)],
                dst.at[pl.ds(mo(dst0 + 256 * i, 16), 256)], sib,
            ),
            NT3,
        )

    s_nm = rows_copy(nm, 0, nm, T)
    s_dn = rows_copy(xs, 0, xr, 0)
    s_db = rows_copy(db, 0, db, T)
    s_bo = rows_copy(xs, 0, xr, 0)
    right = pl.ds(D, D)
    s_da = remote(
        lambda k, i: rc(
            k, dpre.at[pl.ds(mo(256 * i, 16), 256), right],
            dpre.at[pl.ds(mo(T + 256 * i, 16), 256), right], sib,
        ),
        NT3,
    )

    class Chunk:
        pass

    chunks = {}

    def make_chunk(name, g, gbase, nr, l0, nl, recv, rbase, oref, orow, blk):
        ch = Chunk()
        lanes = pl.ds(l0, nl)
        route = ROUTES[name]

        def greg(h, off, n):
            return g.at[pl.ds(mo(gbase(h) + off, 16), n), lanes]

        def rreg(stage, at, n):
            return recv[stage].at[pl.ds((rbase >> (0, 1, 1, 2)[stage]) + at, n), lanes]

        def oreg(core, off, n):
            return oref.at[core, pl.ds(mo(orow + off, 16), n), lanes]

        def at_role(role, fn):
            if role is None:
                fn()
            else:
                pl.when(role)(fn)

        class Stage:
            def __init__(self, copies, sums=(), sender=None, receiver=None):
                self.copies, self.sums = copies, sums
                self.sender, self.receiver = sender, receiver

            def start(self):
                at_role(self.sender, lambda: [cp().start() for cp in self.copies] and None)

            def sent(self):
                at_role(self.sender, lambda: [cp().wait_send() for cp in self.copies] and None)

            def arrive(self):
                def go():
                    for cp in self.copies:
                        cp().wait_recv()
                    for h, at, m, parts in self.sums:
                        add(h, at, m, parts)

                at_role(self.receiver, go)

        k_send = take_send(3)

        def copy(i, src, dst, dev):
            k = take_recv()
            return lambda: pltpu.make_async_remote_copy(
                src_ref=src(), dst_ref=dst(), send_sem=ss.at[k_send + i], recv_sem=rs.at[k],
                device_id=dev, device_id_type=MESH,
            )

        def add(h, off, n, parts):
            gr = greg(h, off, n)
            step = min(blk, n)

            def body(i, carry):
                sl = pl.ds(mo(i * step, 16), step)
                x = gr[sl, :].astype(F32)
                for stage, at in parts:
                    x = x + rreg(stage, at, n)[sl, :].astype(F32)
                gr[sl, :] = x.astype(BF)
                return carry

            lax.fori_loop(0, n // step, body, 0)

        sums, back = [], []
        holder = None
        off, n, both, stage = 0, nr, True, 0

        def give_back(at, m, devs, **roles):
            back.append(lambda src: Stage(
                [
                    copy(i, lambda: src(at, m), lambda: oreg(c, at, m), dev)
                    for i, dev in enumerate(devs)
                ],
                **roles,
            ))

        for step in route:
            if step == "y":
                sums.append(Stage(
                    [copy(
                        0, lambda off=off, n=n: greg(1 - f, off, n),
                        lambda stage=stage, n=n: rreg(stage, 0, n), ypeer,
                    )],
                    [(f, off, n, [(stage, 0)])],
                ))
                both = False
                stage += 1
            elif step == "Z":
                m4 = n // 4
                out, parts, devs = [], [], []
                where = [(stage, 0), (stage, m4), (stage + 1, 0)]
                mine_off = off + (2 * bits[1] + bits[2]) * m4
                for i, (x1, x2) in enumerate(((0, 1), (1, 0), (1, 1))):
                    b1 = 1 - bits[1] if x1 else bits[1]
                    b2 = 1 - bits[2] if x2 else bits[2]
                    dev = (d + (b1 - bits[1]) * 4 + (b2 - bits[2]) * 8, f)
                    to = off + (2 * b1 + b2) * m4
                    st, at = where[i]
                    out.append(copy(
                        i, lambda to=to, m4=m4: greg(f, to, m4),
                        lambda st=st, at=at, m4=m4: rreg(st, at, m4), dev,
                    ))
                    devs.append(dev)
                    parts.append((st, at))
                sums.append(Stage(out, [(f, mine_off, m4, parts)]))
                give_back(mine_off, m4, devs)
                off, n, stage = mine_off, m4, stage + 2
            elif step == "E":
                m2 = n // 2
                inner = bits[1] + bits[2] - 2 * bits[1] * bits[2] == 1
                outer = bits[1] + bits[2] - 2 * bits[1] * bits[2] == 0
                middle = (d + (1 - 2 * bits[1]) * 4 + (1 - 2 * bits[2]) * 8, f)
                keep, give = off + bits[2] * m2, off + (1 - bits[2]) * m2
                sums.append(Stage(
                    [copy(
                        0, lambda off=off, n=n: greg(f, off, n),
                        lambda stage=stage, n=n: rreg(stage, 0, n), peers[1],
                    )],
                    [(f, off, n, [(stage, 0)])], sender=outer, receiver=inner,
                ))
                sums.append(Stage(
                    [copy(
                        0, lambda give=give, m2=m2: greg(f, give, m2),
                        lambda stage=stage, m2=m2: rreg(stage + 1, 0, m2), middle,
                    )],
                    [(f, keep, m2, [(stage + 1, 0)])], sender=inner, receiver=inner,
                ))
                give_back(off, n, [peers[1]], sender=inner, receiver=outer)
                give_back(keep, m2, [middle], sender=inner, receiver=inner)
                holder = inner
                off, n, stage = keep, m2, stage + 2
            else:
                j = int(step)
                m2 = n // 2
                give, keep = off + (1 - bits[j]) * m2, off + bits[j] * m2
                owners = [0, 1] if both else [f]
                sums.append(Stage(
                    [
                        copy(
                            i, lambda h=h, give=give, m2=m2: greg(h, give, m2),
                            lambda stage=stage, i=i, m2=m2: rreg(stage, i * m2, m2), peers[j],
                        )
                        for i, h in enumerate(owners)
                    ],
                    [(h, keep, m2, [(stage, i * m2)]) for i, h in enumerate(owners)],
                ))
                give_back(keep, m2, [peers[j]])
                off, n, stage = keep, m2, stage + 1
        extra = [
            copy(
                0, lambda off=off, n=n: greg(f, off, n),
                lambda j=j, n=n: recv[4].at[j - 3, pl.ds((rbase >> 2), n), lanes], peers[j],
            )
            for j in range(3, nbits)
        ]
        own = local(greg(f, off, n), oreg(c, off, n))
        gathers = [
            make((lambda at, m: greg(f, at, m)) if i == 0 else (lambda at, m: oreg(c, at, m)))
            for i, make in enumerate(reversed(back))
        ]
        gathers.append(Stage([copy(0, lambda: oreg(c, 0, nr), lambda: oreg(c, 0, nr), sib)]))

        def finished():
            for m, cp in enumerate(extra):
                cp().start()
                cp().wait_send()
                cp().wait_recv()
                gr = greg(f, off, n)
                gr[...] = (
                    gr[...].astype(F32)
                    + recv[4][m, pl.ds((rbase >> 2), n), lanes].astype(F32)
                ).astype(BF)
            own().start()

        def reduce_event(i):
            sums[i].arrive()
            sums[i].sent()
            if i + 1 < len(sums):
                sums[i + 1].start()
                return
            at_role(holder, finished)
            gathers[0].start()

        def gather_event(i):
            gathers[i].arrive()
            if i == 0:
                at_role(holder, lambda: own().wait())
            gathers[i].sent()
            if i + 1 < len(gathers):
                gathers[i + 1].start()

        ch.start = sums[0].start
        ch.events = [functools.partial(reduce_event, i) for i in range(len(sums))] + [
            functools.partial(gather_event, i) for i in range(len(gathers))
        ]
        chunks[name] = ch

    recv_d = (r0d, r1d, r2d, r3d, red)
    recv_1 = (r01, r11, r21, r31, re1)
    for k in range(3):
        make_chunk(
            f"d{k}", gd, lambda h, k=k: h * D + 256 * k, 256, 0, D, recv_d, 256 * k,
            od_h, 256 * k, 32,
        )
    for t in range(6):
        make_chunk(f"u{t}", g1, lambda h: h * L, L, 256 * t, 256, recv_1, 0, o1_h, 0, 48)
    for p in range(3):
        make_chunk(f"q{p}", g1, lambda h: h * L, L, 1536 + L * p, L, recv_1, 0, o1_h, 0, 48)
    make_chunk("o", g1, lambda h: h * L, L, 1536 + 3 * L, L, recv_1, 0, o1_h, 0, 48)

    def handle(key):
        for name, stage in SCHEDULE.get(key, ()):
            chunks[name].events[stage]()

    def handle_at(idx, keys):
        for i, key in keys.items():
            if SCHEDULE.get(key):
                pl.when(idx == i)(lambda key=key: handle(key))

    pl.semaphore_wait(bar, 2 + nbits)
    y_small().start()
    for j in range(3):
        yw_q(j).start()
    for j in range(3):
        yw_q2(j).start()
    yw_o().start()
    for i in range(2):
        yw_u(i).start()
        yw_u2(i).start()
    for i in range(2):
        yw_d(i).start()
    for cp in l_og + l_wu + [l_wo, l_wd]:
        cp().start()

    lane = lax.broadcasted_iota(jnp.int32, (1, 128), 1)
    low_half = lane < HD
    rot_low = lax.rem(lane, HD) < HD // 2
    bm = [jnp.where(low_half, 1.0, 0.0).astype(BF), jnp.where(low_half, 0.0, 1.0).astype(BF)]
    ir = lax.div(lax.broadcasted_iota(jnp.int32, (128, 128), 0), BLOCK)
    ic = lax.div(lax.broadcasted_iota(jnp.int32, (128, 128), 1), BLOCK)
    neg = -1e30
    mbb[:, 0:128] = jnp.where(ir < ic, 0.0, neg)
    mbb[:, 128:256] = jnp.where(ir <= ic, 0.0, neg)
    mbe[...] = jnp.where(ir == ic, 0.0, neg)
    nf = noise[...].astype(F32)
    for i in range(NT3):
        mcol[128 * i : 128 * i + 128, :] = jnp.broadcast_to(
            nf[:, 128 * i : 128 * i + 128], (128, 128)
        ).T
    sbuf[0] = jnp.zeros((8, D), F32)

    y_small().wait_recv()
    prow[:, 0:L] = small[0]
    prow[:, L:D] = small[1]
    mvec = prow[0:1, :]
    gain_a = prow[1:2, :]
    gain_m = prow[2:3, :]
    bias_d = prow[3:4, :]

    def wide(m):
        return jnp.concatenate([m] * (D // 128), axis=1)

    for i in range(NT3):
        l_clean[i]().wait()

    def attn_norm(i, carry):
        n0 = mo(256 * i, 128)
        x = stream[pl.ds(n0 + 128, 128), :].astype(F32)
        m = wide(mcol[pl.ds(mo(128 * i, 128), 128), :])
        y = jnp.where(m > 0.5, mvec, x)
        stream[pl.ds(n0, 128), :] = y.astype(BF)
        normed[pl.ds(n0, 128), :] = (normalize(y)[0] * gain_a).astype(BF)
        normed[pl.ds(n0 + 128, 128), :] = (normalize(x)[0] * gain_a).astype(BF)
        s_norm(i).start()
        return carry

    lax.fori_loop(0, NT3, attn_norm, 0)

    for j in range(3):
        yw_q(j).wait_recv()
        xw_q(j).start()
        zw_q(j).start()
    for i in range(NT3):
        s_norm(i).wait_recv()
    for cp in l_og:
        cp().wait()
    s_og().start()
    for j in range(3):
        l_wq[j]().wait()
        yw_q2(j).wait_recv()
        xw_q(j).wait_recv()
        zw_q(j).wait_recv()

    def turn(x, cos, sin):
        return x * cos + jnp.where(rot_low, pltpu.roll(x, 96, 1), pltpu.roll(x, 32, 1)) * sin

    def rows2(tab, i):
        t = tab[pl.ds(mo(128 * i, 128), 128), :]
        return jnp.concatenate([t, t], axis=0)

    def qkv_rows(r, carry):
        rows = pl.ds(mo(256 * r, 128), 256)
        joined = dot(normed[rows, :], wq[...])
        i = lax.rem(r, NT3)
        cos, sin = rows2(cos_r, i), rows2(sin_r, i)
        for p in range(6):
            x = joined[:, 128 * p : 128 * p + 128]
            qkv[rows, 128 * p : 128 * p + 128] = turn(x, cos, sin).astype(BF)
        qkv[rows, 2 * L : 3 * L] = joined[:, 2 * L : 3 * L].astype(BF)
        return carry

    lax.fori_loop(0, 2 * NT3, qkv_rows, 0)

    def run_at(idx, table):
        for k, fns in table.items():
            def go(fns=fns):
                for fn in fns:
                    fn()
            pl.when(idx == k)(go)

    def w_o_1():
        l_wo().wait()
        yw_o().wait_recv()
        xw_o().start()

    def w_o_2():
        xw_o().wait_recv()
        sw_o().start()

    def w_u(i):
        yw_u(i).wait_recv()
        xw_u(i).start()
        zw_u(i).start()

    def w_u_end(i):
        yw_u2(i).wait_recv()
        xw_u(i).wait_recv()
        zw_u(i).wait_recv()

    def w_d(i):
        yw_d(i).wait_recv()
        xw_d(i).start()
        zw_d(i).start()

    fwd_events = {0: [w_o_1], 2: [lambda: w_u(0)], 4: [w_o_2]}

    def attn_fwd(n, carry):
        s, p = 1 - lax.div(n, 3), lax.rem(n, 3)
        r0 = s * T
        lq = pl.ds(mo(128 * p, 128), 128)
        lk = pl.ds(mo(L + 128 * p, 128), 128)
        lv = pl.ds(mo(2 * L + 128 * p, 128), 128)

        def rws(a, m):
            return pl.ds(mo(r0 + a, 128), m)

        kcl = [qkv[rws(256 * j + 128, 128), lk] for j in range(NT3)]
        vcl = [qkv[rws(256 * j + 128, 128), lv] for j in range(NT3)]
        blocks = [(i, a) for i in range(NT3) for a in range(2)]
        sc, pr, mixes = {}, {}, {}
        for i, a in blocks:
            q = qkv[rws(256 * i, 256), lq]
            kc = jnp.concatenate(kcl[: i + 1], axis=0) * bm[a]
            st = dot(kc, q, NT) * LOGIT_SCALE
            kn = qkv[rws(256 * i, 128), lk] * bm[a]
            sn = dot(kn, q[:128], NT) * LOGIT_SCALE + mbe[...]
            last = st[128 * i :] + mbb[...]
            st = last if i == 0 else jnp.concatenate([st[: 128 * i], last], axis=0)
            sc[i, a] = st, sn
        for i, a in blocks:
            st, sn = sc[i, a]
            m1 = jnp.max(st, axis=0, keepdims=True)
            mn = jnp.maximum(m1[:, :128], jnp.max(sn, axis=0, keepdims=True))
            m = jnp.concatenate([mn, m1[:, 128:]], axis=1)
            pt, pn = jnp.exp2(st - m), jnp.exp2(sn - mn)
            tot = jnp.sum(pt, axis=0, keepdims=True)
            totn = tot[:, :128] + jnp.sum(pn, axis=0, keepdims=True)
            tot = jnp.concatenate([totn, tot[:, 128:]], axis=1)
            lbuf[(s * 3 + p) * 2 + a, :, 256 * i : 256 * i + 256] = m + jnp.log2(tot)
            pr[i, a] = pt.astype(BF), pn.astype(BF)
        for i, a in blocks:
            vc = jnp.concatenate(vcl[: i + 1], axis=0) * bm[a] + bm[1 - a]
            vn = qkv[rws(256 * i, 128), lv] * bm[a] + bm[1 - a]
            o = dot(pr[i, a][0], vc, TN)
            mixes[i, a] = jnp.concatenate([o[:128] + dot(pr[i, a][1], vn, TN), o[128:]], axis=0)
        for i in range(NT3):
            o0, o1 = mixes[i, 0], mixes[i, 1]
            sums = pltpu.roll(jnp.where(low_half, o1, o0), HD, 1)
            mixed[rws(256 * i, 256), pl.ds(mo(c * L + 128 * p, 128), 128)] = (
                jnp.where(low_half, o0, o1) * (1.0 / sums)
            ).astype(BF)
        s_mix(n).start()
        run_at(n, fwd_events)
        return carry

    lax.fori_loop(0, 6, attn_fwd, 0)

    sw_o().wait_recv()
    for n in range(3):
        s_mix(n).wait_recv()

    def out_proj(i, carry):
        rows = pl.ds(mo(256 * i, 128), 256)
        x = stream[rows, :].astype(F32) + dot(mixed[rows, :], wo[...])
        aa[rows, :] = x
        nm[rows, :] = (normalize(x)[0] * gain_m).astype(BF)
        s_nm(i).start()
        return carry

    lax.fori_loop(0, NT3, out_proj, 0)
    for h in range(2):
        l_wu[h]().wait()
    w_u_end(0)
    w_u(1)

    for n in range(2):
        h = half_of(n)
        lanes = up_lanes(n)
        if n == 1:
            w_u_end(1)
            w_d(0)
        bu = jnp.concatenate(
            [small[h, pl.ds(4 + 2 * c + r, 1), :] for r in range(2)], axis=1
        )

        def rows_a(r, carry, n=n, lanes=lanes, bu=bu):
            if n == 0:
                @pl.when(r == 2)
                def _():
                    for i in range(NT3):
                        s_nm(i).wait_recv()

            rows = pl.ds(mo(L * r, 128), L)
            pre = dot(nm[rows, :], wu[:, lanes]) + bu
            sq = pre * pre
            half = 0.5 + 0.5 * jnp.tanh(pre * (TANH_SCALE + TANH_SCALE * CUBIC * sq))
            a = pre * half
            act[rows, lanes] = a.astype(BF)
            slope = half + 2.0 * a * (1.0 - half) * (
                TANH_SCALE + 3.0 * CUBIC * TANH_SCALE * sq
            )
            dpre[rows, lanes] = slope.astype(BF)
            return carry

        lax.fori_loop(0, 4, rows_a, 0)
        if n == 0:
            s_og().wait_recv()
        else:
            w_d(1)

        def down_grad(k, carry, n=n, h=h):
            at = mo(h * D + 256 * k, 128)
            gd[pl.ds(at, 256), :] = dot(act[:, pl.ds(at, 256)], og[...], TN).astype(BF)
            for i in range(3):
                if n == 0 and ROUTES[f"d{i}"][0] == "y":
                    pl.when(k == i)(chunks[f"d{i}"].start)
            handle_at(k, {i: ("a", n, i) for i in range(3)})
            return carry

        handle(("a", n))
        lax.fori_loop(0, 3, down_grad, 0)
    zw_d(0).wait_recv()
    xw_d2().start()
    for i in range(3):
        if ROUTES[f"d{i}"][0] != "y":
            chunks[f"d{i}"].start()
    l_wd().wait()

    for n in range(2):
        h = half_of(1 - n)
        lanes = up_lanes(1 - n)

        def rows_b(r, tot, lanes=lanes):
            rows = pl.ds(mo(L * r, 128), L)
            g = dot(og[rows, :], wd[lanes, :], NT) * dpre[rows, lanes].astype(F32)
            dpre[rows, lanes] = g.astype(BF)
            return tot + jnp.sum(g, axis=0, keepdims=True)

        if n == 1:
            xw_d(0).wait_recv()
            zw_d(1).wait_recv()
            xw_d2().wait_recv()
            zw_d2().wait_recv()
        sbuf[0, pl.ds(4 + h, 1), :] = lax.fori_loop(0, 4, rows_b, jnp.zeros((1, D), F32))
        if n == 0:
            xw_d(1).wait_recv()
            zw_d2().start()
        handle(("b", n))
    for n in range(2):
        g1[:, n * D : n * D + D] = dot(nm[...], dpre[:, n * D : n * D + D], TN).astype(BF)
        for t in range(3 * n, 3 * n + 3):
            chunks[f"u{t}"].start()
        handle(("u", n))

    def dn_other(i, carry):
        x = dot(dpre[pl.ds(mo(T + 256 * i, 128), 256), :], wu[...], NT)
        xs[pl.ds(mo(256 * i, 128), 256), :] = x.astype(BF)
        s_dn(i).start()
        return carry

    lax.fori_loop(0, NT3, dn_other, 0)
    handle(("dn", 0))

    def dn_own(i, sums):
        rows = pl.ds(mo(256 * i, 128), 256)
        g = dot(dpre[rows, :], wu[...], NT)
        s_dn(i).wait_recv()
        g = g + xr[rows, :].astype(F32)
        xhat, inv = normalize(aa[rows, :])
        ograd = og[rows, :].astype(F32)
        after = ograd + normalize_backward(g, xhat, inv, gain_m)
        daf[rows, :] = after
        db[rows, :] = after.astype(BF)
        s_db(i).start()
        return (
            sums[0] + jnp.sum(g * xhat, axis=0, keepdims=True),
            sums[1] + jnp.sum(ograd, axis=0, keepdims=True),
        )

    zrow = jnp.zeros((1, D), F32)
    g_gain_m, g_bias_d = lax.fori_loop(0, NT3, dn_own, (zrow, zrow))
    sbuf[0, 2:3, :] = g_gain_m
    sbuf[0, 3:4, :] = g_bias_d
    handle(("dn", 1))

    wo_rows = pl.ds(mo(c * L, 128), L)
    dm[0:T, :] = dot(db[0:T, :], wo[wo_rows, :], NT).astype(BF)
    for i in range(NT3):
        s_db(i).wait_recv()
    dm[T : 2 * T, :] = dot(db[T : 2 * T, :], wo[wo_rows, :], NT).astype(BF)
    for n in range(3, 6):
        s_mix(n).wait_recv()
    g1[:, 1536 + 3 * L : 1536 + 4 * L] = dot(mixed[...], db[:, wo_rows], TN).astype(BF)
    chunks["o"].start()
    handle(("dm", 0))

    pick_lane = lax.rem(lax.broadcasted_iota(jnp.int32, (8, 256), 1), 128)
    pick_row = lax.broadcasted_iota(jnp.int32, (8, 256), 0)
    pick = jnp.where(pick_row == lax.div(pick_lane, HD), 1.0, 0.0).astype(BF)

    def attn_bwd(n, carry):
        s, p = lax.rem(n, 2), lax.div(n, 2)
        r0 = s * T
        lq = pl.ds(mo(128 * p, 128), 128)
        lk = pl.ds(mo(L + 128 * p, 128), 128)
        lv = pl.ds(mo(2 * L + 128 * p, 128), 128)

        def rws(a, m):
            return pl.ds(mo(r0 + a, 128), m)

        prod = dm[rws(0, T), lq].astype(F32) * mixed[
            rws(0, T), pl.ds(mo(c * L + 128 * p, 128), 128)
        ].astype(F32)
        hi = prod.astype(BF)
        lo = (prod - hi.astype(F32)).astype(BF)
        drow = dot(pick, jnp.concatenate([hi, lo], axis=1), NT)

        def heads(x, y):
            return jnp.where(low_half, x, y)

        blocks = [(kt, a) for kt in range(NT3) for a in range(2)]
        sc, dp, res = {}, {}, {}
        for kt, a in blocks:
            q0, nq = 256 * kt, T - 256 * kt
            q = qkv[rws(q0, nq), lq]
            lt = lbuf[(s * 3 + p) * 2 + a][:, q0:]
            kc = qkv[rws(q0 + 128, 128), lk] * bm[a]
            kn = qkv[rws(q0, 128), lk] * bm[a]
            st = dot(kc, q, NT) * LOGIT_SCALE - lt
            first = st[:, :256] + mbb[...]
            st = first if nq == 256 else jnp.concatenate([first, st[:, 256:]], axis=1)
            sn = dot(kn, q[:128], NT) * LOGIT_SCALE - lt[:, :128] + mbe[...]
            sc[kt, a] = st, sn
        for kt, a in blocks:
            q0, nq = 256 * kt, T - 256 * kt
            do = dm[rws(q0, nq), lq]
            vc = qkv[rws(q0 + 128, 128), lv] * bm[a]
            vn = qkv[rws(q0, 128), lv] * bm[a]
            dr = drow[a : a + 1, q0:]
            dp[kt, a] = dot(vc, do, NT) - dr, dot(vn, do[:128], NT) - dr[:, :128]
        for b in blocks:
            pt, pn = jnp.exp2(sc[b][0]), jnp.exp2(sc[b][1])
            res[b] = (
                (pt * dp[b][0]).astype(BF), (pn * dp[b][1]).astype(BF),
                pt.astype(BF), pn.astype(BF),
            )
        for kt in range(NT3):
            q0, nq = 256 * kt, T - 256 * kt
            q, do = qkv[rws(q0, nq), lq], dm[rws(q0, nq), lq]
            r0_, r1_ = res[kt, 0], res[kt, 1]
            dks[pl.ds(q0 + 128, 128), :] = heads(dot(r0_[0], q), dot(r1_[0], q))
            dks[pl.ds(q0, 128), :] = heads(dot(r0_[1], q[:128]), dot(r1_[1], q[:128]))
            qkv[rws(q0 + 128, 128), lv] = heads(dot(r0_[2], do), dot(r1_[2], do)).astype(BF)
            qkv[rws(q0, 128), lv] = heads(
                dot(r0_[3], do[:128]), dot(r1_[3], do[:128])
            ).astype(BF)
        dqs = []
        for i in range(NT3):
            kc = jnp.concatenate([qkv[rws(256 * j + 128, 128), lk] for j in range(i + 1)], axis=0)
            kn = qkv[rws(256 * i, 128), lk]
            both = []
            for a in range(2):
                ds = jnp.concatenate(
                    [
                        res[kt, a][0][:, 256 * (i - kt) : 256 * (i - kt) + 256]
                        for kt in range(i + 1)
                    ],
                    axis=0,
                )
                x = dot(ds, kc, TN)
                x = jnp.concatenate([x[:128] + dot(res[i, a][1], kn, TN), x[128:]], axis=0)
                both.append(x)
            dqs.append(heads(*both))
        for i in range(NT3):
            cos, sin = rows2(cos_r, i), rows2(sin_r, i)
            dk = dks[pl.ds(256 * i, 256), :]
            qkv[rws(256 * i, 256), lq] = (turn(dqs[i], cos, -sin) * 0.125).astype(BF)
            qkv[rws(256 * i, 256), lk] = (turn(dk, cos, -sin) * 0.125).astype(BF)
        handle_at(n, {i: ("att", i) for i in range(6)})

        @pl.when(s == 1)
        def _():
            dj = jnp.concatenate([qkv[:, lq], qkv[:, lk], qkv[:, lv]], axis=1)
            g1[:, pl.ds(mo(1536 + L * p, 128), L)] = dot(normed[...], dj, TN).astype(BF)

        for i in range(3):
            pl.when(n == 2 * i + 1)(chunks[f"q{i}"].start)
        handle_at(n, {2 * i + 1: ("q", i) for i in range(3)})
        return carry

    lax.fori_loop(0, 6, attn_bwd, 0)

    def da_other(i, carry):
        x = dot(qkv[pl.ds(mo(T + 256 * i, 128), 256), :], wq[...], NT)
        dpre[pl.ds(mo(256 * i, 128), 256), right] = x.astype(BF)
        s_da(i).start()
        return carry

    lax.fori_loop(0, NT3, da_other, 0)
    handle(("da", 0))
    cg_out = [
        local(daf.at[pl.ds(256 * i, 128)], cg_h.at[0, pl.ds(128 * i, 128)]) for i in range(NT3)
    ]

    def da_own(i, sums):
        rows = pl.ds(mo(256 * i, 128), 256)
        g = dot(qkv[rows, :], wq[...], NT)
        s_da(i).wait_recv()
        g = g + dpre[pl.ds(mo(T + 256 * i, 128), 256), right].astype(F32)
        xhat, inv = normalize(stream[rows, :].astype(F32))
        ds = daf[rows, :] + normalize_backward(g, xhat, inv, gain_a)
        m = wide(mcol[pl.ds(mo(128 * i, 128), 128), :]) > 0.5
        daf[pl.ds(mo(256 * i, 128), 128), :] = ds[128:] + jnp.where(m, 0.0, ds[:128])
        return (
            sums[0] + jnp.sum(jnp.where(m, ds[:128], 0.0), axis=0, keepdims=True),
            sums[1] + jnp.sum(g * xhat, axis=0, keepdims=True),
        )

    g_mask, g_gain_a = lax.fori_loop(0, NT3, da_own, (zrow, zrow))
    for cp in cg_out:
        cp().start()
    sbuf[0, 0:1, :] = g_mask
    sbuf[0, 1:2, :] = g_gain_a

    smalls = [
        remote(lambda k, i, n=n, dev=dev: rc(k, sbuf.at[n], srec.at[n], dev))
        for n, dev in enumerate([sib, ypeer] + peers)
    ]
    s_last = remote(
        lambda k, i: rc(k, sbuf.at[nbits + 2], srec.at[nbits + 2], sib)
    )
    row = lax.broadcasted_iota(jnp.int32, (8, D), 0)

    def small_step(n):
        smalls[n]().wait_recv()
        new = srec[n]
        if n == 0:
            new = jnp.where(row < 4, new, 0.0)
        sbuf[n + 1] = sbuf[n] + new
        if n + 1 < len(smalls):
            smalls[n + 1]().start()
        else:
            s_last().start()

    def small_rest():
        for n in range(4, len(smalls)):
            small_step(n)

    small_sum = Chunk()
    small_sum.events = [functools.partial(small_step, n) for n in range(4)] + [
        small_rest, lambda: s_last().wait_recv(),
    ]
    chunks["s"] = small_sum
    smalls[0]().start()
    handle(("da", 1))

    sent(s_dn)

    def bo_other(i, carry):
        x = dot(act[pl.ds(mo(T + 256 * i, 128), 256), :], wd[...])
        xs[pl.ds(mo(256 * i, 128), 256), :] = x.astype(BF)
        s_bo(i).start()
        return carry

    lax.fori_loop(0, NT3, bo_other, 0)
    handle(("bo", 0))
    sent(s_nm)

    def bo_own(i, carry):
        rows = pl.ds(mo(256 * i, 128), 256)
        x = aa[rows, :] + dot(act[rows, :], wd[...])
        s_bo(i).wait_recv()
        nm[rows, :] = (x + xr[rows, :].astype(F32) + bias_d).astype(BF)
        return carry

    lax.fori_loop(0, NT3, bo_own, 0)
    l_out = [
        local(
            nm.at[pl.ds(128 * r, 128)],
            out_h.at[0, pl.ds((r % 2) * L + 128 * (r // 2), 128)],
        )
        for r in range(2 * NT3)
    ]
    for cp in l_out:
        cp().start()
    handle(("bo", 1))
    handle("tail")
    for ch in chunks.values():
        ch.events[-1]()
    last = len(smalls)
    tot = sbuf[last]
    oth = srec[last]
    mh = jnp.where(f == 0, tot[0:4, 0:L], tot[0:4, L:D])
    fin[0:4, :] = mh
    for core_off, x in ((c, tot), (1 - c, oth)):
        v = jnp.where(f == 0, x[4:5, :], x[5:6, :])
        fin[pl.ds(4 + 2 * core_off, 1), :] = v[:, 0:L]
        fin[pl.ds(5 + 2 * core_off, 1), :] = v[:, L:D]
    for cp in l_out + cg_out:
        cp().wait()
    for fam, n in list(ends):
        sent(fam)


def tables(length):
    pos = np.arange(length, dtype=np.float32)
    half = HD // 2
    spacing = (10000.0 ** (-2.0 * np.arange(half, dtype=np.float64) / HD)).astype(np.float32)
    ang = (pos[:, None] * spacing[None, :]).astype(np.float64)
    cos = np.tile(np.cos(ang), (1, 4)).astype(np.float32)
    sin = np.sin(ang)
    sin = np.tile(np.concatenate([-sin, sin], axis=1), (1, 2)).astype(np.float32)
    return cos, sin


def finish_kernel(
    o1_h, od_h, fin, bo_h, cg_h,
    gq_h, go_h, gu_h, gd_h, out_h, clean_h, v_mask, v_ga, v_gm, v_bd, v_bu,
    b1, bd, fq, fo, fu, fd, bo, cg, ls,
):
    L, D, NB = 384, 768, 8
    count = [0]

    def copy(src, dst):
        k = count[0]
        count[0] += 1
        cp = pltpu.make_async_copy(src, dst, ls.at[k])
        cp.start()
        return cp

    rows = [pl.ds(L // NB * r, L // NB) for r in range(NB)]
    in1 = [copy(o1_h.at[:, rows[r]], b1.at[:, rows[r]]) for r in range(NB)]
    ind = [copy(od_h.at[core], bd.at[core]) for core in range(2)]
    through = [copy(bo_h, bo), copy(cg_h, cg)]
    outs = []
    for r in range(NB):
        in1[r].wait()
        for core in range(2):
            for h in range(2):
                fu[rows[r], 1536 * h + D * core : 1536 * h + D * core + D] = b1[
                    core, rows[r], D * h : D * h + D
                ].astype(F32)
            for p in range(3):
                for kind in range(3):
                    src = 1536 + L * p + 128 * kind
                    dst = D * kind + L * core + 128 * p
                    fq[rows[r], dst : dst + 128] = b1[core, rows[r], src : src + 128].astype(F32)
            fo[rows[r], L * core : L * core + L] = b1[
                core, rows[r], 1536 + 3 * L : 1536 + 4 * L
            ].astype(F32)
        for buf, ref in ((fu, gu_h), (fq, gq_h), (fo, go_h)):
            outs.append(copy(buf.at[rows[r]], ref.at[rows[r]]))
        if r < 2:
            through[r].wait()
            outs.append(copy((bo, cg)[r], (out_h, clean_h)[r]))
    for core in range(2):
        ind[core].wait()
        for r in range(2):
            part = slice(L * r, L * r + L)
            at = D * core + L * r
            fd[at : at + L, :] = bd[core, part, :].astype(F32)
            outs.append(copy(fd.at[pl.ds(at, L)], gd_h.at[pl.ds(at, L)]))
    v_mask[...] = fin[0, :]
    v_ga[...] = fin[1, :]
    v_gm[...] = fin[2, :]
    v_bd[...] = fin[3, :]
    for r in range(4):
        v_bu[L * r : L * r + L] = fin[4 + r, :]
    for cp in outs:
        cp.wait()


def on_device(
    nbits, clean_in, noise_bits, mask_vector, gain_attn, w_qkv, w_out, gain_mlp,
    w_up, bias_up, w_down, bias_down, out_grad,
):
    L, D, T = 384, 768, 768
    cos, sin = tables(L)
    nx = max(1, nbits - 3)
    hbm = pl.BlockSpec(memory_space=pltpu.HBM)
    vm = pl.BlockSpec(memory_space=pltpu.VMEM)
    scratch = [
        ((8, L), F32), ((2, 8, L), F32), ((8, D), F32), ((L, 128), F32),
        ((128, 256), F32), ((128, 128), F32),
        ((T, D), BF), ((2 * T, D), BF), ((D, 1152), BF), ((D, D), BF), ((D, 1536), BF),
        ((1536, D), BF), ((2 * T, D), BF),
        ((2 * T, 1152), BF), ((12, 1, T), F32), ((2 * T, D), BF), ((T, D), F32),
        ((2 * T, D), BF), ((2 * T, 1536), BF), ((2 * T, 1536), BF), ((T, D), BF),
        ((T, D), BF), ((T, D), F32), ((2 * T, D), BF), ((2 * T, L), BF), ((T, 128), F32),
        ((1536, D), BF), ((D, 3072), BF),
        ((D, D), BF), ((L, 3072), BF), ((L, D), BF), ((192, 3072), BF),
        ((L, D), BF), ((192, 3072), BF), ((192, D), BF), ((96, 3072), BF),
        ((nx, 192, D), BF) if nbits > 3 else ((1, 16, 128), BF),
        ((nx, 96, 3072), BF) if nbits > 3 else ((1, 16, 128), BF),
        ((nbits + 3, 8, D), F32), ((nbits + 3, 8, D), F32),
    ]
    block_out, clean_grad, fin, g1, gd = pl.pallas_call(
        functools.partial(layer_kernel, nbits),
        out_shape=[
            jax.ShapeDtypeStruct((1, T, D), BF),
            jax.ShapeDtypeStruct((1, L, D), F32),
            jax.ShapeDtypeStruct((8, L), F32),
            jax.ShapeDtypeStruct((2, L, 3072), BF),
            jax.ShapeDtypeStruct((2, D, D), BF),
        ],
        in_specs=[hbm] + [vm] * 8 + [hbm] * 5,
        out_specs=[hbm, hbm, vm, hbm, hbm],
        scratch_shapes=[pltpu.VMEM(s, t) for s, t in scratch]
        + [
            pltpu.SemaphoreType.DMA((N_SEND + 1 * (nbits - 3),)),
            pltpu.SemaphoreType.DMA((N_RECV + 14 * (nbits - 3),)),
            pltpu.SemaphoreType.DMA((N_LOCAL,)),
        ],
        compiler_params=pltpu.CompilerParams(
            collective_id=0, has_side_effects=True, vmem_limit_bytes=64 * 2**20
        ),
        name="layer",
    )(
        clean_in, noise_bits, mask_vector, gain_attn, gain_mlp, bias_down, bias_up, cos, sin,
        w_qkv, w_out, w_up, w_down, out_grad,
    )
    vec = jax.ShapeDtypeStruct((L,), F32)
    gq, go, gu, gdown, out, clean, v_mask, v_ga, v_gm, v_bd, v_bu = pl.pallas_call(
        finish_kernel,
        out_shape=[
            jax.ShapeDtypeStruct((L, 2304), F32),
            jax.ShapeDtypeStruct((L, D), F32),
            jax.ShapeDtypeStruct((L, 3072), F32),
            jax.ShapeDtypeStruct((1536, D), F32),
            jax.ShapeDtypeStruct((1, T, D), BF),
            jax.ShapeDtypeStruct((1, L, D), F32),
            vec, vec, vec, vec, jax.ShapeDtypeStruct((4 * L,), F32),
        ],
        in_specs=[hbm, hbm, vm, hbm, hbm],
        out_specs=[hbm] * 6 + [vm] * 5,
        scratch_shapes=[
            pltpu.VMEM((2, L, 3072), BF), pltpu.VMEM((2, D, D), BF),
            pltpu.VMEM((L, 2304), F32), pltpu.VMEM((L, D), F32),
            pltpu.VMEM((L, 3072), F32), pltpu.VMEM((1536, D), F32),
            pltpu.VMEM((1, T, D), BF), pltpu.VMEM((1, L, D), F32),
            pltpu.SemaphoreType.DMA((42,)),
        ],
        compiler_params=pltpu.CompilerParams(vmem_limit_bytes=64 * 2**20),
        name="finish",
    )(g1, gd, fin, block_out, clean_grad)
    return out, clean, v_mask, v_ga, gq, go, v_gm, gu, v_bu, gdown, v_bd


def solution(mesh):
    nbits = int(math.log2(mesh.shape["dp"])) - 1
    seq = P(("dp", "fsdp"), None, None)
    row, vec = P("fsdp", None), P("fsdp")
    in_specs = (seq, P(("dp", "fsdp"), None), vec, vec, row, row, vec, row, vec, row, vec, seq)
    out_specs = (seq, seq, vec, vec, row, row, vec, row, vec, row, vec)
    return jax.shard_map(
        functools.partial(on_device, nbits), mesh=mesh,
        in_specs=in_specs, out_specs=out_specs, check_vma=False,
    )
```

```python
import functools
import math

import jax
import jax.numpy as jnp
import numpy as np
from jax import lax
from jax.experimental import pallas as pl
from jax.experimental.pallas import tpu as pltpu
from jax.sharding import PartitionSpec as P

HD = 64
BLOCK = 16
NORM_FLOOR = 1e-05
TANH_SCALE = 0.7978845608028654
CUBIC = 0.044715
BF = jnp.bfloat16
F32 = jnp.float32
MESH = pl.DeviceIdType.MESH
LOGIT_SCALE = 0.125 * math.log2(math.e)
N_SEND, N_RECV, N_LOCAL = 93, 185, 38
NN = (((1,), (0,)), ((), ()))
NT = (((1,), (1,)), ((), ()))
TN = (((0,), (0,)), ((), ()))


ROUTES = {
    "d0": "y0Z",
    "d1": "0y12",
    "d2": "y0Z",
    "u0": "y012",
    "u1": "y0Z",
    "u2": "10y2",
    "u3": "1y02",
    "u4": "y0Z",
    "u5": "y0Z",
    "q0": "0y12",
    "q1": "y102",
    "q2": "y0Z",
    "o": "0y12",
}
SCHEDULE = {
    ("b", 1): (
        ("d0", 0),
    ),
    ("dn", 0): (
        ("d1", 0),
        ("d2", 0),
    ),
    ("dn", 1): (
        ("u2", 0),
        ("d0", 1),
        ("u0", 0),
    ),
    ("dm", 0): (
        ("u3", 0),
        ("d2", 1),
        ("u1", 0),
    ),
    ("att", 0): (
        ("u2", 1),
        ("u4", 0),
        ("u0", 1),
        ("d0", 2),
    ),
    ("q", 0): (
        ("u5", 0),
        ("u0", 2),
        ("d2", 2),
    ),
    ("att", 2): (
        ("o", 0),
        ("d1", 1),
        ("u1", 1),
    ),
    ("att", 3): (
        ("d0", 3),
        ("u0", 3),
        ("u3", 1),
        ("u4", 1),
        ("u2", 2),
    ),
    ("q", 1): (
        ("d1", 2),
    ),
    ("att", 4): (
        ("d2", 3),
        ("o", 1),
        ("u1", 2),
    ),
    ("att", 5): (
        ("q0", 0),
        ("u0", 4),
        ("u5", 1),
        ("u4", 2),
    ),
    ("q", 2): (
        ("o", 2),
        ("u2", 3),
    ),
    ("da", 0): (
        ("q1", 0),
        ("d1", 3),
        ("u0", 5),
        ("d0", 4),
        ("u3", 2),
        ("u1", 3),
    ),
    ("da", 1): (
        ("q0", 1),
        ("u5", 2),
        ("d2", 4),
        ("u4", 3),
    ),
    ("bo", 0): (
        ("o", 3),
        ("s", 0),
        ("q1", 1),
        ("u0", 6),
        ("u2", 4),
        ("q2", 0),
        ("u1", 4),
        ("d1", 4),
        ("q0", 2),
    ),
    ("bo", 1): (
        ("u3", 3),
        ("u4", 4),
        ("s", 1),
        ("u5", 3),
        ("q1", 2),
    ),
    "tail": (
        ("u2", 5),
        ("d1", 5),
        ("o", 4),
        ("q0", 3),
        ("u3", 4),
        ("q2", 1),
        ("s", 2),
        ("q1", 3),
        ("u2", 6),
        ("u5", 4),
        ("o", 5),
        ("q0", 4),
        ("q2", 2),
        ("s", 3),
        ("d1", 6),
        ("q1", 4),
        ("u3", 5),
        ("q0", 5),
        ("o", 6),
        ("q2", 3),
        ("q1", 5),
        ("s", 4),
        ("u3", 6),
        ("q0", 6),
        ("q1", 6),
        ("q2", 4),
    ),
}


def dot(a, b, dims=NN):
    return lax.dot_general(a, b, dims, preferred_element_type=F32)


def mo(x, n):
    return pl.multiple_of(x, n)


def normalize(x):
    d = x - jnp.mean(x, axis=-1, keepdims=True)
    inv = lax.rsqrt(jnp.mean(d * d, axis=-1, keepdims=True) + NORM_FLOOR)
    return d * inv, inv


def normalize_backward(g, xhat, inv, gain):
    e = g * gain
    return inv * (
        e
        - jnp.mean(e, axis=-1, keepdims=True)
        - xhat * jnp.mean(e * xhat, axis=-1, keepdims=True)
    )


def layer_kernel(
    nbits,
    clean_h, noise, v_mask, v_ga, v_gm, v_bd, v_bu, cos_r, sin_r, wq_h, wo_h, wu_h, wd_h, og_h,
    out_h, cg_h, fin, o1_h, od_h,
    small_in, small, prow, mcol, mbb, mbe,
    stream, normed, wq, wo, wu, wd, og,
    qkv, lbuf, mixed, aa, nm, act, dpre, xs, xr, daf, db, dm, dks,
    gd, g1, r0d, r01, r1d, r11, r2d, r21, r3d, r31, red, re1,
    sbuf, srec, ss, rs, ls,
):
    L = 384
    D = 768
    T = 2 * L
    NT3 = L // 128
    d = lax.axis_index("dp")
    f = lax.axis_index("fsdp")
    c = lax.rem(d, 2)
    bits = [lax.rem(lax.div(d, 2 ** (b + 1)), 2) for b in range(nbits)]
    sib = (d + 1 - 2 * c, f)
    ypeer = (d, 1 - f)
    peers = [(d + (1 - 2 * bits[b]) * 2 ** (b + 1), f) for b in range(nbits)]
    u = 2 * bits[1] + bits[0]
    send_count, recv_count, local_count = [0], [0], [0]
    ends = []

    def take_send(n):
        k = send_count[0]
        send_count[0] += n
        return k

    def take_recv(n=1):
        k = recv_count[0]
        recv_count[0] += n
        return k

    def rc(k, src, dst, dev):
        return pltpu.make_async_remote_copy(
            src_ref=src, dst_ref=dst, send_sem=ss.at[k[0]], recv_sem=rs.at[k[1]],
            device_id=dev, device_id_type=MESH,
        )

    def remote(make, n=1):
        k = (take_send(n), take_recv(n))
        fam = lambda i=0: make((k[0] + i, k[1] + i), i)
        ends.append((fam, n))
        return fam

    def sent(fam):
        for at, (other_fam, n) in enumerate(ends):
            if other_fam is fam:
                for i in range(n):
                    fam(i).wait_send()
                ends.pop(at)
                return

    def local(src, dst):
        k = local_count[0]
        local_count[0] += 1
        return lambda: pltpu.make_async_copy(src, dst, ls.at[k])

    bar = pltpu.get_barrier_semaphore()
    for dev in [sib, ypeer] + peers:
        pl.semaphore_signal(bar, inc=1, device_id=dev, device_id_type=MESH)

    l_clean = [
        local(clean_h.at[0, pl.ds(128 * i, 128)], stream.at[pl.ds(256 * i + 128, 128)])
        for i in range(NT3)
    ]
    mine = mo(f * L, 128)
    other = mo((1 - f) * L, 128)
    l_wq = [
        local(
            wq_h.at[:, pl.ds(mo(j * D + c * L, 128), L)],
            wq.at[pl.ds(mine, L), pl.ds(j * L, L)],
        )
        for j in range(3)
    ]
    l_wo = local(wo_h, wo.at[pl.ds(mine, L)])
    l_wu = [
        local(
            wu_h.at[:, pl.ds(mo(h * 1536 + c * D, 128), D)],
            wu.at[pl.ds(mine, L), pl.ds(h * D, D)],
        )
        for h in range(2)
    ]
    l_wd = local(wd_h.at[pl.ds(mo(c * D, 128), D)], wd.at[pl.ds(mo(f * D, 128), D)])
    l_og = [
        local(
            og_h.at[0, pl.ds((r % 2) * L + 128 * (r // 2), 128)],
            og.at[pl.ds(128 * r, 128)],
        )
        for r in range(2 * NT3)
    ]
    for cp in l_clean + l_wq:
        cp().start()
    for r, v in enumerate((v_mask, v_ga, v_gm, v_bd)):
        small_in[r : r + 1, :] = v[...].astype(F32).reshape(1, L)
    for r in range(4):
        small_in[4 + r : 5 + r, :] = v_bu[pl.ds(L * r, L)].astype(F32).reshape(1, L)
    small[pl.ds(f, 1)] = small_in[...][None]

    def y_wq(unit):
        rows = mo(96 * unit, 16)
        return remote(
            lambda k, j: rc(
                k,
                wq_h.at[pl.ds(rows, 96), pl.ds(mo(j * D + c * L, 128), L)],
                wq.at[pl.ds(mo(f * L + rows, 16), 96), pl.ds(j * L, L)],
                ypeer,
            ),
            3,
        )

    yw_q = y_wq(u)
    yw_q2 = y_wq(3 - u)
    y_small = remote(lambda k, i: rc(k, small_in, small.at[f], ypeer))

    def spread(buf, base, unit_rows, unit, dev):
        rows = mo(base + unit_rows * unit, 16)
        return remote(
            lambda k, i: rc(
                k, buf.at[pl.ds(rows, unit_rows)], buf.at[pl.ds(rows, unit_rows)], dev
            )
        )


    def spread_q(dev):
        rows = mo(other + 96 * u, 16)
        return remote(
            lambda k, j: rc(
                k, wq.at[pl.ds(rows, 96), pl.ds(j * L, L)],
                wq.at[pl.ds(rows, 96), pl.ds(j * L, L)], dev,
            ),
            3,
        )

    xw_q = spread_q(peers[0])
    zw_q = spread_q(peers[1])
    def half_of(i):
        if isinstance(i, int):
            return 1 - f if i == 0 else f
        return (1 - f) * (1 - i) + f * i

    def up_lanes(i):
        return pl.ds(mo(half_of(i) * D, 128), D)

    def y_wu_to(unit):
        rows = mo(96 * unit, 16)

        def make(k, i):
            h = f if i == 0 else 1 - f
            return rc(
                k,
                wu_h.at[pl.ds(rows, 96), pl.ds(mo(h * 1536 + c * D, 128), D)],
                wu.at[pl.ds(mo(f * L + rows, 16), 96), pl.ds(mo(h * D, 128), D)],
                ypeer,
            )

        return remote(make, 2)

    def spread_u(dev):
        rows = mo(other + 96 * u, 16)
        return remote(
            lambda k, i: rc(
                k, wu.at[pl.ds(rows, 96), up_lanes(i)], wu.at[pl.ds(rows, 96), up_lanes(i)], dev
            ),
            2,
        )

    yw_u = y_wu_to(u)
    yw_u2 = y_wu_to(3 - u)
    xw_u = spread_u(peers[0])
    zw_u = spread_u(peers[1])
    ux, uz = 2 * bits[1] + 1 - bits[0], 2 * (1 - bits[1]) + bits[0]
    odown = mo((1 - f) * D, 128)
    yw_d = remote(
        lambda k, i: rc(
            k,
            wd_h.at[pl.ds(mo(c * D + 192 * u + 96 * i, 16), 96)],
            wd.at[pl.ds(mo(f * D + 192 * u + 96 * i, 16), 96)],
            ypeer,
        ),
        2,
    )

    def spread_d(dev):
        def make(k, i):
            rows = pl.ds(mo(odown + 192 * u + 96 * i, 16), 96)
            return rc(k, wd.at[rows], wd.at[rows], dev)

        return remote(make, 2)

    xw_d = spread_d(peers[0])
    zw_d = spread_d(peers[1])
    xw_d2 = spread(wd, odown, 96, 2 * uz, peers[0])
    zw_d2 = spread(wd, odown, 96, 2 * ux + 1, peers[1])
    yw_o = remote(
        lambda k, i: rc(
            k,
            wo_h.at[pl.ds(mo(192 * c + 96 * bits[0], 16), 96)],
            wo.at[pl.ds(mo(f * L + 192 * c + 96 * bits[0], 16), 96)],
            ypeer,
        )
    )
    xw_o = spread(wo, mo(other + 192 * c, 16), 96, bits[0], peers[0])
    sw_o = spread(wo, other, 192, c, sib)

    s_norm = remote(
        lambda k, i: rc(
            k, normed.at[pl.ds(mo(256 * i, 16), 256)],
            normed.at[pl.ds(mo(T + 256 * i, 16), 256)], sib,
        ),
        NT3,
    )
    s_og = remote(lambda k, i: rc(k, og.at[pl.ds(0, T)], og.at[pl.ds(T, T)], sib))

    def mixed_copy(k, i):
        s = 1 - i // 3 if isinstance(i, int) else 1 - lax.div(i, 3)
        p = i % 3 if isinstance(i, int) else lax.rem(i, 3)
        lanes = pl.ds(mo(c * L + 128 * p, 128), 128)
        return rc(
            k, mixed.at[pl.ds(mo(s * T, 16), T), lanes],
            mixed.at[pl.ds(mo((1 - s) * T, 16), T), lanes], sib,
        )

    s_mix = remote(mixed_copy, 6)

    def rows_copy(buf, src0, dst, dst0):
        return remote(
            lambda k, i: rc(
                k, buf.at[pl.ds(mo(src0 + 256 * i, 16), 256)],
                dst.at[pl.ds(mo(dst0 + 256 * i, 16), 256)], sib,
            ),
            NT3,
        )

    s_nm = rows_copy(nm, 0, nm, T)
    s_dn = rows_copy(xs, 0, xr, 0)
    s_db = rows_copy(db, 0, db, T)
    s_bo = rows_copy(xs, 0, xr, 0)
    right = pl.ds(D, D)
    s_da = remote(
        lambda k, i: rc(
            k, dpre.at[pl.ds(mo(256 * i, 16), 256), right],
            dpre.at[pl.ds(mo(T + 256 * i, 16), 256), right], sib,
        ),
        NT3,
    )

    class Chunk:
        pass

    chunks = {}

    def make_chunk(name, g, gbase, nr, l0, nl, recv, rbase, oref, orow, blk):
        ch = Chunk()
        lanes = pl.ds(l0, nl)
        route = ROUTES[name]

        def greg(h, off, n):
            return g.at[pl.ds(mo(gbase(h) + off, 16), n), lanes]

        def rreg(stage, at, n):
            return recv[stage].at[pl.ds((rbase >> (0, 1, 1, 2)[stage]) + at, n), lanes]

        def oreg(core, off, n):
            return oref.at[core, pl.ds(mo(orow + off, 16), n), lanes]

        def at_role(role, fn):
            if role is None:
                fn()
            else:
                pl.when(role)(fn)

        class Stage:
            def __init__(self, copies, sums=(), sender=None, receiver=None):
                self.copies, self.sums = copies, sums
                self.sender, self.receiver = sender, receiver

            def start(self):
                at_role(self.sender, lambda: [cp().start() for cp in self.copies] and None)

            def sent(self):
                at_role(self.sender, lambda: [cp().wait_send() for cp in self.copies] and None)

            def arrive(self):
                def go():
                    for cp in self.copies:
                        cp().wait_recv()
                    for h, at, m, parts in self.sums:
                        add(h, at, m, parts)

                at_role(self.receiver, go)

        k_send = take_send(3 if "Z" in route else 1 if route[0] == "y" else 2)

        def copy(i, src, dst, dev):
            k = take_recv()
            return lambda: pltpu.make_async_remote_copy(
                src_ref=src(), dst_ref=dst(), send_sem=ss.at[k_send + i], recv_sem=rs.at[k],
                device_id=dev, device_id_type=MESH,
            )

        def add(h, off, n, parts):
            gr = greg(h, off, n)
            step = min(blk, n)

            def body(i, carry):
                sl = pl.ds(mo(i * step, 16), step)
                x = gr[sl, :].astype(F32)
                for stage, at in parts:
                    x = x + rreg(stage, at, n)[sl, :].astype(F32)
                gr[sl, :] = x.astype(BF)
                return carry

            lax.fori_loop(0, n // step, body, 0)

        sums, back = [], []
        holder = None
        off, n, both, stage = 0, nr, True, 0

        def give_back(at, m, devs, **roles):
            back.append(lambda src: Stage(
                [
                    copy(i, lambda: src(at, m), lambda: oreg(c, at, m), dev)
                    for i, dev in enumerate(devs)
                ],
                **roles,
            ))

        for step in route:
            if step == "y":
                sums.append(Stage(
                    [copy(
                        0, lambda off=off, n=n: greg(1 - f, off, n),
                        lambda stage=stage, n=n: rreg(stage, 0, n), ypeer,
                    )],
                    [(f, off, n, [(stage, 0)])],
                ))
                both = False
                stage += 1
            elif step == "Z":
                m4 = n // 4
                out, parts, devs = [], [], []
                where = [(stage, 0), (stage, m4), (stage + 1, 0)]
                mine_off = off + (2 * bits[1] + bits[2]) * m4
                for i, (x1, x2) in enumerate(((0, 1), (1, 0), (1, 1))):
                    b1 = 1 - bits[1] if x1 else bits[1]
                    b2 = 1 - bits[2] if x2 else bits[2]
                    dev = (d + (b1 - bits[1]) * 4 + (b2 - bits[2]) * 8, f)
                    to = off + (2 * b1 + b2) * m4
                    st, at = where[i]
                    out.append(copy(
                        i, lambda to=to, m4=m4: greg(f, to, m4),
                        lambda st=st, at=at, m4=m4: rreg(st, at, m4), dev,
                    ))
                    devs.append(dev)
                    parts.append((st, at))
                sums.append(Stage(out, [(f, mine_off, m4, parts)]))
                give_back(mine_off, m4, devs)
                off, n, stage = mine_off, m4, stage + 2
            elif step == "E":
                m2 = n // 2
                inner = bits[1] + bits[2] - 2 * bits[1] * bits[2] == 1
                outer = bits[1] + bits[2] - 2 * bits[1] * bits[2] == 0
                middle = (d + (1 - 2 * bits[1]) * 4 + (1 - 2 * bits[2]) * 8, f)
                keep, give = off + bits[2] * m2, off + (1 - bits[2]) * m2
                sums.append(Stage(
                    [copy(
                        0, lambda off=off, n=n: greg(f, off, n),
                        lambda stage=stage, n=n: rreg(stage, 0, n), peers[1],
                    )],
                    [(f, off, n, [(stage, 0)])], sender=outer, receiver=inner,
                ))
                sums.append(Stage(
                    [copy(
                        0, lambda give=give, m2=m2: greg(f, give, m2),
                        lambda stage=stage, m2=m2: rreg(stage + 1, 0, m2), middle,
                    )],
                    [(f, keep, m2, [(stage + 1, 0)])], sender=inner, receiver=inner,
                ))
                give_back(off, n, [peers[1]], sender=inner, receiver=outer)
                give_back(keep, m2, [middle], sender=inner, receiver=inner)
                holder = inner
                off, n, stage = keep, m2, stage + 2
            else:
                j = int(step)
                m2 = n // 2
                give, keep = off + (1 - bits[j]) * m2, off + bits[j] * m2
                owners = [0, 1] if both else [f]
                sums.append(Stage(
                    [
                        copy(
                            i, lambda h=h, give=give, m2=m2: greg(h, give, m2),
                            lambda stage=stage, i=i, m2=m2: rreg(stage, i * m2, m2), peers[j],
                        )
                        for i, h in enumerate(owners)
                    ],
                    [(h, keep, m2, [(stage, i * m2)]) for i, h in enumerate(owners)],
                ))
                give_back(keep, m2, [peers[j]])
                off, n, stage = keep, m2, stage + 1
        extra = [
            copy(
                0, lambda off=off, n=n: greg(f, off, n),
                lambda j=j, n=n: recv[4].at[j - 3, pl.ds((rbase >> 2), n), lanes], peers[j],
            )
            for j in range(3, nbits)
        ]
        own = local(greg(f, off, n), oreg(c, off, n))
        gathers = [
            make((lambda at, m: greg(f, at, m)) if i == 0 else (lambda at, m: oreg(c, at, m)))
            for i, make in enumerate(reversed(back))
        ]
        gathers.append(Stage([copy(0, lambda: oreg(c, 0, nr), lambda: oreg(c, 0, nr), sib)]))

        def finished():
            for m, cp in enumerate(extra):
                cp().start()
                cp().wait_send()
                cp().wait_recv()
                gr = greg(f, off, n)
                gr[...] = (
                    gr[...].astype(F32)
                    + recv[4][m, pl.ds((rbase >> 2), n), lanes].astype(F32)
                ).astype(BF)
            own().start()

        def reduce_event(i):
            sums[i].arrive()
            sums[i].sent()
            if i + 1 < len(sums):
                sums[i + 1].start()
                return
            at_role(holder, finished)
            gathers[0].start()

        def gather_event(i):
            gathers[i].arrive()
            if i == 0:
                at_role(holder, lambda: own().wait())
            gathers[i].sent()
            if i + 1 < len(gathers):
                gathers[i + 1].start()

        ch.start = sums[0].start
        ch.events = [functools.partial(reduce_event, i) for i in range(len(sums))] + [
            functools.partial(gather_event, i) for i in range(len(gathers))
        ]
        chunks[name] = ch

    recv_d = (r0d, r1d, r2d, r3d, red)
    recv_1 = (r01, r11, r21, r31, re1)
    for k in range(3):
        make_chunk(
            f"d{k}", gd, lambda h, k=k: h * D + 256 * k, 256, 0, D, recv_d, 256 * k,
            od_h, 256 * k, 32,
        )
    for t in range(6):
        make_chunk(f"u{t}", g1, lambda h: h * L, L, 256 * t, 256, recv_1, 0, o1_h, 0, 48)
    for p in range(3):
        make_chunk(f"q{p}", g1, lambda h: h * L, L, 1536 + L * p, L, recv_1, 0, o1_h, 0, 48)
    make_chunk("o", g1, lambda h: h * L, L, 1536 + 3 * L, L, recv_1, 0, o1_h, 0, 48)

    def handle(key):
        for name, stage in SCHEDULE.get(key, ()):
            chunks[name].events[stage]()

    def handle_at(idx, keys):
        for i, key in keys.items():
            if SCHEDULE.get(key):
                pl.when(idx == i)(lambda key=key: handle(key))

    pl.semaphore_wait(bar, 2 + nbits)
    y_small().start()
    for j in range(3):
        yw_q(j).start()
    for j in range(3):
        yw_q2(j).start()
    yw_o().start()
    for i in range(2):
        yw_u(i).start()
        yw_u2(i).start()
    for i in range(2):
        yw_d(i).start()
    for cp in l_og + l_wu + [l_wo, l_wd]:
        cp().start()

    lane = lax.broadcasted_iota(jnp.int32, (1, 128), 1)
    low_half = lane < HD
    rot_low = lax.rem(lane, HD) < HD // 2
    bm = [jnp.where(low_half, 1.0, 0.0).astype(BF), jnp.where(low_half, 0.0, 1.0).astype(BF)]
    ir = lax.div(lax.broadcasted_iota(jnp.int32, (128, 128), 0), BLOCK)
    ic = lax.div(lax.broadcasted_iota(jnp.int32, (128, 128), 1), BLOCK)
    neg = -1e30
    mbb[:, 0:128] = jnp.where(ir < ic, 0.0, neg)
    mbb[:, 128:256] = jnp.where(ir <= ic, 0.0, neg)
    mbe[...] = jnp.where(ir == ic, 0.0, neg)
    nf = noise[...].astype(F32)
    for i in range(NT3):
        mcol[128 * i : 128 * i + 128, :] = jnp.broadcast_to(
            nf[:, 128 * i : 128 * i + 128], (128, 128)
        ).T
    sbuf[0] = jnp.zeros((8, D), F32)

    y_small().wait_recv()
    prow[:, 0:L] = small[0]
    prow[:, L:D] = small[1]
    mvec = prow[0:1, :]
    gain_a = prow[1:2, :]
    gain_m = prow[2:3, :]
    bias_d = prow[3:4, :]

    def wide(m):
        return jnp.concatenate([m] * (D // 128), axis=1)

    for i in range(NT3):
        l_clean[i]().wait()

    def attn_norm(i, carry):
        n0 = mo(256 * i, 128)
        x = stream[pl.ds(n0 + 128, 128), :].astype(F32)
        m = wide(mcol[pl.ds(mo(128 * i, 128), 128), :])
        y = jnp.where(m > 0.5, mvec, x)
        stream[pl.ds(n0, 128), :] = y.astype(BF)
        normed[pl.ds(n0, 128), :] = (normalize(y)[0] * gain_a).astype(BF)
        normed[pl.ds(n0 + 128, 128), :] = (normalize(x)[0] * gain_a).astype(BF)
        s_norm(i).start()
        return carry

    lax.fori_loop(0, NT3, attn_norm, 0)

    for j in range(3):
        yw_q(j).wait_recv()
        xw_q(j).start()
        zw_q(j).start()
    for i in range(NT3):
        s_norm(i).wait_recv()
    for cp in l_og:
        cp().wait()
    s_og().start()
    for j in range(3):
        l_wq[j]().wait()
        yw_q2(j).wait_recv()
        xw_q(j).wait_recv()
        zw_q(j).wait_recv()

    def turn(x, cos, sin):
        return x * cos + jnp.where(rot_low, pltpu.roll(x, 96, 1), pltpu.roll(x, 32, 1)) * sin

    def rows2(tab, i):
        t = tab[pl.ds(mo(128 * i, 128), 128), :]
        return jnp.concatenate([t, t], axis=0)

    def qkv_rows(r, carry):
        rows = pl.ds(mo(256 * r, 128), 256)
        joined = dot(normed[rows, :], wq[...])
        i = lax.rem(r, NT3)
        cos, sin = rows2(cos_r, i), rows2(sin_r, i)
        for p in range(6):
            x = joined[:, 128 * p : 128 * p + 128]
            qkv[rows, 128 * p : 128 * p + 128] = turn(x, cos, sin).astype(BF)
        qkv[rows, 2 * L : 3 * L] = joined[:, 2 * L : 3 * L].astype(BF)
        return carry

    lax.fori_loop(0, 2 * NT3, qkv_rows, 0)

    def run_at(idx, table):
        for k, fns in table.items():
            def go(fns=fns):
                for fn in fns:
                    fn()
            pl.when(idx == k)(go)

    def w_o_1():
        l_wo().wait()
        yw_o().wait_recv()
        xw_o().start()

    def w_o_2():
        xw_o().wait_recv()
        sw_o().start()

    def w_u(i):
        yw_u(i).wait_recv()
        xw_u(i).start()
        zw_u(i).start()

    def w_u_end(i):
        yw_u2(i).wait_recv()
        xw_u(i).wait_recv()
        zw_u(i).wait_recv()

    def w_d(i):
        yw_d(i).wait_recv()
        xw_d(i).start()
        zw_d(i).start()

    fwd_events = {0: [w_o_1], 2: [lambda: w_u(0)], 4: [w_o_2]}

    def attn_fwd(n, carry):
        s, p = 1 - lax.div(n, 3), lax.rem(n, 3)
        r0 = s * T
        lq = pl.ds(mo(128 * p, 128), 128)
        lk = pl.ds(mo(L + 128 * p, 128), 128)
        lv = pl.ds(mo(2 * L + 128 * p, 128), 128)

        def rws(a, m):
            return pl.ds(mo(r0 + a, 128), m)

        kcl = [qkv[rws(256 * j + 128, 128), lk] for j in range(NT3)]
        vcl = [qkv[rws(256 * j + 128, 128), lv] for j in range(NT3)]
        blocks = [(i, a) for i in range(NT3) for a in range(2)]
        sc, pr, mixes = {}, {}, {}
        for i, a in blocks:
            q = qkv[rws(256 * i, 256), lq]
            kc = jnp.concatenate(kcl[: i + 1], axis=0) * bm[a]
            st = dot(kc, q, NT) * LOGIT_SCALE
            kn = qkv[rws(256 * i, 128), lk] * bm[a]
            sn = dot(kn, q[:128], NT) * LOGIT_SCALE + mbe[...]
            last = st[128 * i :] + mbb[...]
            st = last if i == 0 else jnp.concatenate([st[: 128 * i], last], axis=0)
            sc[i, a] = st, sn
        for i, a in blocks:
            st, sn = sc[i, a]
            m1 = jnp.max(st, axis=0, keepdims=True)
            mn = jnp.maximum(m1[:, :128], jnp.max(sn, axis=0, keepdims=True))
            m = jnp.concatenate([mn, m1[:, 128:]], axis=1)
            pt, pn = jnp.exp2(st - m), jnp.exp2(sn - mn)
            tot = jnp.sum(pt, axis=0, keepdims=True)
            totn = tot[:, :128] + jnp.sum(pn, axis=0, keepdims=True)
            tot = jnp.concatenate([totn, tot[:, 128:]], axis=1)
            lbuf[(s * 3 + p) * 2 + a, :, 256 * i : 256 * i + 256] = m + jnp.log2(tot)
            pr[i, a] = pt.astype(BF), pn.astype(BF)
        for i, a in blocks:
            vc = jnp.concatenate(vcl[: i + 1], axis=0) * bm[a] + bm[1 - a]
            vn = qkv[rws(256 * i, 128), lv] * bm[a] + bm[1 - a]
            o = dot(pr[i, a][0], vc, TN)
            mixes[i, a] = jnp.concatenate([o[:128] + dot(pr[i, a][1], vn, TN), o[128:]], axis=0)
        for i in range(NT3):
            o0, o1 = mixes[i, 0], mixes[i, 1]
            sums = pltpu.roll(jnp.where(low_half, o1, o0), HD, 1)
            mixed[rws(256 * i, 256), pl.ds(mo(c * L + 128 * p, 128), 128)] = (
                jnp.where(low_half, o0, o1) * (1.0 / sums)
            ).astype(BF)
        s_mix(n).start()
        run_at(n, fwd_events)
        return carry

    lax.fori_loop(0, 6, attn_fwd, 0)

    sw_o().wait_recv()
    for n in range(3):
        s_mix(n).wait_recv()

    def out_proj(i, carry):
        rows = pl.ds(mo(256 * i, 128), 256)
        x = stream[rows, :].astype(F32) + dot(mixed[rows, :], wo[...])
        aa[rows, :] = x
        nm[rows, :] = (normalize(x)[0] * gain_m).astype(BF)
        s_nm(i).start()
        return carry

    lax.fori_loop(0, NT3, out_proj, 0)
    for h in range(2):
        l_wu[h]().wait()
    w_u(1)
    w_u_end(0)

    for n in range(2):
        h = half_of(n)
        lanes = up_lanes(n)
        if n == 1:
            w_u_end(1)
        bu = jnp.concatenate(
            [small[h, pl.ds(4 + 2 * c + r, 1), :] for r in range(2)], axis=1
        )

        def rows_a(r, carry, n=n, lanes=lanes, bu=bu):
            if n == 0:
                @pl.when(r == 2)
                def _():
                    for i in range(NT3):
                        s_nm(i).wait_recv()

            rows = pl.ds(mo(L * r, 128), L)
            pre = dot(nm[rows, :], wu[:, lanes]) + bu
            sq = pre * pre
            half = 0.5 + 0.5 * jnp.tanh(pre * (TANH_SCALE + TANH_SCALE * CUBIC * sq))
            a = pre * half
            act[rows, lanes] = a.astype(BF)
            slope = half + 2.0 * a * (1.0 - half) * (
                TANH_SCALE + 3.0 * CUBIC * TANH_SCALE * sq
            )
            dpre[rows, lanes] = slope.astype(BF)
            return carry

        lax.fori_loop(0, 4, rows_a, 0)
        if n == 0:
            s_og().wait_recv()
            w_d(0)
        else:
            w_d(1)

        def down_grad(k, carry, n=n, h=h):
            at = mo(h * D + 256 * k, 128)
            gd[pl.ds(at, 256), :] = dot(act[:, pl.ds(at, 256)], og[...], TN).astype(BF)
            for i in range(3):
                if n == 0 and ROUTES[f"d{i}"][0] == "y":
                    pl.when(k == i)(chunks[f"d{i}"].start)
            handle_at(k, {i: ("a", n, i) for i in range(3)})
            return carry

        handle(("a", n))
        lax.fori_loop(0, 3, down_grad, 0)
    zw_d(0).wait_recv()
    xw_d2().start()
    for i in range(3):
        if ROUTES[f"d{i}"][0] != "y":
            chunks[f"d{i}"].start()
    l_wd().wait()

    for n in range(2):
        h = half_of(1 - n)
        lanes = up_lanes(1 - n)

        def rows_b(r, tot, lanes=lanes):
            rows = pl.ds(mo(L * r, 128), L)
            g = dot(og[rows, :], wd[lanes, :], NT) * dpre[rows, lanes].astype(F32)
            dpre[rows, lanes] = g.astype(BF)
            return tot + jnp.sum(g, axis=0, keepdims=True)

        if n == 1:
            xw_d(0).wait_recv()
            zw_d(1).wait_recv()
            xw_d2().wait_recv()
            zw_d2().wait_recv()
        sbuf[0, pl.ds(4 + h, 1), :] = lax.fori_loop(0, 4, rows_b, jnp.zeros((1, D), F32))
        if n == 0:
            xw_d(1).wait_recv()
            zw_d2().start()
        handle(("b", n))
    for n in range(2):
        g1[:, n * D : n * D + D] = dot(nm[...], dpre[:, n * D : n * D + D], TN).astype(BF)
        for t in range(3 * n, 3 * n + 3):
            chunks[f"u{t}"].start()
        handle(("u", n))

    def dn_other(i, carry):
        x = dot(dpre[pl.ds(mo(T + 256 * i, 128), 256), :], wu[...], NT)
        xs[pl.ds(mo(256 * i, 128), 256), :] = x.astype(BF)
        s_dn(i).start()
        return carry

    lax.fori_loop(0, NT3, dn_other, 0)
    handle(("dn", 0))

    def dn_own(i, sums):
        rows = pl.ds(mo(256 * i, 128), 256)
        g = dot(dpre[rows, :], wu[...], NT)
        s_dn(i).wait_recv()
        g = g + xr[rows, :].astype(F32)
        xhat, inv = normalize(aa[rows, :])
        ograd = og[rows, :].astype(F32)
        after = ograd + normalize_backward(g, xhat, inv, gain_m)
        daf[rows, :] = after
        db[rows, :] = after.astype(BF)
        s_db(i).start()
        return (
            sums[0] + jnp.sum(g * xhat, axis=0, keepdims=True),
            sums[1] + jnp.sum(ograd, axis=0, keepdims=True),
        )

    zrow = jnp.zeros((1, D), F32)
    g_gain_m, g_bias_d = lax.fori_loop(0, NT3, dn_own, (zrow, zrow))
    sbuf[0, 2:3, :] = g_gain_m
    sbuf[0, 3:4, :] = g_bias_d
    handle(("dn", 1))

    wo_rows = pl.ds(mo(c * L, 128), L)
    dm[0:T, :] = dot(db[0:T, :], wo[wo_rows, :], NT).astype(BF)
    for i in range(NT3):
        s_db(i).wait_recv()
    dm[T : 2 * T, :] = dot(db[T : 2 * T, :], wo[wo_rows, :], NT).astype(BF)
    for n in range(3, 6):
        s_mix(n).wait_recv()
    g1[:, 1536 + 3 * L : 1536 + 4 * L] = dot(mixed[...], db[:, wo_rows], TN).astype(BF)
    chunks["o"].start()
    handle(("dm", 0))

    pick_lane = lax.rem(lax.broadcasted_iota(jnp.int32, (8, 256), 1), 128)
    pick_row = lax.broadcasted_iota(jnp.int32, (8, 256), 0)
    pick = jnp.where(pick_row == lax.div(pick_lane, HD), 1.0, 0.0).astype(BF)

    def attn_bwd(n, carry):
        s, p = lax.rem(n, 2), lax.div(n, 2)
        r0 = s * T
        lq = pl.ds(mo(128 * p, 128), 128)
        lk = pl.ds(mo(L + 128 * p, 128), 128)
        lv = pl.ds(mo(2 * L + 128 * p, 128), 128)

        def rws(a, m):
            return pl.ds(mo(r0 + a, 128), m)

        prod = dm[rws(0, T), lq].astype(F32) * mixed[
            rws(0, T), pl.ds(mo(c * L + 128 * p, 128), 128)
        ].astype(F32)
        hi = prod.astype(BF)
        lo = (prod - hi.astype(F32)).astype(BF)
        drow = dot(pick, jnp.concatenate([hi, lo], axis=1), NT)

        def heads(x, y):
            return jnp.where(low_half, x, y)

        blocks = [(kt, a) for kt in range(NT3) for a in range(2)]
        sc, dp, res = {}, {}, {}
        for kt, a in blocks:
            q0, nq = 256 * kt, T - 256 * kt
            q = qkv[rws(q0, nq), lq]
            lt = lbuf[(s * 3 + p) * 2 + a][:, q0:]
            kc = qkv[rws(q0 + 128, 128), lk] * bm[a]
            kn = qkv[rws(q0, 128), lk] * bm[a]
            st = dot(kc, q, NT) * LOGIT_SCALE - lt
            first = st[:, :256] + mbb[...]
            st = first if nq == 256 else jnp.concatenate([first, st[:, 256:]], axis=1)
            sn = dot(kn, q[:128], NT) * LOGIT_SCALE - lt[:, :128] + mbe[...]
            sc[kt, a] = st, sn
        for kt, a in blocks:
            q0, nq = 256 * kt, T - 256 * kt
            do = dm[rws(q0, nq), lq]
            vc = qkv[rws(q0 + 128, 128), lv] * bm[a]
            vn = qkv[rws(q0, 128), lv] * bm[a]
            dr = drow[a : a + 1, q0:]
            dp[kt, a] = dot(vc, do, NT) - dr, dot(vn, do[:128], NT) - dr[:, :128]
        for b in blocks:
            pt, pn = jnp.exp2(sc[b][0]), jnp.exp2(sc[b][1])
            res[b] = (
                (pt * dp[b][0]).astype(BF), (pn * dp[b][1]).astype(BF),
                pt.astype(BF), pn.astype(BF),
            )
        for kt in range(NT3):
            q0, nq = 256 * kt, T - 256 * kt
            q, do = qkv[rws(q0, nq), lq], dm[rws(q0, nq), lq]
            r0_, r1_ = res[kt, 0], res[kt, 1]
            dks[pl.ds(q0 + 128, 128), :] = heads(dot(r0_[0], q), dot(r1_[0], q))
            dks[pl.ds(q0, 128), :] = heads(dot(r0_[1], q[:128]), dot(r1_[1], q[:128]))
            qkv[rws(q0 + 128, 128), lv] = heads(dot(r0_[2], do), dot(r1_[2], do)).astype(BF)
            qkv[rws(q0, 128), lv] = heads(
                dot(r0_[3], do[:128]), dot(r1_[3], do[:128])
            ).astype(BF)
        dqs = []
        for i in range(NT3):
            kc = jnp.concatenate([qkv[rws(256 * j + 128, 128), lk] for j in range(i + 1)], axis=0)
            kn = qkv[rws(256 * i, 128), lk]
            both = []
            for a in range(2):
                ds = jnp.concatenate(
                    [
                        res[kt, a][0][:, 256 * (i - kt) : 256 * (i - kt) + 256]
                        for kt in range(i + 1)
                    ],
                    axis=0,
                )
                x = dot(ds, kc, TN)
                x = jnp.concatenate([x[:128] + dot(res[i, a][1], kn, TN), x[128:]], axis=0)
                both.append(x)
            dqs.append(heads(*both))
        for i in range(NT3):
            cos, sin = rows2(cos_r, i), rows2(sin_r, i)
            dk = dks[pl.ds(256 * i, 256), :]
            qkv[rws(256 * i, 256), lq] = (turn(dqs[i], cos, -sin) * 0.125).astype(BF)
            qkv[rws(256 * i, 256), lk] = (turn(dk, cos, -sin) * 0.125).astype(BF)
        handle_at(n, {i: ("att", i) for i in range(6)})

        @pl.when(s == 1)
        def _():
            dj = jnp.concatenate([qkv[:, lq], qkv[:, lk], qkv[:, lv]], axis=1)
            g1[:, pl.ds(mo(1536 + L * p, 128), L)] = dot(normed[...], dj, TN).astype(BF)

        for i in range(3):
            pl.when(n == 2 * i + 1)(chunks[f"q{i}"].start)
        handle_at(n, {2 * i + 1: ("q", i) for i in range(3)})
        return carry

    lax.fori_loop(0, 6, attn_bwd, 0)

    def da_other(i, carry):
        x = dot(qkv[pl.ds(mo(T + 256 * i, 128), 256), :], wq[...], NT)
        dpre[pl.ds(mo(256 * i, 128), 256), right] = x.astype(BF)
        s_da(i).start()
        return carry

    lax.fori_loop(0, NT3, da_other, 0)
    handle(("da", 0))
    cg_out = [
        local(daf.at[pl.ds(256 * i, 128)], cg_h.at[0, pl.ds(128 * i, 128)]) for i in range(NT3)
    ]

    def da_own(i, sums):
        rows = pl.ds(mo(256 * i, 128), 256)
        g = dot(qkv[rows, :], wq[...], NT)
        s_da(i).wait_recv()
        g = g + dpre[pl.ds(mo(T + 256 * i, 128), 256), right].astype(F32)
        xhat, inv = normalize(stream[rows, :].astype(F32))
        ds = daf[rows, :] + normalize_backward(g, xhat, inv, gain_a)
        m = wide(mcol[pl.ds(mo(128 * i, 128), 128), :]) > 0.5
        daf[pl.ds(mo(256 * i, 128), 128), :] = ds[128:] + jnp.where(m, 0.0, ds[:128])
        return (
            sums[0] + jnp.sum(jnp.where(m, ds[:128], 0.0), axis=0, keepdims=True),
            sums[1] + jnp.sum(g * xhat, axis=0, keepdims=True),
        )

    g_mask, g_gain_a = lax.fori_loop(0, NT3, da_own, (zrow, zrow))
    for cp in cg_out:
        cp().start()
    sbuf[0, 0:1, :] = g_mask
    sbuf[0, 1:2, :] = g_gain_a

    smalls = [
        remote(lambda k, i, n=n, dev=dev: rc(k, sbuf.at[n], srec.at[n], dev))
        for n, dev in enumerate([sib, ypeer] + peers)
    ]
    s_last = remote(
        lambda k, i: rc(k, sbuf.at[nbits + 2], srec.at[nbits + 2], sib)
    )
    row = lax.broadcasted_iota(jnp.int32, (8, D), 0)

    def small_step(n):
        smalls[n]().wait_recv()
        new = srec[n]
        if n == 0:
            new = jnp.where(row < 4, new, 0.0)
        sbuf[n + 1] = sbuf[n] + new
        if n + 1 < len(smalls):
            smalls[n + 1]().start()
        else:
            s_last().start()

    def small_rest():
        for n in range(4, len(smalls)):
            small_step(n)

    small_sum = Chunk()
    small_sum.events = [functools.partial(small_step, n) for n in range(4)] + [
        small_rest, lambda: s_last().wait_recv(),
    ]
    chunks["s"] = small_sum
    smalls[0]().start()
    handle(("da", 1))

    sent(s_dn)

    def bo_other(i, carry):
        x = dot(act[pl.ds(mo(T + 256 * i, 128), 256), :], wd[...])
        xs[pl.ds(mo(256 * i, 128), 256), :] = x.astype(BF)
        s_bo(i).start()
        return carry

    lax.fori_loop(0, NT3, bo_other, 0)
    handle(("bo", 0))
    sent(s_nm)

    def bo_own(i, carry):
        rows = pl.ds(mo(256 * i, 128), 256)
        x = aa[rows, :] + dot(act[rows, :], wd[...])
        s_bo(i).wait_recv()
        nm[rows, :] = (x + xr[rows, :].astype(F32) + bias_d).astype(BF)
        return carry

    lax.fori_loop(0, NT3, bo_own, 0)
    l_out = [
        local(
            nm.at[pl.ds(128 * r, 128)],
            out_h.at[0, pl.ds((r % 2) * L + 128 * (r // 2), 128)],
        )
        for r in range(2 * NT3)
    ]
    for cp in l_out:
        cp().start()
    handle(("bo", 1))
    handle("tail")
    for ch in chunks.values():
        ch.events[-1]()
    last = len(smalls)
    tot = sbuf[last]
    oth = srec[last]
    mh = jnp.where(f == 0, tot[0:4, 0:L], tot[0:4, L:D])
    fin[0:4, :] = mh
    for core_off, x in ((c, tot), (1 - c, oth)):
        v = jnp.where(f == 0, x[4:5, :], x[5:6, :])
        fin[pl.ds(4 + 2 * core_off, 1), :] = v[:, 0:L]
        fin[pl.ds(5 + 2 * core_off, 1), :] = v[:, L:D]
    for cp in l_out + cg_out:
        cp().wait()
    for fam, n in list(ends):
        sent(fam)


def tables(length):
    pos = np.arange(length, dtype=np.float32)
    half = HD // 2
    spacing = (10000.0 ** (-2.0 * np.arange(half, dtype=np.float64) / HD)).astype(np.float32)
    ang = (pos[:, None] * spacing[None, :]).astype(np.float64)
    cos = np.tile(np.cos(ang), (1, 4)).astype(np.float32)
    sin = np.sin(ang)
    sin = np.tile(np.concatenate([-sin, sin], axis=1), (1, 2)).astype(np.float32)
    return cos, sin


def finish_kernel(
    o1_h, od_h, fin, bo_h, cg_h,
    gq_h, go_h, gu_h, gd_h, out_h, clean_h, v_mask, v_ga, v_gm, v_bd, v_bu,
    b1, bd, fq, fo, fu, fd, bo, cg, ls,
):
    L, D, NB = 384, 768, 4
    count = [0]

    def copy(src, dst):
        k = count[0]
        count[0] += 1
        cp = pltpu.make_async_copy(src, dst, ls.at[k])
        cp.start()
        return cp

    rows = [pl.ds(L // NB * r, L // NB) for r in range(NB)]
    in1 = [copy(o1_h.at[:, rows[r]], b1.at[:, rows[r]]) for r in range(NB)]
    ind = [copy(od_h.at[core], bd.at[core]) for core in range(2)]
    through = [copy(bo_h, bo), copy(cg_h, cg)]
    outs = []
    for r in range(NB):
        in1[r].wait()
        for core in range(2):
            for h in range(2):
                fu[rows[r], 1536 * h + D * core : 1536 * h + D * core + D] = b1[
                    core, rows[r], D * h : D * h + D
                ].astype(F32)
            for p in range(3):
                for kind in range(3):
                    src = 1536 + L * p + 128 * kind
                    dst = D * kind + L * core + 128 * p
                    fq[rows[r], dst : dst + 128] = b1[core, rows[r], src : src + 128].astype(F32)
            fo[rows[r], L * core : L * core + L] = b1[
                core, rows[r], 1536 + 3 * L : 1536 + 4 * L
            ].astype(F32)
        for buf, ref in ((fu, gu_h), (fq, gq_h), (fo, go_h)):
            outs.append(copy(buf.at[rows[r]], ref.at[rows[r]]))
        if r < 2:
            through[r].wait()
            outs.append(copy((bo, cg)[r], (out_h, clean_h)[r]))
    for core in range(2):
        ind[core].wait()
        for r in range(2):
            part = slice(L * r, L * r + L)
            at = D * core + L * r
            fd[at : at + L, :] = bd[core, part, :].astype(F32)
            outs.append(copy(fd.at[pl.ds(at, L)], gd_h.at[pl.ds(at, L)]))
    v_mask[...] = fin[0, :]
    v_ga[...] = fin[1, :]
    v_gm[...] = fin[2, :]
    v_bd[...] = fin[3, :]
    for r in range(4):
        v_bu[L * r : L * r + L] = fin[4 + r, :]
    for cp in outs:
        cp.wait()


def on_device(
    nbits, clean_in, noise_bits, mask_vector, gain_attn, w_qkv, w_out, gain_mlp,
    w_up, bias_up, w_down, bias_down, out_grad,
):
    L, D, T = 384, 768, 768
    cos, sin = tables(L)
    nx = max(1, nbits - 3)
    hbm = pl.BlockSpec(memory_space=pltpu.HBM)
    vm = pl.BlockSpec(memory_space=pltpu.VMEM)
    scratch = [
        ((8, L), F32), ((2, 8, L), F32), ((8, D), F32), ((L, 128), F32),
        ((128, 256), F32), ((128, 128), F32),
        ((T, D), BF), ((2 * T, D), BF), ((D, 1152), BF), ((D, D), BF), ((D, 1536), BF),
        ((1536, D), BF), ((2 * T, D), BF),
        ((2 * T, 1152), BF), ((12, 1, T), F32), ((2 * T, D), BF), ((T, D), F32),
        ((2 * T, D), BF), ((2 * T, 1536), BF), ((2 * T, 1536), BF), ((T, D), BF),
        ((T, D), BF), ((T, D), F32), ((2 * T, D), BF), ((2 * T, L), BF), ((T, 128), F32),
        ((1536, D), BF), ((D, 3072), BF),
        ((D, D), BF), ((L, 3072), BF), ((L, D), BF), ((192, 3072), BF),
        ((L, D), BF), ((192, 3072), BF), ((192, D), BF), ((96, 3072), BF),
        ((nx, 192, D), BF) if nbits > 3 else ((1, 16, 128), BF),
        ((nx, 96, 3072), BF) if nbits > 3 else ((1, 16, 128), BF),
        ((nbits + 3, 8, D), F32), ((nbits + 3, 8, D), F32),
    ]
    block_out, clean_grad, fin, g1, gd = pl.pallas_call(
        functools.partial(layer_kernel, nbits),
        out_shape=[
            jax.ShapeDtypeStruct((1, T, D), BF),
            jax.ShapeDtypeStruct((1, L, D), F32),
            jax.ShapeDtypeStruct((8, L), F32),
            jax.ShapeDtypeStruct((2, L, 3072), BF),
            jax.ShapeDtypeStruct((2, D, D), BF),
        ],
        in_specs=[hbm] + [vm] * 8 + [hbm] * 5,
        out_specs=[hbm, hbm, vm, hbm, hbm],
        scratch_shapes=[pltpu.VMEM(s, t) for s, t in scratch]
        + [
            pltpu.SemaphoreType.DMA((N_SEND + 1 * (nbits - 3),)),
            pltpu.SemaphoreType.DMA((N_RECV + 14 * (nbits - 3),)),
            pltpu.SemaphoreType.DMA((N_LOCAL,)),
        ],
        compiler_params=pltpu.CompilerParams(
            collective_id=0, has_side_effects=True, vmem_limit_bytes=64 * 2**20
        ),
        name="layer",
    )(
        clean_in, noise_bits, mask_vector, gain_attn, gain_mlp, bias_down, bias_up, cos, sin,
        w_qkv, w_out, w_up, w_down, out_grad,
    )
    vec = jax.ShapeDtypeStruct((L,), F32)
    gq, go, gu, gdown, out, clean, v_mask, v_ga, v_gm, v_bd, v_bu = pl.pallas_call(
        finish_kernel,
        out_shape=[
            jax.ShapeDtypeStruct((L, 2304), F32),
            jax.ShapeDtypeStruct((L, D), F32),
            jax.ShapeDtypeStruct((L, 3072), F32),
            jax.ShapeDtypeStruct((1536, D), F32),
            jax.ShapeDtypeStruct((1, T, D), BF),
            jax.ShapeDtypeStruct((1, L, D), F32),
            vec, vec, vec, vec, jax.ShapeDtypeStruct((4 * L,), F32),
        ],
        in_specs=[hbm, hbm, vm, hbm, hbm],
        out_specs=[hbm] * 6 + [vm] * 5,
        scratch_shapes=[
            pltpu.VMEM((2, L, 3072), BF), pltpu.VMEM((2, D, D), BF),
            pltpu.VMEM((L, 2304), F32), pltpu.VMEM((L, D), F32),
            pltpu.VMEM((L, 3072), F32), pltpu.VMEM((1536, D), F32),
            pltpu.VMEM((1, T, D), BF), pltpu.VMEM((1, L, D), F32),
            pltpu.SemaphoreType.DMA((26,)),
        ],
        compiler_params=pltpu.CompilerParams(vmem_limit_bytes=64 * 2**20),
        name="finish",
    )(g1, gd, fin, block_out, clean_grad)
    return out, clean, v_mask, v_ga, gq, go, v_gm, gu, v_bu, gdown, v_bd


def solution(mesh):
    nbits = int(math.log2(mesh.shape["dp"])) - 1
    seq = P(("dp", "fsdp"), None, None)
    row, vec = P("fsdp", None), P("fsdp")
    in_specs = (seq, P(("dp", "fsdp"), None), vec, vec, row, row, vec, row, vec, row, vec, seq)
    out_specs = (seq, seq, vec, vec, row, row, vec, row, vec, row, vec)
    return jax.shard_map(
        functools.partial(on_device, nbits), mesh=mesh,
        in_specs=in_specs, out_specs=out_specs, check_vma=False,
    )
```
